128 devices in a mesh: gx: 16 (over z, x), gy: 8 (over y, core).
Axes of the slice: x: 4, y: 4, z: 4, core: 2. Of those that a mesh axis runs over, the one named last changes fastest.
Arguments:
- adj_fields: float32 [3, 8192, 4096], P(None, 'gx', 'gy'), may hold values from -6 to 6
- depth: float32 [8192, 4096], P('gx', 'gy'), may hold values from 0.2 to 1
- block_x: float32 [64, 128, 128], replicated
- reduced_x: float32 [128, 128], replicated
- block_y: float32 [32, 128, 128], replicated
- reduced_y: float32 [64, 64], replicated
- basis: float32 [4, 32, 128], replicated, may hold values from -0.09375 to 0.09375
- coef: float32 [2048, 8, 4], replicated, may hold values from -1 to 1
- footprint: int32 [2048, 8], replicated, may hold values from 0 to 8191, as said below
- owner: int32 [2048], replicated, may hold values from 0 to 2047, each once
- wet: int32 [256, 32], P('gx', 'gy'), may hold values 0 or 1
Outputs:
- adj_before: float32 [3, 8192, 4096], P(None, 'gx', 'gy')
- grad: float32 [2048], P(('gx', 'gy'))
The draws below stay inside these ranges and needn't reach their ends.
Inputs may be any that keep to these rules, and one draw needn't show every extreme that they name: Each subfault's footprint is a patch of 2 x 4 neighbouring tiles, numbered tile row * 32 + tile column.
All inputs are finite; a program needn't handle non-finite values. No bound on the sum of `wet` on one device may be relied on, other than what follows from the above.
Results may differ from the reference program's by a relative error of at most 0.00021.
Values sent between devices are 32-bit elements; how exact they have to be, the bound alone decides.
No kernel may reach another device: no remote copies, remote signals or barrier semaphores. Data moves between devices by JAX's collectives and lax.ppermute only.
A program may use at most 128 MiB of HBM per device.

```python
import math
import jax
import jax.numpy as jnp
from jax import lax

K = 128
TH = 32
TW = 128
NB = 4
FP = 8
NX = 8192
NY = 4096
CHX = 64
CHY = 32
NTX = 256
NTY = 32
NT = 8192
SUBF = 2048


def kernel_matrix(key, count, size, level, decay):
    rows = jnp.arange(size)[:, None]
    cols = jnp.arange(size)[None, :]
    distance = jnp.abs(rows - cols).astype(jnp.float32)
    noise = jax.random.uniform(key, (count, size, size), jnp.float32, 0.5, 1.5)
    return level * jnp.power(jnp.float32(decay), distance)[None] * noise


def draw_block_x(key, part):
    key = jax.random.fold_in(key, 11)
    return kernel_matrix(key, CHX, K, 0.25, 0.9)


def draw_block_y(key, part):
    key = jax.random.fold_in(key, 12)
    return kernel_matrix(key, CHY, K, 0.25, 0.9)


def draw_reduced_x(key, part):
    key = jax.random.fold_in(key, 13)
    return kernel_matrix(key, 1, 2 * CHX, 0.4, 0.97)[0]


def draw_reduced_y(key, part):
    key = jax.random.fold_in(key, 14)
    return kernel_matrix(key, 1, 2 * CHY, 0.4, 0.97)[0]


def draw_footprint(key, part):
    key = jax.random.fold_in(key, 15)
    key_row, key_col = jax.random.split(key)
    tile_row = jax.random.randint(key_row, (SUBF, 1), 0, NTX - 1, dtype=jnp.int32)
    tile_col = jax.random.randint(key_col, (SUBF, 1), 0, NTY - 3, dtype=jnp.int32)
    number = jnp.arange(SUBF, dtype=jnp.int32)[:, None]
    tile_row = jnp.where(number == 0, NTX - 2, jnp.where(number == 1, 0, tile_row))
    tile_col = jnp.where(number == 0, NTY - 4, jnp.where(number == 1, 0, tile_col))
    slots = jnp.arange(FP, dtype=jnp.int32)[None, :]
    rows = tile_row + slots // 4
    cols = tile_col + slots % 4
    return (rows * NTY + cols).astype(jnp.int32)


def with_ends(drawn, rng, smallest, high):
    extent = drawn.shape
    index_at = [jax.random.randint(jax.random.fold_in(rng, axis), (), 0, extent[axis]) for axis in range(len(extent))]
    drawn = drawn.at[tuple(index_at)].set(smallest)
    longest = extent.index(max(extent))
    index_at[longest] = (index_at[longest] + 1) % extent[longest]
    return drawn.at[tuple(index_at)].set(high)


def block_scale(stream_key, dims, pieces, least, top_value):
    def one(position, blocks):
        draws = jax.random.uniform(jax.random.fold_in(jax.random.fold_in(stream_key, 6), position), (blocks,), jnp.float32, least / len(pieces), top_value / len(pieces))
        return jnp.repeat(jnp.exp(draws), dims[position] // blocks).reshape((-1,) + (1,) * (len(dims) - position - 1))

    level = one(*pieces[0])
    for cut in pieces[1:]:
        level = level * one(*cut)
    return level


def bell_draw(own_key, shape, scale, most, cuts=(), kind=jnp.bfloat16):
    values = scale * jax.random.normal(own_key, shape, jnp.float32)
    if cuts:
        values = values * block_scale(own_key, shape, cuts, -0.22, 0.18)
    return jnp.clip(values, -most, most).astype(kind)


def setup_inputs(seed: int = 0) -> dict:
    keys = jax.random.split(jax.random.key(seed), 12)
    return {
        "adj_fields": bell_draw(keys[0], (3, NX, NY), 1.0, 6.0, ((1, 16), (2, 8)), jnp.float32),
        "depth": jnp.clip(jnp.exp(math.log(1.0) - 1.609438 * jax.random.uniform(keys[1], (NX, NY), jnp.float32) ** block_scale(keys[1], (NX, NY), ((0, 16), (1, 8)), -0.2, 0.2)), 0.2, 1.0),
        "block_x": draw_block_x(jax.random.fold_in(keys[11], 71), 0),
        "reduced_x": draw_reduced_x(jax.random.fold_in(keys[11], 71), 0),
        "block_y": draw_block_y(jax.random.fold_in(keys[11], 71), 0),
        "reduced_y": draw_reduced_y(jax.random.fold_in(keys[11], 71), 0),
        "basis": bell_draw(keys[6], (NB, TH, TW), (TH * TW) ** -0.5, 0.09375, (), jnp.float32),
        "coef": bell_draw(keys[7], (SUBF, FP, NB), (FP * NB) ** -0.5, 1.0, (), jnp.float32),
        "footprint": draw_footprint(jax.random.fold_in(keys[11], 71), 0),
        "owner": jax.random.permutation(keys[9], SUBF).astype(jnp.int32),
        "wet": with_ends((jax.random.randint(keys[10], (NTX, NTY), 0, 4) < 3).astype(jnp.int32), jax.random.fold_in(keys[10], 1), 0, 1),
    }


courant = 0.5


def solve_last(lines, blocks, reduced):
    count = lines.shape[0]
    nblk = blocks.shape[0]
    width = blocks.shape[1]
    split = lines.reshape(count, nblk, width)
    inner = jnp.einsum("cjk,mck->mcj", blocks, split, precision=lax.Precision.HIGHEST)
    ends = jnp.stack((inner[:, :, 0], inner[:, :, width - 1]), axis=2).reshape(count, 2 * nblk)
    coupled = jnp.dot(ends, reduced.T, precision=lax.Precision.HIGHEST).reshape(count, nblk, 2)
    result = inner + coupled[:, :, 0:1] * blocks[None, :, :, 0] + coupled[:, :, 1:2] * blocks[None, :, :, width - 1]
    return result.reshape(count, nblk * width)


def reference(adj_fields, depth, block_x, reduced_x, block_y, reduced_y, basis, coef, footprint, owner, wet):
    flux_x = solve_last(adj_fields[1].T, block_x, reduced_x).T
    flux_y = solve_last(adj_fields[2], block_y, reduced_y)
    weighted_x = depth * flux_x
    weighted_y = depth * flux_y
    back_x = weighted_x - jnp.concatenate([jnp.zeros_like(weighted_x[:1]), weighted_x[:-1]], axis=0)
    back_y = weighted_y - jnp.concatenate([jnp.zeros_like(weighted_y[:, :1]), weighted_y[:, :-1]], axis=1)
    elev = adj_fields[0] + courant * (back_x + back_y)
    fore_x = jnp.concatenate([elev[1:], jnp.zeros_like(elev[:1])], axis=0) - elev
    fore_y = jnp.concatenate([elev[:, 1:], jnp.zeros_like(elev[:, :1])], axis=1) - elev
    adj_before = jnp.stack([elev, flux_x + courant * fore_x, flux_y + courant * fore_y])
    tiled = elev.reshape(NTX, TH, NTY, TW)
    moments = jnp.einsum("ahbw,khw->abk", tiled, basis, precision=lax.Precision.HIGHEST)
    moments = (moments * wet[:, :, None].astype(jnp.float32)).reshape(NT, NB)
    picked = moments[footprint]
    per_fault = jnp.sum(coef * picked, axis=(1, 2))
    grad = jnp.zeros((SUBF,), jnp.float32).at[owner].set(per_fault)
    return adj_before, grad
```

```python
import jax
import jax.numpy as jnp
from jax import lax
from jax.experimental import pallas as pl
from jax.experimental.pallas import tpu as pltpu
from jax.sharding import PartitionSpec as P

courant = 0.5
f32 = jnp.float32
bf16 = jnp.bfloat16
K = 128
EXTRA = 128

NN = (((1,), (0,)), ((), ()))
NT = (((1,), (1,)), ((), ()))
TN = (((0,), (0,)), ((), ()))


def halves(x):
    high = x.astype(bf16)
    return high, (x - high.astype(f32)).astype(bf16)


def mm(a, b, dims):
    return lax.dot_general(a, b, dims, preferred_element_type=f32)


def mm3(a, b, dims):
    ah, al = a
    bh, bl = b
    return mm(ah, bh, dims) + (mm(ah, bl, dims) + mm(al, bh, dims))


def exact(a, b, dims):
    return lax.dot_general(a, b, dims, precision=lax.Precision.HIGHEST, preferred_element_type=f32)


def iota(shape, dim):
    return lax.broadcasted_iota(jnp.int32, shape, dim)


def any_spec():
    return pl.BlockSpec(memory_space=pl.ANY)


def vmem_spec():
    return pl.BlockSpec(memory_space=pltpu.VMEM)


def cost(flops, nbytes):
    return pl.CostEstimate(flops=flops, bytes_accessed=nbytes, transcendentals=0)


def ends_kernel(
    adj, depth, block_x, block_y, px, py, vx, vy, wx0, wx1, wy0, wy1, drow, dcol, sems
):
    u = lax.axis_index("gx")
    v = lax.axis_index("gy")
    rows, cols = vx.shape
    nbx = wx0.shape[0]
    nby = wy0.shape[0]
    small = [
        pltpu.make_async_copy(block_x.at[pl.ds(u * nbx, nbx), pl.ds(0, 8), :], wx0, sems.at[0]),
        pltpu.make_async_copy(block_x.at[pl.ds(u * nbx, nbx), pl.ds(K - 8, 8), :], wx1, sems.at[1]),
        pltpu.make_async_copy(block_y.at[pl.ds(v * nby, nby), pl.ds(0, 8), :], wy0, sems.at[2]),
        pltpu.make_async_copy(block_y.at[pl.ds(v * nby, nby), pl.ds(K - 8, 8), :], wy1, sems.at[3]),
        pltpu.make_async_copy(depth.at[pl.ds(rows - 8, 8), :], drow, sems.at[4]),
        pltpu.make_async_copy(depth.at[:, pl.ds(cols - K, K)], dcol, sems.at[5]),
    ]
    for copy in small:
        copy.start()
    big = []
    for c in range(nbx):
        here = pl.ds(c * K, K)
        big.append(pltpu.make_async_copy(adj.at[2, here, :], vy.at[here, :], sems.at[6 + c]))
    for c in range(nbx):
        here = pl.ds(c * K, K)
        big.append(pltpu.make_async_copy(adj.at[1, here, :], vx.at[here, :], sems.at[6 + nbx + c]))
    for copy in big:
        copy.start()
    for copy in small:
        copy.wait()
    ends_y = [halves(jnp.concatenate([wy0[c, 0:1, :], wy1[c, 7:8, :]], axis=0)) for c in range(nby)]
    ends_x = [halves(jnp.concatenate([wx0[c, 0:1, :], wx1[c, 7:8, :]], axis=0)) for c in range(nbx)]
    for part in range(cols // K):
        px[0, part : part + 1, cols:] = drow[7:8, part * K : (part + 1) * K]
    px[0, cols // K :, cols:] = jnp.zeros((8 - cols // K, EXTRA), f32)
    last = (iota((8, K), 1) == K - 1).astype(f32)
    side = exact(last, dcol[...], NT)
    for part in range(rows // K):
        py[part : part + 1, rows:] = side[0:1, part * K : (part + 1) * K]
    py[rows // K :, rows:] = jnp.zeros((8 - rows // K, EXTRA), f32)
    for r in range(nbx):
        big[r].wait()
        for c in range(nby):
            part = halves(vy[r * K : (r + 1) * K, c * K : (c + 1) * K])
            py[2 * c : 2 * c + 2, r * K : (r + 1) * K] = mm3(ends_y[c], part, NT)
    for c in range(nbx):
        big[nbx + c].wait()
        part = halves(vx[c * K : (c + 1) * K, :])
        px[0, 2 * c : 2 * c + 2, :cols] = mm3(ends_x[c], part, NN)
    for d in range(1, px.shape[0]):
        px[d] = px[0]


def ends(adj, depth, block_x, block_y, size_x, size_y):
    rows, cols = depth.shape
    nbx = block_x.shape[0] // size_x
    nby = block_y.shape[0] // size_y
    return pl.pallas_call(
        ends_kernel,
        out_shape=(
            jax.ShapeDtypeStruct((size_x, 2 * nbx, cols + EXTRA), f32),
            jax.ShapeDtypeStruct((2 * nby, rows + EXTRA), f32),
        ),
        in_specs=[any_spec()] * 4,
        out_specs=(vmem_spec(), vmem_spec()),
        scratch_shapes=[
            pltpu.VMEM((rows, cols), f32),
            pltpu.VMEM((rows, cols), f32),
            pltpu.VMEM((nbx, 8, K), f32),
            pltpu.VMEM((nbx, 8, K), f32),
            pltpu.VMEM((nby, 8, K), f32),
            pltpu.VMEM((nby, 8, K), f32),
            pltpu.VMEM((8, cols), f32),
            pltpu.VMEM((rows, K), f32),
            pltpu.SemaphoreType.DMA((6 + 2 * nbx,)),
        ],
        compiler_params=pltpu.CompilerParams(vmem_limit_bytes=16 << 20),
        cost_estimate=cost(2 * rows * cols * 32, 3 << 20),
        name="ends",
    )(adj, depth, block_x, block_y)


def local_kernel(
    adj, block_x, block_y, reduced_x, reduced_y,
    yx, yy, gxh, gxl, gyh, gyl, gside, vx, vy, wx, wy, wpx, wpy, sems,
):
    u = lax.axis_index("gx")
    v = lax.axis_index("gy")
    rows, cols = vx.shape
    nbx = wx.shape[0]
    nby = wy.shape[0]
    before_x = jnp.maximum(u * nbx - 1, 0)
    before_y = jnp.maximum(v * nby - 1, 0)
    copies = [
        pltpu.make_async_copy(block_x.at[pl.ds(u * nbx, nbx)], wx, sems.at[0]),
        pltpu.make_async_copy(block_y.at[pl.ds(v * nby, nby)], wy, sems.at[1]),
        pltpu.make_async_copy(block_x.at[before_x, pl.ds(K - 8, 8), :], wpx, sems.at[2]),
        pltpu.make_async_copy(block_y.at[before_y, pl.ds(K - 8, 8), :], wpy, sems.at[3]),
        pltpu.make_async_copy(adj.at[1], vx, sems.at[4]),
        pltpu.make_async_copy(adj.at[2], vy, sems.at[5]),
    ]
    for copy in copies:
        copy.start()
    for copy in copies[:4]:
        copy.wait()
    own_x = reduced_x[pl.ds(pl.multiple_of(u * 8, 8), 8), :]
    own_y = reduced_y[pl.ds(pl.multiple_of(v * 8, 8), 8), :]
    prev_x = reduced_x[pl.ds(pl.multiple_of(jnp.maximum(u - 1, 0) * 8, 8), 8), :]
    prev_y = reduced_y[pl.ds(pl.multiple_of(jnp.maximum(v - 1, 0) * 8, 8), 8), :]
    for c in range(nbx):
        w = wx[c]
        g = w[:, 0:1] * own_x[2 * c : 2 * c + 1, :] + w[:, K - 1 : K] * own_x[2 * c + 1 : 2 * c + 2, :]
        high, low = halves(g)
        gxh[c * K : (c + 1) * K, :] = high
        gxl[c * K : (c + 1) * K, :] = low
    row = iota((8, K), 0)
    lane = iota((8, K), 1)
    for c in range(nby):
        pick = (((row == 2 * c) & (lane == 0)) | ((row == 2 * c + 1) & (lane == K - 1))).astype(f32)
        across = exact(pick, wy[c], NT)
        high, low = halves(exact(own_y, across, TN))
        gyh[:, c * K : (c + 1) * K] = high
        gyl[:, c * K : (c + 1) * K] = low

    def side(w, prev, index):
        width = prev.shape[1]
        g = w[7:8, 0:1] * prev[6:7, :] + w[7:8, K - 1 : K] * prev[7:8, :]
        g = g + (iota((1, width), 1) == index * 8 - 1).astype(f32)
        return jnp.where(index > 0, g, 0.0)

    gside[...] = jnp.zeros(gside.shape, f32)
    gside[0:1, :] = side(wpx[...], prev_x, u)
    gside[1:2, : reduced_y.shape[1]] = side(wpy[...], prev_y, v)
    copies[4].wait()
    for c in range(nbx):
        yx[c * K : (c + 1) * K, :] = mm3(halves(wx[c]), halves(vx[c * K : (c + 1) * K, :]), NN)
    copies[5].wait()
    for c in range(nby):
        yy[:, c * K : (c + 1) * K] = mm3(halves(vy[:, c * K : (c + 1) * K]), halves(wy[c]), NT)


def local(adj, block_x, block_y, reduced_x, reduced_y, size_x, size_y):
    _, rows, cols = adj.shape
    nbx = block_x.shape[0] // size_x
    nby = block_y.shape[0] // size_y
    field = jax.ShapeDtypeStruct((rows, cols), f32)
    return pl.pallas_call(
        local_kernel,
        out_shape=(
            field,
            field,
            jax.ShapeDtypeStruct((rows, reduced_x.shape[0]), bf16),
            jax.ShapeDtypeStruct((rows, reduced_x.shape[0]), bf16),
            jax.ShapeDtypeStruct((reduced_y.shape[0], cols), bf16),
            jax.ShapeDtypeStruct((reduced_y.shape[0], cols), bf16),
            jax.ShapeDtypeStruct((8, reduced_x.shape[0]), f32),
        ),
        in_specs=[any_spec()] * 3 + [vmem_spec()] * 2,
        out_specs=(vmem_spec(),) * 7,
        scratch_shapes=[
            pltpu.VMEM((rows, cols), f32),
            pltpu.VMEM((rows, cols), f32),
            pltpu.VMEM((nbx, K, K), f32),
            pltpu.VMEM((nby, K, K), f32),
            pltpu.VMEM((8, K), f32),
            pltpu.VMEM((8, K), f32),
            pltpu.SemaphoreType.DMA((6,)),
        ],
        compiler_params=pltpu.CompilerParams(vmem_limit_bytes=24 << 20),
        cost_estimate=cost(12 * rows * cols * K, 5 << 20),
        name="local",
    )(adj, block_x, block_y, reduced_x, reduced_y)


def faults_kernel(wet, coef, footprint, owner, weights, high_of, low_of, dist, coef8):
    u = lax.axis_index("gx")
    v = lax.axis_index("gy")
    tiles_x, tiles_y = wet.shape
    total_cols = tiles_y * lax.axis_size("gy")
    shift = total_cols.bit_length() - 1
    count = footprint.shape[1]
    places = footprint.shape[0]
    sub = iota((8, count), 0)
    for f in range(places):
        tile = footprint[f : f + 1, :]
        row = lax.shift_right_logical(tile, shift) - u * tiles_x
        col = (tile & (total_cols - 1)) - v * tiles_y
        inside = (row >= 0) & (row < tiles_x) & (col >= 0) & (col < tiles_y)
        flat = jnp.where(inside, col * tiles_x + row, -1000)
        dist[f] = flat - lax.shift_right_logical(sub, 2)
        four = coef[4 * f : 4 * f + 4, :]
        coef8[f] = jnp.concatenate([four, four], axis=0)

    def group(g, carry):
        acc = jnp.zeros((8, count), f32)
        for f in range(places):
            acc = acc + jnp.where(dist[f] == 2 * g, coef8[f], 0.0)
        col = (2 * g) // tiles_x
        row = 2 * g - col * tiles_x
        keep = jnp.where(sub < 4, wet[row, col].astype(f32), wet[row + 1, col].astype(f32))
        weights[pl.ds(pl.multiple_of(g * 8, 8), 8), :] = acc * keep
        return carry

    lax.fori_loop(0, tiles_x * tiles_y // 2, group, 0)
    own = owner[...]
    slots = low_of.shape[0]
    bits = slots.bit_length() - 1
    high_of[...] = (iota(high_of.shape, 0) == lax.shift_right_logical(own, bits)).astype(f32).astype(bf16)
    low_of[...] = (iota(low_of.shape, 0) == (own & (slots - 1))).astype(f32)


def faults(wet, coef, footprint, owner, devices):
    tiles_x, tiles_y = wet.shape
    subf, places, modes = coef.shape
    slots = subf // devices
    return pl.pallas_call(
        faults_kernel,
        out_shape=(
            jax.ShapeDtypeStruct((tiles_x * tiles_y * modes, subf), f32),
            jax.ShapeDtypeStruct((devices, subf), bf16),
            jax.ShapeDtypeStruct((slots, subf), f32),
        ),
        in_specs=[pl.BlockSpec(memory_space=pltpu.SMEM)] + [vmem_spec()] * 3,
        out_specs=(vmem_spec(),) * 3,
        scratch_shapes=[
            pltpu.VMEM((places, 8, subf), jnp.int32),
            pltpu.VMEM((places, 8, subf), f32),
        ],
        compiler_params=pltpu.CompilerParams(vmem_limit_bytes=16 << 20),
        cost_estimate=cost(40 << 20, 3 << 20),
        name="faults",
    )(
        wet,
        coef.reshape(subf, places * modes).T,
        footprint.T,
        owner.reshape(1, subf),
    )


def elev_kernel(
    tx, ta, tb, yx, yy, gxh, gxl, gyh, gyl, gside, adj, depth, basis, weights, high_of, low_of,
    elev, fx, fy, erow, ecol, parts, dep, a0, tyn, mom, sems,
):
    u = lax.axis_index("gx")
    v = lax.axis_index("gy")
    rows, cols = dep.shape
    steps = rows // K
    copies = []
    for r in range(steps):
        here = pl.ds(r * K, K)
        copies.append(
            (
                pltpu.make_async_copy(depth.at[here, :], dep.at[here, :], sems.at[2 * r]),
                pltpu.make_async_copy(adj.at[0, here, :], a0.at[here, :], sems.at[2 * r + 1]),
            )
        )
    for pair in copies:
        for copy in pair:
            copy.start()
    nx = tx.shape[0]
    half = ta.shape[0]
    tx_all = jnp.concatenate([tx[d][:, :cols] for d in range(nx)], axis=0)
    for j in range(2 * half):
        k = j ^ v
        first = ta[k & (half - 1)]
        second = tb[k & (half - 1)]
        tyn[j * 8 : (j + 1) * 8, :] = jnp.where(k < half, first, second)
    ty_all = tyn[:, :rows]
    txs = halves(tx_all)
    tys = halves(ty_all)
    up = jnp.maximum(u - 1, 0)
    left = jnp.maximum(v - 1, 0)
    gs = gside[...]
    edge_x = exact(gs, tx_all, NN)[0:1, :]
    edge_y = exact(gs[:, : ty_all.shape[0]], ty_all, NN)[1:2, :]
    drow = tx[up][:, cols:]
    drow = jnp.concatenate([drow[p : p + 1, :] for p in range(cols // K)], axis=1)
    dcol = tyn[pl.ds(pl.multiple_of(left * 8, 8), 8), rows:]
    dcol = jnp.concatenate([dcol[p : p + 1, :] for p in range(rows // K)], axis=1)
    carry = edge_x * drow
    side = jnp.broadcast_to(edge_y * dcol, (8, rows))
    row = iota((K, cols), 0)
    lane = iota((K, cols), 1)
    first_lane = (iota((8, K), 1) == 0) & (iota((8, K), 0) == 0)
    first_lane = first_lane.astype(f32)
    modes, tile_h, tile_w = basis.shape
    per = K // tile_h
    wide = [jnp.concatenate([basis[b]] * (cols // tile_w), axis=1) for b in range(modes)]
    for r in range(steps):
        here = slice(r * K, (r + 1) * K)
        for copy in copies[r]:
            copy.wait()
        d = dep[here, :]
        flux_x = yx[here, :] + mm3((gxh[here, :], gxl[here, :]), txs, NN)
        part = (tys[0][:, here], tys[1][:, here])
        flux_y = yy[here, :] + mm3(part, (gyh[...], gyl[...]), TN)
        fx[here, :] = flux_x
        fy[here, :] = flux_y
        weighted_x = d * flux_x
        weighted_y = d * flux_y
        before_x = jnp.where(row == 0, carry, pltpu.roll(weighted_x, 1, 0))
        carry = weighted_x[K - 1 : K, :]
        edge = exact(side[:, here], first_lane, TN)
        edge = jnp.concatenate([edge, jnp.zeros((K, cols - K), f32)], axis=1)
        before_y = jnp.where(lane == 0, edge, pltpu.roll(weighted_y, 1, 1))
        e = a0[here, :] + courant * ((weighted_x - before_x) + (weighted_y - before_y))
        elev[here, :] = e
        if r == 0:
            erow[...] = e[0:1, :]
        ecol[:, here] = exact(first_lane, e[:, :K], NT)[0:1, :]
        for a in range(per):
            tile = e[a * tile_h : (a + 1) * tile_h, :]
            for b in range(modes):
                at = (r * per + a) * modes + b
                mom[at : at + 1, :] = jnp.sum(tile * wide[b], axis=0, keepdims=True)
    total = None
    group = mom.shape[0]
    for w in range(cols // tile_w):
        m = jnp.sum(mom[:, w * tile_w : (w + 1) * tile_w], axis=1, keepdims=True)
        term = jnp.sum(weights[w * group : (w + 1) * group, :] * m, axis=0, keepdims=True)
        total = term if total is None else total + term
    high, low = halves(low_of[...] * total)
    sums = mm(high_of[...], high, NT) + mm(high_of[...], low, NT)
    parts[...] = jnp.zeros(parts.shape, f32)
    parts[:, : sums.shape[1]] = sums


def elevation(tx, ta, tb, solved, adj, depth, basis, weights, high_of, low_of):
    rows, cols = depth.shape
    field = jax.ShapeDtypeStruct((rows, cols), f32)
    modes, tile_h, tile_w = basis.shape
    return pl.pallas_call(
        elev_kernel,
        out_shape=(
            field,
            field,
            field,
            jax.ShapeDtypeStruct((1, cols), f32),
            jax.ShapeDtypeStruct((1, rows), f32),
            jax.ShapeDtypeStruct((high_of.shape[0], K), f32),
        ),
        in_specs=[vmem_spec()] * 10 + [any_spec()] * 2 + [vmem_spec()] * 4,
        out_specs=(vmem_spec(),) * 6,
        scratch_shapes=[
            pltpu.VMEM((rows, cols), f32),
            pltpu.VMEM((rows, cols), f32),
            pltpu.VMEM((2 * ta.shape[0] * 8, rows + EXTRA), f32),
            pltpu.VMEM((rows // tile_h * modes, cols), f32),
            pltpu.SemaphoreType.DMA((2 * (rows // K),)),
        ],
        compiler_params=pltpu.CompilerParams(vmem_limit_bytes=32 << 20),
        cost_estimate=cost(12 * rows * cols * K, 10 << 20),
        name="elevation",
    )(tx, ta, tb, *solved, adj, depth, basis, weights, high_of, low_of)


def fluxes_kernel(elev, fx, fy, hrow, hcol, out, e, x, y, sems):
    rows, cols = e.shape
    steps = rows // K
    reads = []
    for r in range(steps):
        here = pl.ds(r * K, K)
        reads.append(
            (
                pltpu.make_async_copy(elev.at[here, :], e.at[here, :], sems.at[r, 0]),
                pltpu.make_async_copy(fx.at[here, :], x.at[here, :], sems.at[r, 1]),
                pltpu.make_async_copy(fy.at[here, :], y.at[here, :], sems.at[r, 2]),
            )
        )
    for group in reads:
        for copy in group:
            copy.start()
    last_lane = ((iota((8, K), 1) == K - 1) & (iota((8, K), 0) == 0)).astype(f32)
    side = jnp.broadcast_to(hcol[...], (8, rows))
    row = iota((K, cols), 0)
    lane = iota((K, cols), 1)
    writes = []
    for copy in reads[0]:
        copy.wait()
    for r in range(steps):
        here = slice(r * K, (r + 1) * K)
        if r + 1 < steps:
            for copy in reads[r + 1]:
                copy.wait()
            after = e[(r + 1) * K : (r + 1) * K + 1, :]
        else:
            after = hrow[...]
        now = e[here, :]
        edge = exact(side[:, here], last_lane, TN)
        edge = jnp.concatenate([jnp.zeros((K, cols - K), f32), edge], axis=1)
        below = jnp.where(row == K - 1, after, pltpu.roll(now, K - 1, 0))
        right = jnp.where(lane == cols - 1, edge, pltpu.roll(now, cols - 1, 1))
        x[here, :] = x[here, :] + courant * (below - now)
        y[here, :] = y[here, :] + courant * (right - now)
        where = pl.ds(r * K, K)
        group = (
            pltpu.make_async_copy(e.at[where, :], out.at[0, where, :], sems.at[r, 3]),
            pltpu.make_async_copy(x.at[where, :], out.at[1, where, :], sems.at[r, 4]),
            pltpu.make_async_copy(y.at[where, :], out.at[2, where, :], sems.at[r, 5]),
        )
        for copy in group:
            copy.start()
        writes.append(group)
    for group in writes:
        for copy in group:
            copy.wait()


def fluxes(elev, fx, fy, hrow, hcol):
    rows, cols = elev.shape
    return pl.pallas_call(
        fluxes_kernel,
        out_shape=jax.ShapeDtypeStruct((3, rows, cols), f32),
        in_specs=[any_spec()] * 3 + [vmem_spec()] * 2,
        out_specs=any_spec(),
        scratch_shapes=[
            pltpu.VMEM((rows, cols), f32),
            pltpu.VMEM((rows, cols), f32),
            pltpu.VMEM((rows, cols), f32),
            pltpu.SemaphoreType.DMA((rows // K, 6)),
        ],
        compiler_params=pltpu.CompilerParams(vmem_limit_bytes=16 << 20),
        cost_estimate=cost(10 * rows * cols, 6 << 20),
        name="fluxes",
    )(elev, fx, fy, hrow, hcol)


def partner(axis, bit):
    return [(i, i ^ bit) for i in range(lax.axis_size(axis))]


def previous(axis):
    return [(i, i - 1) for i in range(1, lax.axis_size(axis))]


def body(
    adj_fields, depth, block_x, reduced_x, block_y, reduced_y, basis, coef, footprint, owner, wet
):
    size_x = lax.axis_size("gx")
    size_y = lax.axis_size("gy")
    px, py = ends(adj_fields, depth, block_x, block_y, size_x, size_y)
    tx = lax.all_to_all(px, "gx", split_axis=0, concat_axis=0, tiled=True)
    ty = py[None]
    bit = 1
    while 2 * bit < size_y:
        ty = jnp.concatenate([ty, lax.ppermute(ty, "gy", partner("gy", bit))], axis=0)
        bit *= 2
    ty_far = lax.ppermute(ty, "gy", partner("gy", bit))
    solved = local(adj_fields, block_x, block_y, reduced_x, reduced_y, size_x, size_y)
    chosen = faults(wet, coef, footprint, owner, size_x * size_y)
    elev, fx, fy, erow, ecol, parts = elevation(
        tx, ty, ty_far, solved, adj_fields, depth, basis, *chosen
    )
    devices, width = parts.shape
    sums = lax.all_to_all(
        parts.reshape(devices, 1, width), ("gx", "gy"), split_axis=0, concat_axis=0, tiled=True
    )
    hrow = lax.ppermute(erow, "gx", previous("gx"))
    hcol = lax.ppermute(ecol, "gy", previous("gy"))
    adj_before = fluxes(elev, fx, fy, hrow, hcol)
    slots = owner.shape[0] // devices
    grad = jnp.sum(sums[:, 0, :slots], axis=0)
    return adj_before, grad


def solution(mesh):
    in_specs = (
        P(None, "gx", "gy"),
        P("gx", "gy"),
        P(),
        P(),
        P(),
        P(),
        P(),
        P(),
        P(),
        P(),
        P("gx", "gy"),
    )
    out_specs = (P(None, "gx", "gy"), P(("gx", "gy")))
    return jax.shard_map(body, mesh=mesh, in_specs=in_specs, out_specs=out_specs, check_vma=False)
```

```python
import jax
import jax.numpy as jnp
from jax import lax
from jax.experimental import pallas as pl
from jax.experimental.pallas import tpu as pltpu
from jax.sharding import PartitionSpec as P

courant = 0.5
f32 = jnp.float32
bf16 = jnp.bfloat16
K = 128
EXTRA = 128

NN = (((1,), (0,)), ((), ()))
NT = (((1,), (1,)), ((), ()))
TN = (((0,), (0,)), ((), ()))


def halves(x):
    high = x.astype(bf16)
    return high, (x - high.astype(f32)).astype(bf16)


def mm(a, b, dims):
    return lax.dot_general(a, b, dims, preferred_element_type=f32)


def mm3(a, b, dims):
    ah, al = a
    bh, bl = b
    return mm(ah, bh, dims) + (mm(ah, bl, dims) + mm(al, bh, dims))


def exact(a, b, dims):
    return lax.dot_general(a, b, dims, precision=lax.Precision.HIGHEST, preferred_element_type=f32)


def iota(shape, dim):
    return lax.broadcasted_iota(jnp.int32, shape, dim)


def hbm_spec():
    return pl.BlockSpec(memory_space=pltpu.HBM)


def vmem_spec():
    return pl.BlockSpec(memory_space=pltpu.VMEM)


def in_hbm(*arrays):
    return tuple(pltpu.with_memory_space_constraint(a, pltpu.HBM) for a in arrays)


def in_vmem(*arrays):
    return tuple(pltpu.with_memory_space_constraint(a, pltpu.VMEM) for a in arrays)


def cost(flops, nbytes):
    return pl.CostEstimate(flops=flops, bytes_accessed=nbytes, transcendentals=0)


def ends_kernel(
    adj, depth, block_x, block_y, px_hbm, py, vx, vy, wx0, wx1, wy0, wy1, drow, dcol, px, sems, out_sems
):
    u = lax.axis_index("gx")
    v = lax.axis_index("gy")
    rows, cols = vx.shape
    nbx = wx0.shape[0]
    nby = wy0.shape[0]
    small = [
        pltpu.make_async_copy(block_x.at[pl.ds(u * nbx, nbx), pl.ds(0, 8), :], wx0, sems.at[0]),
        pltpu.make_async_copy(block_x.at[pl.ds(u * nbx, nbx), pl.ds(K - 8, 8), :], wx1, sems.at[1]),
        pltpu.make_async_copy(block_y.at[pl.ds(v * nby, nby), pl.ds(0, 8), :], wy0, sems.at[2]),
        pltpu.make_async_copy(block_y.at[pl.ds(v * nby, nby), pl.ds(K - 8, 8), :], wy1, sems.at[3]),
        pltpu.make_async_copy(depth.at[pl.ds(rows - 8, 8), :], drow, sems.at[4]),
        pltpu.make_async_copy(depth.at[:, pl.ds(cols - K, K)], dcol, sems.at[5]),
    ]
    for copy in small:
        copy.start()
    big = []
    for c in range(nbx):
        here = pl.ds(c * K, K)
        big.append(pltpu.make_async_copy(adj.at[1, here, :], vx.at[here, :], sems.at[6 + c]))
    for c in range(nbx):
        here = pl.ds(c * K, K)
        big.append(pltpu.make_async_copy(adj.at[2, here, :], vy.at[here, :], sems.at[6 + nbx + c]))
    for copy in big:
        copy.start()
    for copy in small:
        copy.wait()

    def stacked(first, last, c):
        high, low = halves(jnp.concatenate([first[c, 0:1, :], last[c, 7:8, :]], axis=0))
        return jnp.concatenate([high, low], axis=0)

    def product(weights, high, low, dims):
        both = mm(weights, high, dims)
        return both[0:2] + both[2:4] + mm(weights[0:2], low, dims)

    ends_x = [stacked(wx0, wx1, c) for c in range(nbx)]
    ends_y = [stacked(wy0, wy1, c) for c in range(nby)]
    for part in range(cols // K):
        px[part : part + 1, cols:] = drow[7:8, part * K : (part + 1) * K]
    px[cols // K :, cols:] = jnp.zeros((8 - cols // K, EXTRA), f32)
    for c in range(nbx):
        big[c].wait()
        high, low = halves(vx[c * K : (c + 1) * K, :])
        px[2 * c : 2 * c + 2, :cols] = product(ends_x[c], high, low, NN)
    outs = [pltpu.make_async_copy(px, px_hbm.at[d], out_sems.at[d]) for d in range(px_hbm.shape[0])]
    for copy in outs:
        copy.start()
    last = (iota((8, K), 1) == K - 1).astype(f32).astype(bf16)
    high, low = halves(dcol[...])
    side = mm(last, high, NT) + mm(last, low, NT)
    for part in range(rows // K):
        py[part : part + 1, rows:] = side[0:1, part * K : (part + 1) * K]
    py[rows // K :, rows:] = jnp.zeros((8 - rows // K, EXTRA), f32)
    for r in range(nbx):
        big[nbx + r].wait()
        for c in range(nby):
            high, low = halves(vy[r * K : (r + 1) * K, c * K : (c + 1) * K])
            py[2 * c : 2 * c + 2, r * K : (r + 1) * K] = product(ends_y[c], high, low, NT)
    for copy in outs:
        copy.wait()


def ends(adj, depth, block_x, block_y, size_x, size_y):
    rows, cols = depth.shape
    nbx = block_x.shape[0] // size_x
    nby = block_y.shape[0] // size_y
    return pl.pallas_call(
        ends_kernel,
        out_shape=(
            pltpu.HBM((size_x, 2 * nbx, cols + EXTRA), f32),
            jax.ShapeDtypeStruct((2 * nby, rows + EXTRA), f32),
        ),
        in_specs=[hbm_spec()] * 4,
        out_specs=(hbm_spec(), vmem_spec()),
        scratch_shapes=[
            pltpu.VMEM((rows, cols), f32),
            pltpu.VMEM((rows, cols), f32),
            pltpu.VMEM((nbx, 8, K), f32),
            pltpu.VMEM((nbx, 8, K), f32),
            pltpu.VMEM((nby, 8, K), f32),
            pltpu.VMEM((nby, 8, K), f32),
            pltpu.VMEM((8, cols), f32),
            pltpu.VMEM((rows, K), f32),
            pltpu.VMEM((2 * nbx, cols + EXTRA), f32),
            pltpu.SemaphoreType.DMA((6 + 2 * nbx,)),
            pltpu.SemaphoreType.DMA((size_x,)),
        ],
        compiler_params=pltpu.CompilerParams(vmem_limit_bytes=16 << 20),
        cost_estimate=cost(2 * rows * cols * 32, 3 << 20),
        name="ends",
    )(*in_hbm(adj, depth, block_x, block_y))


def local_kernel(
    adj, block_x, block_y, reduced_x_hbm, reduced_y_hbm,
    yx_hbm, yy_hbm, gxh_hbm, gxl_hbm, gyh_hbm, gyl_hbm, gside_hbm,
    yx, yy, gxh, gxl, gyh, gyl, gside, vx, vy, wx, wy, wpx, wpy, reduced_x, reduced_y, sems, out_sems,
):
    u = lax.axis_index("gx")
    v = lax.axis_index("gy")
    rows, cols = vx.shape
    nbx = wx.shape[0]
    nby = wy.shape[0]
    before_x = jnp.maximum(u * nbx - 1, 0)
    before_y = jnp.maximum(v * nby - 1, 0)
    copies = [
        pltpu.make_async_copy(block_x.at[pl.ds(u * nbx, nbx)], wx, sems.at[0]),
        pltpu.make_async_copy(block_y.at[pl.ds(v * nby, nby)], wy, sems.at[1]),
        pltpu.make_async_copy(block_x.at[before_x, pl.ds(K - 8, 8), :], wpx, sems.at[2]),
        pltpu.make_async_copy(block_y.at[before_y, pl.ds(K - 8, 8), :], wpy, sems.at[3]),
        pltpu.make_async_copy(reduced_x_hbm, reduced_x, sems.at[4]),
        pltpu.make_async_copy(reduced_y_hbm, reduced_y, sems.at[5]),
        pltpu.make_async_copy(adj.at[1], vx, sems.at[6]),
        pltpu.make_async_copy(adj.at[2], vy, sems.at[7]),
    ]
    for copy in copies:
        copy.start()
    for copy in copies[:6]:
        copy.wait()
    own_x = reduced_x[pl.ds(pl.multiple_of(u * 8, 8), 8), :]
    own_y = reduced_y[pl.ds(pl.multiple_of(v * 8, 8), 8), :]
    prev_x = reduced_x[pl.ds(pl.multiple_of(jnp.maximum(u - 1, 0) * 8, 8), 8), :]
    prev_y = reduced_y[pl.ds(pl.multiple_of(jnp.maximum(v - 1, 0) * 8, 8), 8), :]
    for c in range(nbx):
        w = wx[c]
        g = w[:, 0:1] * own_x[2 * c : 2 * c + 1, :] + w[:, K - 1 : K] * own_x[2 * c + 1 : 2 * c + 2, :]
        high, low = halves(g)
        gxh[c * K : (c + 1) * K, :] = high
        gxl[c * K : (c + 1) * K, :] = low
    row = iota((8, K), 0)
    lane = iota((8, K), 1)
    for c in range(nby):
        pick = (((row == 2 * c) & (lane == 0)) | ((row == 2 * c + 1) & (lane == K - 1))).astype(f32)
        across = exact(pick, wy[c], NT)
        high, low = halves(exact(own_y, across, TN))
        gyh[:, c * K : (c + 1) * K] = high
        gyl[:, c * K : (c + 1) * K] = low

    def side(w, prev, index):
        width = prev.shape[1]
        g = w[7:8, 0:1] * prev[6:7, :] + w[7:8, K - 1 : K] * prev[7:8, :]
        g = g + (iota((1, width), 1) == index * 8 - 1).astype(f32)
        return jnp.where(index > 0, g, 0.0)

    gside[...] = jnp.zeros(gside.shape, f32)
    gside[0:1, :] = side(wpx[...], prev_x, u)
    gside[1:2, : reduced_y.shape[1]] = side(wpy[...], prev_y, v)
    outs = [
        pltpu.make_async_copy(gxh, gxh_hbm, out_sems.at[2]),
        pltpu.make_async_copy(gxl, gxl_hbm, out_sems.at[3]),
        pltpu.make_async_copy(gyh, gyh_hbm, out_sems.at[4]),
        pltpu.make_async_copy(gyl, gyl_hbm, out_sems.at[5]),
        pltpu.make_async_copy(gside, gside_hbm, out_sems.at[6]),
    ]
    for copy in outs:
        copy.start()
    copies[6].wait()
    for c in range(nbx):
        yx[c * K : (c + 1) * K, :] = mm3(halves(wx[c]), halves(vx[c * K : (c + 1) * K, :]), NN)
    outs.append(pltpu.make_async_copy(yx, yx_hbm, out_sems.at[0]))
    outs[-1].start()
    copies[7].wait()
    for c in range(nby):
        yy[:, c * K : (c + 1) * K] = mm3(halves(vy[:, c * K : (c + 1) * K]), halves(wy[c]), NT)
    outs.append(pltpu.make_async_copy(yy, yy_hbm, out_sems.at[1]))
    outs[-1].start()
    for copy in outs:
        copy.wait()


def local(adj, block_x, block_y, reduced_x, reduced_y, size_x, size_y):
    _, rows, cols = adj.shape
    nbx = block_x.shape[0] // size_x
    nby = block_y.shape[0] // size_y
    results = [
        ((rows, cols), f32),
        ((rows, cols), f32),
        ((rows, reduced_x.shape[0]), bf16),
        ((rows, reduced_x.shape[0]), bf16),
        ((reduced_y.shape[0], cols), bf16),
        ((reduced_y.shape[0], cols), bf16),
        ((8, reduced_x.shape[0]), f32),
    ]
    return pl.pallas_call(
        local_kernel,
        out_shape=tuple(pltpu.HBM(*result) for result in results),
        in_specs=[hbm_spec()] * 5,
        out_specs=(hbm_spec(),) * 7,
        scratch_shapes=[pltpu.VMEM(*result) for result in results]
        + [
            pltpu.VMEM((rows, cols), f32),
            pltpu.VMEM((rows, cols), f32),
            pltpu.VMEM((nbx, K, K), f32),
            pltpu.VMEM((nby, K, K), f32),
            pltpu.VMEM((8, K), f32),
            pltpu.VMEM((8, K), f32),
            pltpu.VMEM(reduced_x.shape, f32),
            pltpu.VMEM(reduced_y.shape, f32),
            pltpu.SemaphoreType.DMA((8,)),
            pltpu.SemaphoreType.DMA((7,)),
        ],
        compiler_params=pltpu.CompilerParams(vmem_limit_bytes=16 << 20),
        cost_estimate=cost(12 * rows * cols * K, 5 << 20),
        name="local",
    )(*in_hbm(adj, block_x, block_y, reduced_x, reduced_y))


def faults_kernel(
    wet_hbm, coef_hbm, footprint_hbm, owner_hbm,
    weights_hbm, high_hbm, low_hbm,
    weights, high_of, low_of, dist, coef8, wet, coef, footprint, owner, sems, out_sems,
):
    copies = [
        pltpu.make_async_copy(wet_hbm, wet, sems.at[0]),
        pltpu.make_async_copy(coef_hbm, coef, sems.at[1]),
        pltpu.make_async_copy(footprint_hbm, footprint, sems.at[2]),
        pltpu.make_async_copy(owner_hbm, owner, sems.at[3]),
    ]
    for copy in copies:
        copy.start()
    for copy in copies:
        copy.wait()
    u = lax.axis_index("gx")
    v = lax.axis_index("gy")
    tiles_y, tiles_x = wet.shape
    total_cols = tiles_y * lax.axis_size("gy")
    shift = total_cols.bit_length() - 1
    count = footprint.shape[1]
    places = footprint.shape[0]
    sub = iota((8, count), 0)
    for f in range(places):
        tile = footprint[f : f + 1, :]
        row = lax.shift_right_logical(tile, shift) - u * tiles_x
        col = (tile & (total_cols - 1)) - v * tiles_y
        inside = (row >= 0) & (row < tiles_x) & (col >= 0) & (col < tiles_y)
        flat = jnp.where(inside, col * tiles_x + row, -1000)
        dist[f] = flat - lax.shift_right_logical(sub, 2)
        four = coef[f]
        coef8[f] = jnp.concatenate([four, four], axis=0)

    def group(g, carry):
        acc = jnp.zeros((8, count), f32)
        for f in range(places):
            acc = acc + jnp.where(dist[f] == 2 * g, coef8[f], 0.0)
        col = (2 * g) // tiles_x
        row = 2 * g - col * tiles_x
        keep = jnp.where(sub < 4, wet[col, row].astype(f32), wet[col, row + 1].astype(f32))
        weights[pl.ds(pl.multiple_of(g * 8, 8), 8), :] = acc * keep
        return carry

    lax.fori_loop(0, tiles_x * tiles_y // 2, group, 0)
    own = owner[...]
    slots = low_of.shape[0]
    bits = slots.bit_length() - 1
    high_of[...] = (iota(high_of.shape, 0) == lax.shift_right_logical(own, bits)).astype(f32).astype(bf16)
    low_of[...] = (iota(low_of.shape, 0) == (own & (slots - 1))).astype(f32)
    outs = [
        pltpu.make_async_copy(weights, weights_hbm, out_sems.at[0]),
        pltpu.make_async_copy(high_of, high_hbm, out_sems.at[1]),
        pltpu.make_async_copy(low_of, low_hbm, out_sems.at[2]),
    ]
    for copy in outs:
        copy.start()
    for copy in outs:
        copy.wait()


def faults(wet, coef, footprint, owner, devices):
    tiles_x, tiles_y = wet.shape
    subf, places, modes = coef.shape
    slots = subf // devices
    results = [
        ((tiles_x * tiles_y * modes, subf), f32),
        ((devices, subf), bf16),
        ((slots, subf), f32),
    ]
    return pl.pallas_call(
        faults_kernel,
        out_shape=tuple(pltpu.HBM(*result) for result in results),
        in_specs=[hbm_spec()] * 4,
        out_specs=(hbm_spec(),) * 3,
        scratch_shapes=[pltpu.VMEM(*result) for result in results]
        + [
            pltpu.VMEM((places, 8, subf), jnp.int32),
            pltpu.VMEM((places, 8, subf), f32),
            pltpu.SMEM((tiles_y, tiles_x), jnp.int32),
            pltpu.VMEM((places, modes, subf), f32),
            pltpu.VMEM((places, subf), jnp.int32),
            pltpu.VMEM((1, subf), jnp.int32),
            pltpu.SemaphoreType.DMA((4,)),
            pltpu.SemaphoreType.DMA((3,)),
        ],
        compiler_params=pltpu.CompilerParams(vmem_limit_bytes=16 << 20),
        cost_estimate=cost(40 << 20, 3 << 20),
        name="faults",
    )(*in_hbm(wet.T, coef.transpose(1, 2, 0), footprint.T, owner.reshape(1, subf)))


def elev_kernel(
    tx_in, ta_in, tb_in, yx_in, yy_in, gxh_in, gxl_in, gyh_in, gyl_in, gside_in, adj, depth, basis_in,
    weights_in, high_in, low_in,
    elev_out, fx_out, fy_out, parts_out,
    tx, ty, yx, yy, gxh, gxl, gyh, gyl, gside, a0, dep, basis, weights, high_of, low_of,
    elev, fx, fy, tyn, mom, parts, sems, row_sems, out_sems,
):
    u = lax.axis_index("gx")
    v = lax.axis_index("gy")
    rows, cols = dep.shape
    steps = rows // K
    half = ta_in.shape[0]
    first = [
        pltpu.make_async_copy(tx_in, tx, sems.at[0]),
        pltpu.make_async_copy(ta_in, ty.at[pl.ds(0, half)], sems.at[1]),
        pltpu.make_async_copy(tb_in, ty.at[pl.ds(half, half)], sems.at[2]),
        pltpu.make_async_copy(gside_in, gside, sems.at[3]),
        pltpu.make_async_copy(gxh_in, gxh, sems.at[4]),
        pltpu.make_async_copy(gxl_in, gxl, sems.at[5]),
        pltpu.make_async_copy(gyh_in, gyh, sems.at[6]),
        pltpu.make_async_copy(gyl_in, gyl, sems.at[7]),
        pltpu.make_async_copy(basis_in, basis, sems.at[8]),
    ]
    last = [
        pltpu.make_async_copy(weights_in, weights, sems.at[9]),
        pltpu.make_async_copy(high_in, high_of, sems.at[10]),
        pltpu.make_async_copy(low_in, low_of, sems.at[11]),
    ]
    fields = []
    for r in range(steps):
        here = pl.ds(r * K, K)
        fields.append(
            [
                pltpu.make_async_copy(yx_in.at[here, :], yx.at[here, :], row_sems.at[r, 0]),
                pltpu.make_async_copy(yy_in.at[here, :], yy.at[here, :], row_sems.at[r, 1]),
                pltpu.make_async_copy(depth.at[here, :], dep.at[here, :], row_sems.at[r, 2]),
                pltpu.make_async_copy(adj.at[0, here, :], a0.at[here, :], row_sems.at[r, 3]),
            ]
        )
    for group in [first, *fields, last]:
        for copy in group:
            copy.start()
    for copy in first:
        copy.wait()
    nx = tx.shape[0]
    tx_all = jnp.concatenate([tx[d][:, :cols] for d in range(nx)], axis=0)
    for j in range(2 * half):
        tyn[j * 8 : (j + 1) * 8, :] = ty[j ^ v]
    ty_all = tyn[:, :rows]
    txs = halves(tx_all)
    tys = halves(ty_all)
    up = jnp.maximum(u - 1, 0)
    left = jnp.maximum(v - 1, 0)
    gs = gside[...]
    edge_x = mm3(halves(gs), txs, NN)[0:1, :]
    edge_y = mm3(halves(gs[:, : ty_all.shape[0]]), tys, NN)[1:2, :]
    drow = tx[up][:, cols:]
    drow = jnp.concatenate([drow[p : p + 1, :] for p in range(cols // K)], axis=1)
    dcol = tyn[pl.ds(pl.multiple_of(left * 8, 8), 8), rows:]
    dcol = jnp.concatenate([dcol[p : p + 1, :] for p in range(rows // K)], axis=1)
    carry = edge_x * drow
    side = halves(jnp.broadcast_to(edge_y * dcol, (8, rows)))
    row = iota((K, cols), 0)
    lane = iota((K, cols), 1)
    corner = ((iota((8, K), 1) == 0) & (iota((8, K), 0) == 0)).astype(f32).astype(bf16)
    modes, tile_h, tile_w = basis.shape
    per = K // tile_h
    wide = [jnp.concatenate([basis[b]] * (cols // tile_w), axis=1) for b in range(modes)]
    outs = []
    firsts = []
    for r in range(steps):
        here = slice(r * K, (r + 1) * K)
        for copy in fields[r]:
            copy.wait()
        d = dep[here, :]
        flux_x = yx[here, :] + mm3((gxh[here, :], gxl[here, :]), txs, NN)
        part = (tys[0][:, here], tys[1][:, here])
        flux_y = yy[here, :] + mm3(part, (gyh[...], gyl[...]), TN)
        fx[here, :] = flux_x
        fy[here, :] = flux_y
        weighted_x = d * flux_x
        weighted_y = d * flux_y
        before_x = jnp.where(row == 0, carry, pltpu.roll(weighted_x, 1, 0))
        carry = weighted_x[K - 1 : K, :]
        edge = mm(side[0][:, here], corner, TN) + mm(side[1][:, here], corner, TN)
        edge = jnp.concatenate([edge, jnp.zeros((K, cols - K), f32)], axis=1)
        before_y = jnp.where(lane == 0, edge, pltpu.roll(weighted_y, 1, 1))
        e = a0[here, :] + courant * ((weighted_x - before_x) + (weighted_y - before_y))
        elev[here, :] = e
        where = pl.ds(r * K, K)
        for i, (source, target) in enumerate(((elev, elev_out), (fx, fx_out), (fy, fy_out))):
            copy = pltpu.make_async_copy(source.at[where, :], target.at[where, :], out_sems.at[r, i])
            copy.start()
            outs.append(copy)
        if r == 0:
            top = e[0:1, :]
        eh, el = halves(e[:, :K])
        firsts.append((mm(corner, eh, NT) + mm(corner, el, NT))[0:1, :])
        for a in range(per):
            tile = e[a * tile_h : (a + 1) * tile_h, :]
            for b in range(modes):
                at = (r * per + a) * modes + b
                mom[at : at + 1, :] = jnp.sum(tile * wide[b], axis=0, keepdims=True)
    for copy in last:
        copy.wait()
    total = None
    group = mom.shape[0]
    for w in range(cols // tile_w):
        m = jnp.sum(mom[:, w * tile_w : (w + 1) * tile_w], axis=1, keepdims=True)
        term = jnp.sum(weights[w * group : (w + 1) * group, :] * m, axis=0, keepdims=True)
        total = term if total is None else total + term
    high, low = halves(low_of[...] * total)
    sums = mm(high_of[...], high, NT) + mm(high_of[...], low, NT)
    devices, slots = sums.shape
    parts[...] = jnp.zeros(parts.shape, f32)
    parts[pl.ds(0, devices, stride=8), :] = jnp.concatenate(
        [sums, jnp.zeros((devices, K - slots), f32)], axis=1
    )
    size_y = lax.axis_size("gy")

    def put(device, line):
        at = pl.ds(pl.multiple_of(device * 8, 8), 8)
        below = jnp.concatenate(
            [jnp.zeros((4, K), f32)] + [line[:, p * K : (p + 1) * K] for p in range(4)], axis=0
        )
        parts[at, :] = parts[at, :] + below

    @pl.when(u > 0)
    def _():
        put((u - 1) * size_y + v, top)

    @pl.when(v > 0)
    def _():
        put(u * size_y + v - 1, jnp.concatenate(firsts, axis=1))

    outs.append(pltpu.make_async_copy(parts, parts_out, sems.at[12]))
    outs[-1].start()
    for copy in outs:
        copy.wait()


def elevation(tx, ta, tb, solved, adj, depth, basis, weights, high_of, low_of):
    rows, cols = depth.shape
    modes, tile_h, tile_w = basis.shape
    devices = high_of.shape[0]
    steps = rows // K
    field = ((rows, cols), f32)
    far = (2 * ta.shape[0], 8, rows + EXTRA)
    parts = ((devices * 8, K), f32)
    like = lambda a: pltpu.VMEM(a.shape, a.dtype)
    return pl.pallas_call(
        elev_kernel,
        out_shape=(pltpu.HBM(*field),) * 3 + (pltpu.HBM(*parts),),
        in_specs=[pl.BlockSpec(memory_space=pl.ANY)] * 3 + [hbm_spec()] * 13,
        out_specs=(hbm_spec(),) * 4,
        scratch_shapes=[like(tx), pltpu.VMEM(far, f32)]
        + [like(a) for a in solved]
        + [pltpu.VMEM(*field)] * 2
        + [like(a) for a in (basis, weights, high_of, low_of)]
        + [pltpu.VMEM(*field)] * 3
        + [
            pltpu.VMEM((far[0] * 8, far[2]), f32),
            pltpu.VMEM((rows // tile_h * modes, cols), f32),
            pltpu.VMEM(*parts),
            pltpu.SemaphoreType.DMA((13,)),
            pltpu.SemaphoreType.DMA((steps, 4)),
            pltpu.SemaphoreType.DMA((steps, 3)),
        ],
        compiler_params=pltpu.CompilerParams(vmem_limit_bytes=32 << 20),
        cost_estimate=cost(12 * rows * cols * K, 10 << 20),
        name="elevation",
    )(tx, ta, tb, *in_hbm(*solved, adj, depth, basis, weights, high_of, low_of))


def fluxes_kernel(elev_in, fx_in, fy_in, out, e, x, y, sems, out_sems):
    rows, cols = e.shape
    steps = rows // K
    reads = []
    for r in range(steps):
        here = pl.ds(r * K, K)
        pairs = ((elev_in, e), (fx_in, x), (fy_in, y))
        reads.append(
            [
                pltpu.make_async_copy(source.at[here, :], target.at[here, :], sems.at[r, i])
                for i, (source, target) in enumerate(pairs)
            ]
        )
    for group in reads:
        for copy in group:
            copy.start()
    row = iota((K, cols), 0)
    lane = iota((K, cols), 1)
    writes = []
    for copy in reads[0]:
        copy.wait()
    for r in range(steps):
        here = slice(r * K, (r + 1) * K)
        after = 0.0
        if r + 1 < steps:
            for copy in reads[r + 1]:
                copy.wait()
            after = e[(r + 1) * K : (r + 1) * K + 1, :]
        now = e[here, :]
        below = jnp.where(row == K - 1, after, pltpu.roll(now, K - 1, 0))
        right = jnp.where(lane == cols - 1, 0.0, pltpu.roll(now, cols - 1, 1))
        x[here, :] = x[here, :] + courant * (below - now)
        y[here, :] = y[here, :] + courant * (right - now)
        where = pl.ds(r * K, K)
        for i, source in enumerate((e, x, y)):
            copy = pltpu.make_async_copy(source.at[where, :], out.at[i, where, :], out_sems.at[r, i])
            copy.start()
            writes.append(copy)
    for copy in writes:
        copy.wait()


def fluxes(elev, fx, fy):
    rows, cols = elev.shape
    return pl.pallas_call(
        fluxes_kernel,
        out_shape=pltpu.HBM((3, rows, cols), f32),
        in_specs=[hbm_spec()] * 3,
        out_specs=hbm_spec(),
        scratch_shapes=[
            pltpu.VMEM((rows, cols), f32),
            pltpu.VMEM((rows, cols), f32),
            pltpu.VMEM((rows, cols), f32),
            pltpu.SemaphoreType.DMA((rows // K, 3)),
            pltpu.SemaphoreType.DMA((rows // K, 3)),
        ],
        compiler_params=pltpu.CompilerParams(vmem_limit_bytes=16 << 20),
        cost_estimate=cost(10 * rows * cols, 6 << 20),
        name="fluxes",
    )(*in_hbm(elev, fx, fy))


def finish_kernel(fields_in, sums_in, fields, grad, sums, bottom, edge, sems, out_sems):
    u = lax.axis_index("gx")
    v = lax.axis_index("gy")
    size_x = lax.axis_size("gx")
    size_y = lax.axis_size("gy")
    rows, cols = fields.shape[1:]
    reads = [
        pltpu.make_async_copy(sums_in, sums, sems.at[0]),
        pltpu.make_async_copy(fields.at[1, pl.ds(rows - 8, 8), :], bottom, sems.at[1]),
        pltpu.make_async_copy(fields.at[2, :, pl.ds(cols - K, K)], edge, sems.at[2]),
    ]
    for copy in reads:
        copy.start()
    for copy in reads:
        copy.wait()

    def line(device):
        part = sums[pl.ds(pl.multiple_of(device * 8, 8), 8), :]
        return jnp.concatenate([part[4 + p : 5 + p, :] for p in range(4)], axis=1)

    below = line(jnp.minimum(u + 1, size_x - 1) * size_y + v) * jnp.where(u + 1 < size_x, courant, 0.0)
    right = line(u * size_y + jnp.minimum(v + 1, size_y - 1)) * jnp.where(v + 1 < size_y, courant, 0.0)
    bottom[7:8, :] = bottom[7:8, :] + below
    corner = ((iota((8, K), 1) == K - 1) & (iota((8, K), 0) == 0)).astype(f32).astype(bf16)
    high, low = halves(jnp.broadcast_to(right, (8, rows)))
    edge[...] = edge[...] + (mm(high, corner, TN) + mm(low, corner, TN))
    writes = [
        pltpu.make_async_copy(bottom, fields.at[1, pl.ds(rows - 8, 8), :], out_sems.at[0]),
        pltpu.make_async_copy(edge, fields.at[2, :, pl.ds(cols - K, K)], out_sems.at[1]),
    ]
    for copy in writes:
        copy.start()
    devices = sums.shape[0] // 8
    grad[...] = jnp.sum(sums[pl.ds(0, devices, stride=8), :], axis=0, keepdims=True)
    for copy in writes:
        copy.wait()


def finish(fields, sums):
    _, rows, cols = fields.shape
    return pl.pallas_call(
        finish_kernel,
        out_shape=(pltpu.HBM(fields.shape, f32), jax.ShapeDtypeStruct((1, K), f32)),
        in_specs=[hbm_spec(), pl.BlockSpec(memory_space=pl.ANY)],
        out_specs=(hbm_spec(), vmem_spec()),
        input_output_aliases={0: 0},
        scratch_shapes=[
            pltpu.VMEM(sums.shape, f32),
            pltpu.VMEM((8, cols), f32),
            pltpu.VMEM((rows, K), f32),
            pltpu.SemaphoreType.DMA((3,)),
            pltpu.SemaphoreType.DMA((2,)),
        ],
        compiler_params=pltpu.CompilerParams(vmem_limit_bytes=16 << 20),
        cost_estimate=cost(1 << 20, 1 << 20),
        name="finish",
    )(*in_hbm(fields), sums)


def partner(axis, bit):
    return [(i, i ^ bit) for i in range(lax.axis_size(axis))]


def body(
    adj_fields, depth, block_x, reduced_x, block_y, reduced_y, basis, coef, footprint, owner, wet
):
    size_x = lax.axis_size("gx")
    size_y = lax.axis_size("gy")
    px, py = ends(adj_fields, depth, block_x, block_y, size_x, size_y)
    tx = lax.all_to_all(px, "gx", split_axis=0, concat_axis=0, tiled=True)
    ty = py[None]
    bit = 1
    while 2 * bit < size_y:
        ty = jnp.concatenate([ty, lax.ppermute(ty, "gy", partner("gy", bit))], axis=0)
        bit *= 2
    ty_far = lax.ppermute(ty, "gy", partner("gy", bit))
    solved = local(adj_fields, block_x, block_y, reduced_x, reduced_y, size_x, size_y)
    chosen = faults(wet, coef, footprint, owner, size_x * size_y)
    elev, fx, fy, parts = elevation(tx, ty, ty_far, solved, adj_fields, depth, basis, *chosen)
    devices = size_x * size_y
    sums = lax.all_to_all(
        parts.reshape(devices, 8, K), ("gx", "gy"), split_axis=0, concat_axis=0, tiled=True
    )
    adj_before, grad = finish(fluxes(elev, fx, fy), sums.reshape(parts.shape))
    return adj_before, grad[0, : owner.shape[0] // devices]


def solution(mesh):
    in_specs = (
        P(None, "gx", "gy"),
        P("gx", "gy"),
        P(),
        P(),
        P(),
        P(),
        P(),
        P(),
        P(),
        P(),
        P("gx", "gy"),
    )
    out_specs = (P(None, "gx", "gy"), P(("gx", "gy")))
    return jax.shard_map(body, mesh=mesh, in_specs=in_specs, out_specs=out_specs, check_vma=False)
```

```python
import jax
import jax.numpy as jnp
from jax import lax
from jax.experimental import pallas as pl
from jax.experimental.pallas import tpu as pltpu
from jax.sharding import PartitionSpec as P

courant = 0.5
f32 = jnp.float32
bf16 = jnp.bfloat16
K = 128
EXTRA = 128

NN = (((1,), (0,)), ((), ()))
NT = (((1,), (1,)), ((), ()))
TN = (((0,), (0,)), ((), ()))


def halves(x):
    high = x.astype(bf16)
    return high, (x - high.astype(f32)).astype(bf16)


def mm(a, b, dims):
    return lax.dot_general(a, b, dims, preferred_element_type=f32)


def mm3(a, b, dims):
    ah, al = a
    bh, bl = b
    return mm(ah, bh, dims) + (mm(ah, bl, dims) + mm(al, bh, dims))


def exact(a, b, dims):
    return lax.dot_general(a, b, dims, precision=lax.Precision.HIGHEST, preferred_element_type=f32)


def iota(shape, dim):
    return lax.broadcasted_iota(jnp.int32, shape, dim)


def hbm_spec():
    return pl.BlockSpec(memory_space=pltpu.HBM)


def vmem_spec():
    return pl.BlockSpec(memory_space=pltpu.VMEM)


def in_hbm(*arrays):
    return tuple(pltpu.with_memory_space_constraint(a, pltpu.HBM) for a in arrays)


def in_vmem(*arrays):
    return tuple(pltpu.with_memory_space_constraint(a, pltpu.VMEM) for a in arrays)


def cost(flops, nbytes):
    return pl.CostEstimate(flops=flops, bytes_accessed=nbytes, transcendentals=0)


def stacked(first, last, c):
    high, low = halves(jnp.concatenate([first[c, 0:1, :], last[c, 7:8, :]], axis=0))
    return jnp.concatenate([high, low], axis=0)


def two_rows(weights, field, dims):
    high, low = halves(field)
    both = mm(weights, high, dims)
    return both[0:2] + both[2:4] + mm(weights[0:2], low, dims)


def block_ends(blocks, index, first, last, sems):
    here = pl.ds(index * first.shape[0], first.shape[0])
    return [
        pltpu.make_async_copy(blocks.at[here, pl.ds(0, 8), :], first, sems.at[0]),
        pltpu.make_async_copy(blocks.at[here, pl.ds(K - 8, 8), :], last, sems.at[1]),
    ]


def ends_x_kernel(adj, depth, block_x, px_hbm, vx, first, last, drow, px, sems, row_sems, out_sems):
    rows, cols = vx.shape
    count = first.shape[0]
    small = block_ends(block_x, lax.axis_index("gx"), first, last, sems)
    small.append(pltpu.make_async_copy(depth.at[pl.ds(rows - 8, 8), :], drow, sems.at[2]))
    big = []
    for c in range(count):
        here = pl.ds(c * K, K)
        big.append(pltpu.make_async_copy(adj.at[1, here, :], vx.at[here, :], row_sems.at[c]))
    for copy in small + big:
        copy.start()
    for copy in small:
        copy.wait()
    for part in range(cols // K):
        px[part : part + 1, cols:] = drow[7:8, part * K : (part + 1) * K]
    px[cols // K :, cols:] = jnp.zeros((8 - cols // K, EXTRA), f32)
    weights = [stacked(first, last, c) for c in range(count)]
    for c in range(count):
        big[c].wait()
        px[2 * c : 2 * c + 2, :cols] = two_rows(weights[c], vx[c * K : (c + 1) * K, :], NN)
    outs = [pltpu.make_async_copy(px, px_hbm.at[d], out_sems.at[d]) for d in range(px_hbm.shape[0])]
    for copy in outs:
        copy.start()
    for copy in outs:
        copy.wait()


def ends_x(adj, depth, block_x, size_x):
    rows, cols = depth.shape
    count = block_x.shape[0] // size_x
    shape = (2 * count, cols + EXTRA)
    return pl.pallas_call(
        ends_x_kernel,
        out_shape=pltpu.HBM((size_x, *shape), f32),
        in_specs=[hbm_spec()] * 3,
        out_specs=hbm_spec(),
        scratch_shapes=[
            pltpu.VMEM((rows, cols), f32),
            pltpu.VMEM((count, 8, K), f32),
            pltpu.VMEM((count, 8, K), f32),
            pltpu.VMEM((8, cols), f32),
            pltpu.VMEM(shape, f32),
            pltpu.SemaphoreType.DMA((3,)),
            pltpu.SemaphoreType.DMA((count,)),
            pltpu.SemaphoreType.DMA((size_x,)),
        ],
        compiler_params=pltpu.CompilerParams(vmem_limit_bytes=16 << 20),
        cost_estimate=cost(2 * rows * cols * 16, 2 << 20),
        name="ends_x",
    )(*in_hbm(adj, depth, block_x))


def ends_y_kernel(adj, depth, block_y, py, vy, first, last, dcol, sems, row_sems):
    rows, cols = vy.shape
    count = first.shape[0]
    small = block_ends(block_y, lax.axis_index("gy"), first, last, sems)
    side = pltpu.make_async_copy(depth.at[:, pl.ds(cols - K, K)], dcol, sems.at[2])
    big = []
    for r in range(rows // K):
        here = pl.ds(r * K, K)
        big.append(pltpu.make_async_copy(adj.at[2, here, :], vy.at[here, :], row_sems.at[r]))
    for copy in small + big + [side]:
        copy.start()
    for copy in small:
        copy.wait()
    weights = [stacked(first, last, c) for c in range(count)]
    for r in range(rows // K):
        big[r].wait()
        for c in range(count):
            field = vy[r * K : (r + 1) * K, c * K : (c + 1) * K]
            py[2 * c : 2 * c + 2, r * K : (r + 1) * K] = two_rows(weights[c], field, NT)
    side.wait()
    at_last = (iota((8, K), 1) == K - 1).astype(f32).astype(bf16)
    high, low = halves(dcol[...])
    line = mm(at_last, high, NT) + mm(at_last, low, NT)
    for part in range(rows // K):
        py[part : part + 1, rows:] = line[0:1, part * K : (part + 1) * K]
    py[rows // K :, rows:] = jnp.zeros((8 - rows // K, EXTRA), f32)


def ends_y(adj, depth, block_y, size_y):
    rows, cols = depth.shape
    count = block_y.shape[0] // size_y
    return pl.pallas_call(
        ends_y_kernel,
        out_shape=jax.ShapeDtypeStruct((2 * count, rows + EXTRA), f32),
        in_specs=[hbm_spec()] * 3,
        out_specs=vmem_spec(),
        scratch_shapes=[
            pltpu.VMEM((rows, cols), f32),
            pltpu.VMEM((count, 8, K), f32),
            pltpu.VMEM((count, 8, K), f32),
            pltpu.VMEM((rows, K), f32),
            pltpu.SemaphoreType.DMA((3,)),
            pltpu.SemaphoreType.DMA((rows // K,)),
        ],
        compiler_params=pltpu.CompilerParams(vmem_limit_bytes=16 << 20),
        cost_estimate=cost(2 * rows * cols * 16, 2 << 20),
        name="ends_y",
    )(*in_hbm(adj, depth, block_y))


def carry_kernel(
    block_x, block_y, reduced_x_hbm, reduced_y_hbm,
    gx_hbm, gy_hbm, gside_hbm,
    gx, gy, gside, wx, wy, wpx, wpy, reduced_x, reduced_y, sems, out_sems,
):
    u = lax.axis_index("gx")
    v = lax.axis_index("gy")
    nbx = wx.shape[0]
    nby = wy.shape[0]
    before_x = jnp.maximum(u * nbx - 1, 0)
    before_y = jnp.maximum(v * nby - 1, 0)
    copies = [
        pltpu.make_async_copy(reduced_x_hbm, reduced_x, sems.at[4]),
        pltpu.make_async_copy(reduced_y_hbm, reduced_y, sems.at[5]),
        pltpu.make_async_copy(block_y.at[pl.ds(v * nby, nby)], wy, sems.at[1]),
        pltpu.make_async_copy(block_x.at[before_x, pl.ds(K - 8, 8), :], wpx, sems.at[2]),
        pltpu.make_async_copy(block_y.at[before_y, pl.ds(K - 8, 8), :], wpy, sems.at[3]),
        pltpu.make_async_copy(block_x.at[pl.ds(u * nbx, nbx)], wx, sems.at[0]),
    ]
    for copy in copies:
        copy.start()
    for copy in copies[:3]:
        copy.wait()
    own_x = reduced_x[pl.ds(pl.multiple_of(u * 8, 8), 8), :]
    own_y = reduced_y[pl.ds(pl.multiple_of(v * 8, 8), 8), :]
    prev_x = reduced_x[pl.ds(pl.multiple_of(jnp.maximum(u - 1, 0) * 8, 8), 8), :]
    prev_y = reduced_y[pl.ds(pl.multiple_of(jnp.maximum(v - 1, 0) * 8, 8), 8), :]
    row = iota((8, K), 0)
    lane = iota((8, K), 1)
    own = halves(own_y)
    for c in range(nby):
        pick = ((row == 2 * c) & (lane == 0)) | ((row == 2 * c + 1) & (lane == K - 1))
        pick = pick.astype(f32).astype(bf16)
        high, low = halves(wy[c])
        across = mm(pick, high, NT) + mm(pick, low, NT)
        gy[:, c * K : (c + 1) * K] = mm3(own, halves(across), TN)
    for copy in copies[3:]:
        copy.wait()
    for c in range(nbx):
        w = wx[c]
        gx[c * K : (c + 1) * K, :] = (
            w[:, 0:1] * own_x[2 * c : 2 * c + 1, :] + w[:, K - 1 : K] * own_x[2 * c + 1 : 2 * c + 2, :]
        )

    def side(w, prev, index):
        width = prev.shape[1]
        g = w[7:8, 0:1] * prev[6:7, :] + w[7:8, K - 1 : K] * prev[7:8, :]
        g = g + (iota((1, width), 1) == index * 8 - 1).astype(f32)
        return jnp.where(index > 0, g, 0.0)

    gside[...] = jnp.zeros(gside.shape, f32)
    gside[0:1, :] = side(wpx[...], prev_x, u)
    gside[1:2, : reduced_y.shape[1]] = side(wpy[...], prev_y, v)
    outs = [
        pltpu.make_async_copy(gx, gx_hbm, out_sems.at[0]),
        pltpu.make_async_copy(gy, gy_hbm, out_sems.at[1]),
        pltpu.make_async_copy(gside, gside_hbm, out_sems.at[2]),
    ]
    for copy in outs:
        copy.start()
    for copy in outs:
        copy.wait()


def carry(block_x, block_y, reduced_x, reduced_y, size_x, size_y):
    nbx = block_x.shape[0] // size_x
    nby = block_y.shape[0] // size_y
    results = [
        ((nbx * K, reduced_x.shape[0]), f32),
        ((reduced_y.shape[0], nby * K), f32),
        ((8, reduced_x.shape[0]), f32),
    ]
    return pl.pallas_call(
        carry_kernel,
        out_shape=tuple(pltpu.HBM(*result) for result in results),
        in_specs=[hbm_spec()] * 4,
        out_specs=(hbm_spec(),) * 3,
        scratch_shapes=[pltpu.VMEM(*result) for result in results]
        + [
            pltpu.VMEM((nbx, K, K), f32),
            pltpu.VMEM((nby, K, K), f32),
            pltpu.VMEM((8, K), f32),
            pltpu.VMEM((8, K), f32),
            pltpu.VMEM(reduced_x.shape, f32),
            pltpu.VMEM(reduced_y.shape, f32),
            pltpu.SemaphoreType.DMA((6,)),
            pltpu.SemaphoreType.DMA((3,)),
        ],
        compiler_params=pltpu.CompilerParams(vmem_limit_bytes=16 << 20),
        cost_estimate=cost(1 << 24, 2 << 20),
        name="carry",
    )(*in_hbm(block_x, block_y, reduced_x, reduced_y))


def elev_kernel(
    tx, ta_in, tb_in, gside_in, gx_in, gy_in, block_x, block_y, adj, depth, basis_in,
    wet_in, coef_in, footprint_in, owner_in,
    elev_out, fx_out, fy_out, parts_out,
    ty, gside, gx, gy, wx, wy, vx, vy, a0, dep, basis, wet, coef, footprint, owner,
    elev, fx, fy, tyn, mom, parts, sems, row_sems, out_sems,
):
    u = lax.axis_index("gx")
    v = lax.axis_index("gy")
    rows, cols = dep.shape
    steps = rows // K
    half = ta_in.shape[0]
    nbx = wx.shape[0]
    nby = wy.shape[0]
    first = [
        pltpu.make_async_copy(ta_in, ty.at[pl.ds(0, half)], sems.at[0]),
        pltpu.make_async_copy(tb_in, ty.at[pl.ds(half, half)], sems.at[1]),
        pltpu.make_async_copy(gside_in, gside, sems.at[2]),
        pltpu.make_async_copy(gy_in, gy, sems.at[3]),
        pltpu.make_async_copy(block_y.at[pl.ds(v * nby, nby)], wy, sems.at[4]),
        pltpu.make_async_copy(gx_in, gx, sems.at[5]),
        pltpu.make_async_copy(block_x.at[pl.ds(u * nbx, nbx)], wx, sems.at[6]),
        pltpu.make_async_copy(basis_in, basis, sems.at[7]),
    ]
    last = [
        pltpu.make_async_copy(wet_in, wet, sems.at[8]),
        pltpu.make_async_copy(coef_in, coef, sems.at[9]),
        pltpu.make_async_copy(footprint_in, footprint, sems.at[10]),
        pltpu.make_async_copy(owner_in, owner, sems.at[11]),
    ]
    fields = []
    for r in range(steps):
        here = pl.ds(r * K, K)
        fields.append(
            [
                pltpu.make_async_copy(adj.at[1, here, :], vx.at[here, :], row_sems.at[r, 0]),
                pltpu.make_async_copy(adj.at[2, here, :], vy.at[here, :], row_sems.at[r, 1]),
                pltpu.make_async_copy(depth.at[here, :], dep.at[here, :], row_sems.at[r, 2]),
                pltpu.make_async_copy(adj.at[0, here, :], a0.at[here, :], row_sems.at[r, 3]),
            ]
        )
    for group in [first, *fields, last]:
        for copy in group:
            copy.start()
    for copy in first:
        copy.wait()
    tx_all = jnp.concatenate([tx[d][:, :cols] for d in range(tx.shape[0])], axis=0)
    for j in range(2 * half):
        tyn[j * 8 : (j + 1) * 8, :] = ty[j ^ v]
    ty_all = tyn[:, :rows]
    txs = halves(tx_all)
    tys = halves(ty_all)
    tyt = halves(ty_all.T)
    up = jnp.maximum(u - 1, 0)
    left = jnp.maximum(v - 1, 0)
    gs = gside[...]
    edge_x = mm3(halves(gs), txs, NN)[0:1, :]
    edge_y = mm3(halves(gs[:, : ty_all.shape[0]]), tys, NN)[1:2, :]
    drow = tx[up][:, cols:]
    drow = jnp.concatenate([drow[p : p + 1, :] for p in range(cols // K)], axis=1)
    dcol = tyn[pl.ds(pl.multiple_of(left * 8, 8), 8), rows:]
    dcol = jnp.concatenate([dcol[p : p + 1, :] for p in range(rows // K)], axis=1)
    carry = edge_x * drow
    side = halves(jnp.broadcast_to(edge_y * dcol, (8, rows)))
    row = iota((K, cols), 0)
    lane = iota((K, K), 1)
    corner = ((iota((8, K), 1) == 0) & (iota((8, K), 0) == 0)).astype(f32).astype(bf16)
    modes, tile_h, tile_w = basis.shape
    per = K // tile_h
    outs = []
    firsts = []
    to_y = []
    for c in range(nby):
        wh, wl = halves(wy[c].T)
        gh, gl = halves(gy[:, c * K : (c + 1) * K])
        to_y.append((jnp.concatenate([wh, gh], axis=0), jnp.concatenate([wl, gl], axis=0)))
    for r in range(steps):
        here = slice(r * K, (r + 1) * K)
        for copy in fields[r]:
            copy.wait()
        d = dep[here, :]
        wh, wl = halves(wx[r])
        gh, gl = halves(gx[here, :])
        vh, vl = halves(vx[here, :])
        flux_x = mm3(
            (jnp.concatenate([wh, gh], axis=1), jnp.concatenate([wl, gl], axis=1)),
            (jnp.concatenate([vh, txs[0]], axis=0), jnp.concatenate([vl, txs[1]], axis=0)),
            NN,
        )
        pieces = []
        for c in range(nby):
            vh, vl = halves(vy[here, c * K : (c + 1) * K])
            lhs = (
                jnp.concatenate([vh, tyt[0][here, :]], axis=1),
                jnp.concatenate([vl, tyt[1][here, :]], axis=1),
            )
            pieces.append(mm3(lhs, to_y[c], NN))
        flux_y = jnp.concatenate(pieces, axis=1)
        fx[here, :] = flux_x
        fy[here, :] = flux_y
        weighted_x = d * flux_x
        weighted_y = d * flux_y
        before_x = jnp.where(row == 0, carry, pltpu.roll(weighted_x, 1, 0))
        carry = weighted_x[K - 1 : K, :]
        edge = mm(side[0][:, here], corner, TN) + mm(side[1][:, here], corner, TN)
        turned = [edge] + [
            pltpu.roll(weighted_y[:, c * K : (c + 1) * K], 1, 1) for c in range(cols // K)
        ]
        before_y = jnp.concatenate(
            [jnp.where(lane == 0, turned[c], turned[c + 1]) for c in range(cols // K)], axis=1
        )
        e = a0[here, :] + courant * ((weighted_x - before_x) + (weighted_y - before_y))
        elev[here, :] = e
        where = pl.ds(r * K, K)
        for i, (source, target) in enumerate(((elev, elev_out), (fx, fx_out), (fy, fy_out))):
            copy = pltpu.make_async_copy(source.at[where, :], target.at[where, :], out_sems.at[r, i])
            copy.start()
            outs.append(copy)
        if r == 0:
            top = e[0:1, :]
        eh, el = halves(e[:, :K])
        firsts.append((mm(corner, eh, NT) + mm(corner, el, NT))[0:1, :])
        for a in range(per):
            for w in range(cols // tile_w):
                tile = e[a * tile_h : (a + 1) * tile_h, w * tile_w : (w + 1) * tile_w]
                for b in range(modes):
                    at = b * (rows // tile_h) + r * per + a
                    mom[at : at + 1, w * tile_w : (w + 1) * tile_w] = jnp.sum(
                        tile * basis[b], axis=0, keepdims=True
                    )
    for copy in last:
        copy.wait()
    tiles_y, tiles_x = wet.shape
    count = footprint.shape[1]
    places = footprint.shape[0]
    ones = jnp.ones((8, tile_w), bf16)
    pieces = []
    for w in range(tiles_y):
        high, low = halves(mom[:, w * tile_w : (w + 1) * tile_w])
        line = (mm(ones, high, NT) + mm(ones, low, NT))[0:1, :]
        keep = wet[w : w + 1, :].astype(f32)
        for b in range(modes):
            pieces.append(line[:, b * tiles_x : (b + 1) * tiles_x] * keep)
    high, low = halves(jnp.concatenate(pieces, axis=0))
    table = jnp.concatenate([high, low], axis=0)
    number = footprint[...]
    total_cols = tiles_y * lax.axis_size("gy")
    local_row = lax.shift_right_logical(number, total_cols.bit_length() - 1) - u * tiles_x
    local_col = (number & (total_cols - 1)) - v * tiles_y
    lines = tiles_y * modes
    tile_row = iota((tiles_x, count), 0)
    tile_col = lax.shift_right_logical(iota((lines, count), 0), modes.bit_length() - 1)
    acc = jnp.zeros((lines, count), f32)
    for f in range(places):
        at_row = (tile_row == local_row[f : f + 1, :]).astype(f32).astype(bf16)
        both = mm(table, at_row, NN)
        four = coef[f]
        scale = jnp.concatenate([four] * tiles_y, axis=0)
        hit = tile_col == local_col[f : f + 1, :]
        acc = acc + jnp.where(hit, (both[:lines] + both[lines:]) * scale, 0.0)
    total = jnp.sum(acc, axis=0, keepdims=True)
    devices = parts.shape[0] // 5
    slots = count // devices
    own = owner[...]
    slot_of = (iota((slots, count), 0) == (own & (slots - 1))).astype(f32)
    device_of = iota((devices, count), 0) == lax.shift_right_logical(own, slots.bit_length() - 1)
    device_of = device_of.astype(f32).astype(bf16)
    high, low = halves(slot_of * total)
    sums = mm(device_of, high, NT) + mm(device_of, low, NT)
    parts[...] = jnp.zeros(parts.shape, f32)
    parts[pl.ds(0, devices, stride=5), :] = jnp.concatenate(
        [sums, jnp.zeros((devices, K - slots), f32)], axis=1
    )
    size_y = lax.axis_size("gy")

    def put(device, line):
        for p in range(4):
            parts[pl.ds(device * 5 + 1 + p, 1), :] = line[:, p * K : (p + 1) * K]

    @pl.when(u > 0)
    def _():
        put((u - 1) * size_y + v, top)

    @pl.when(v > 0)
    def _():
        put(u * size_y + v - 1, jnp.concatenate(firsts, axis=1))

    outs.append(pltpu.make_async_copy(parts, parts_out, sems.at[12]))
    outs[-1].start()
    for copy in outs:
        copy.wait()


def elevation(tx, ta, tb, gx, gy, gside, block_x, block_y, adj, depth, basis, wet, coef, footprint, owner):
    rows, cols = depth.shape
    modes, tile_h, tile_w = basis.shape
    devices = lax.axis_size("gx") * lax.axis_size("gy")
    steps = rows // K
    wet = wet.T
    coef = coef.transpose(1, 2, 0)
    footprint = footprint.T
    owner = owner.reshape(1, -1)
    field = ((rows, cols), f32)
    far = (2 * ta.shape[0], 8, rows + EXTRA)
    parts = ((devices * 5, K), f32)
    like = lambda *arrays: [pltpu.VMEM(a.shape, a.dtype) for a in arrays]
    return pl.pallas_call(
        elev_kernel,
        out_shape=(pltpu.HBM(*field),) * 3 + (pltpu.HBM(*parts),),
        in_specs=[vmem_spec()] + [pl.BlockSpec(memory_space=pl.ANY)] * 2 + [hbm_spec()] * 12,
        out_specs=(hbm_spec(),) * 4,
        scratch_shapes=[pltpu.VMEM(far, f32)]
        + like(gside, gx, gy)
        + [pltpu.VMEM((rows // K, K, K), f32), pltpu.VMEM((cols // K, K, K), f32)]
        + [pltpu.VMEM(*field)] * 4
        + like(basis, wet, coef, footprint, owner)
        + [pltpu.VMEM(*field)] * 3
        + [
            pltpu.VMEM((far[0] * 8, far[2]), f32),
            pltpu.VMEM((rows // tile_h * modes, cols), f32),
            pltpu.VMEM(*parts),
            pltpu.SemaphoreType.DMA((13,)),
            pltpu.SemaphoreType.DMA((steps, 4)),
            pltpu.SemaphoreType.DMA((steps, 3)),
        ],
        compiler_params=pltpu.CompilerParams(vmem_limit_bytes=32 << 20),
        cost_estimate=cost(12 * rows * cols * K, 10 << 20),
        name="elevation",
    )(
        tx,
        ta,
        tb,
        *in_hbm(gside, gx, gy, block_x, block_y, adj, depth, basis, wet, coef, footprint, owner),
    )


def fluxes_kernel(elev_in, fx_in, fy_in, out, e, x, y, sems, out_sems):
    rows, cols = e.shape
    steps = rows // K
    reads = []
    for r in range(steps):
        here = pl.ds(r * K, K)
        pairs = ((elev_in, e), (fx_in, x), (fy_in, y))
        reads.append(
            [
                pltpu.make_async_copy(source.at[here, :], target.at[here, :], sems.at[r, i])
                for i, (source, target) in enumerate(pairs)
            ]
        )
    for group in reads:
        for copy in group:
            copy.start()
    row = iota((K, cols), 0)
    lane = iota((K, cols), 1)
    writes = []
    for copy in reads[0]:
        copy.wait()
    for r in range(steps):
        here = slice(r * K, (r + 1) * K)
        after = 0.0
        if r + 1 < steps:
            for copy in reads[r + 1]:
                copy.wait()
            after = e[(r + 1) * K : (r + 1) * K + 1, :]
        now = e[here, :]
        below = jnp.where(row == K - 1, after, pltpu.roll(now, K - 1, 0))
        right = jnp.where(lane == cols - 1, 0.0, pltpu.roll(now, cols - 1, 1))
        x[here, :] = x[here, :] + courant * (below - now)
        y[here, :] = y[here, :] + courant * (right - now)
        where = pl.ds(r * K, K)
        for i, source in enumerate((e, x, y)):
            copy = pltpu.make_async_copy(source.at[where, :], out.at[i, where, :], out_sems.at[r, i])
            copy.start()
            writes.append(copy)
    for copy in writes:
        copy.wait()


def fluxes(elev, fx, fy):
    rows, cols = elev.shape
    return pl.pallas_call(
        fluxes_kernel,
        out_shape=pltpu.HBM((3, rows, cols), f32),
        in_specs=[hbm_spec()] * 3,
        out_specs=hbm_spec(),
        scratch_shapes=[
            pltpu.VMEM((rows, cols), f32),
            pltpu.VMEM((rows, cols), f32),
            pltpu.VMEM((rows, cols), f32),
            pltpu.SemaphoreType.DMA((rows // K, 3)),
            pltpu.SemaphoreType.DMA((rows // K, 3)),
        ],
        compiler_params=pltpu.CompilerParams(vmem_limit_bytes=16 << 20),
        cost_estimate=cost(10 * rows * cols, 6 << 20),
        name="fluxes",
    )(*in_hbm(elev, fx, fy))


def finish_kernel(fields_in, sums, fields, grad, bottom, edge, sems, out_sems):
    u = lax.axis_index("gx")
    v = lax.axis_index("gy")
    size_x = lax.axis_size("gx")
    size_y = lax.axis_size("gy")
    rows, cols = fields.shape[1:]
    reads = [
        pltpu.make_async_copy(fields.at[1, pl.ds(rows - 8, 8), :], bottom, sems.at[0]),
        pltpu.make_async_copy(fields.at[2, :, pl.ds(cols - K, K)], edge, sems.at[1]),
    ]
    for copy in reads:
        copy.start()

    def line(device):
        return jnp.concatenate([sums[pl.ds(device * 5 + 1 + p, 1), :] for p in range(4)], axis=1)

    below = line(jnp.minimum(u + 1, size_x - 1) * size_y + v) * jnp.where(u + 1 < size_x, courant, 0.0)
    right = line(u * size_y + jnp.minimum(v + 1, size_y - 1)) * jnp.where(v + 1 < size_y, courant, 0.0)
    devices = sums.shape[0] // 5
    total = jnp.sum(sums[pl.ds(0, devices, stride=5), :], axis=0, keepdims=True)
    grad[...] = total[:, : grad.shape[1]]
    corner = ((iota((8, K), 1) == K - 1) & (iota((8, K), 0) == 0)).astype(f32).astype(bf16)
    high, low = halves(jnp.broadcast_to(right, (8, rows)))
    for copy in reads:
        copy.wait()
    bottom[7:8, :] = bottom[7:8, :] + below
    edge[...] = edge[...] + (mm(high, corner, TN) + mm(low, corner, TN))
    writes = [
        pltpu.make_async_copy(bottom, fields.at[1, pl.ds(rows - 8, 8), :], out_sems.at[0]),
        pltpu.make_async_copy(edge, fields.at[2, :, pl.ds(cols - K, K)], out_sems.at[1]),
    ]
    for copy in writes:
        copy.start()
    for copy in writes:
        copy.wait()


def finish(fields, sums, slots):
    _, rows, cols = fields.shape
    return pl.pallas_call(
        finish_kernel,
        out_shape=(pltpu.HBM(fields.shape, f32), jax.ShapeDtypeStruct((1, slots), f32)),
        in_specs=[hbm_spec(), vmem_spec()],
        out_specs=(hbm_spec(), vmem_spec()),
        input_output_aliases={0: 0},
        scratch_shapes=[
            pltpu.VMEM((8, cols), f32),
            pltpu.VMEM((rows, K), f32),
            pltpu.SemaphoreType.DMA((2,)),
            pltpu.SemaphoreType.DMA((2,)),
        ],
        compiler_params=pltpu.CompilerParams(vmem_limit_bytes=16 << 20),
        cost_estimate=cost(1 << 20, 1 << 20),
        name="finish",
    )(*in_hbm(fields), sums)


def partner(axis, bit):
    return [(i, i ^ bit) for i in range(lax.axis_size(axis))]


def body(
    adj_fields, depth, block_x, reduced_x, block_y, reduced_y, basis, coef, footprint, owner, wet
):
    size_x = lax.axis_size("gx")
    size_y = lax.axis_size("gy")
    ty = ends_y(adj_fields, depth, block_y, size_y)[None]
    px = ends_x(adj_fields, depth, block_x, size_x)
    tx = lax.all_to_all(px, "gx", split_axis=0, concat_axis=0, tiled=True)
    bit = 1
    while 2 * bit < size_y:
        ty = jnp.concatenate([ty, lax.ppermute(ty, "gy", partner("gy", bit))], axis=0)
        bit *= 2
    ty_far = lax.ppermute(ty, "gy", partner("gy", bit))
    carried = carry(block_x, block_y, reduced_x, reduced_y, size_x, size_y)
    elev, fx, fy, parts = elevation(
        tx, ty, ty_far, *carried, block_x, block_y, adj_fields, depth, basis, wet, coef, footprint, owner
    )
    devices = size_x * size_y
    sums = lax.all_to_all(
        parts[:, None, :], ("gx", "gy"), split_axis=0, concat_axis=0, tiled=True
    )
    slots = owner.shape[0] // devices
    adj_before, grad = finish(fluxes(elev, fx, fy), sums[:, 0, :], slots)
    return adj_before, grad.reshape(slots)


def solution(mesh):
    in_specs = (
        P(None, "gx", "gy"),
        P("gx", "gy"),
        P(),
        P(),
        P(),
        P(),
        P(),
        P(),
        P(),
        P(),
        P("gx", "gy"),
    )
    out_specs = (P(None, "gx", "gy"), P(("gx", "gy")))
    return jax.shard_map(body, mesh=mesh, in_specs=in_specs, out_specs=out_specs, check_vma=False)
```

```python
import jax
import jax.numpy as jnp
from jax import lax
from jax.experimental import pallas as pl
from jax.experimental.pallas import tpu as pltpu
from jax.sharding import PartitionSpec as P

courant = 0.5
f32 = jnp.float32
bf16 = jnp.bfloat16
K = 128
EXTRA = 128

NN = (((1,), (0,)), ((), ()))
NT = (((1,), (1,)), ((), ()))
TN = (((0,), (0,)), ((), ()))


def halves(x):
    high = x.astype(bf16)
    return high, (x - high.astype(f32)).astype(bf16)


def mm(a, b, dims):
    return lax.dot_general(a, b, dims, preferred_element_type=f32)


def mm3(a, b, dims):
    ah, al = a
    bh, bl = b
    return mm(ah, bh, dims) + (mm(ah, bl, dims) + mm(al, bh, dims))


def exact(a, b, dims):
    return lax.dot_general(a, b, dims, precision=lax.Precision.HIGHEST, preferred_element_type=f32)


def iota(shape, dim):
    return lax.broadcasted_iota(jnp.int32, shape, dim)


def hbm_spec():
    return pl.BlockSpec(memory_space=pltpu.HBM)


def vmem_spec():
    return pl.BlockSpec(memory_space=pltpu.VMEM)


def in_hbm(*arrays):
    return tuple(pltpu.with_memory_space_constraint(a, pltpu.HBM) for a in arrays)


def in_vmem(*arrays):
    return tuple(pltpu.with_memory_space_constraint(a, pltpu.VMEM) for a in arrays)


def cost(flops, nbytes):
    return pl.CostEstimate(flops=flops, bytes_accessed=nbytes, transcendentals=0)


def stacked(first, last, c):
    high, low = halves(jnp.concatenate([first[c, 0:1, :], last[c, 7:8, :]], axis=0))
    return jnp.concatenate([high, low], axis=0)


def two_rows(weights, field, dims):
    high, low = halves(field)
    both = mm(weights, high, dims)
    return both[0:2] + both[2:4] + mm(weights[0:2], low, dims)


def block_ends(blocks, index, first, last, sems):
    here = pl.ds(index * first.shape[0], first.shape[0])
    return [
        pltpu.make_async_copy(blocks.at[here, pl.ds(0, 8), :], first, sems.at[0]),
        pltpu.make_async_copy(blocks.at[here, pl.ds(K - 8, 8), :], last, sems.at[1]),
    ]


def ends_x_kernel(adj, depth, block_x, px_hbm, vx, first, last, drow, px, sems, row_sems, out_sems):
    rows, cols = vx.shape
    count = first.shape[0]
    small = block_ends(block_x, lax.axis_index("gx"), first, last, sems)
    small.append(pltpu.make_async_copy(depth.at[pl.ds(rows - 8, 8), :], drow, sems.at[2]))
    big = []
    for c in range(count):
        here = pl.ds(c * K, K)
        big.append(pltpu.make_async_copy(adj.at[1, here, :], vx.at[here, :], row_sems.at[c]))
    for copy in small + big:
        copy.start()
    for copy in small:
        copy.wait()
    for part in range(cols // K):
        px[part : part + 1, cols:] = drow[7:8, part * K : (part + 1) * K]
    px[cols // K :, cols:] = jnp.zeros((8 - cols // K, EXTRA), f32)
    weights = [stacked(first, last, c) for c in range(count)]
    for c in range(count):
        big[c].wait()
        px[2 * c : 2 * c + 2, :cols] = two_rows(weights[c], vx[c * K : (c + 1) * K, :], NN)
    outs = [pltpu.make_async_copy(px, px_hbm.at[d], out_sems.at[d]) for d in range(px_hbm.shape[0])]
    for copy in outs:
        copy.start()
    for copy in outs:
        copy.wait()


def ends_x(adj, depth, block_x, size_x):
    rows, cols = depth.shape
    count = block_x.shape[0] // size_x
    shape = (2 * count, cols + EXTRA)
    return pl.pallas_call(
        ends_x_kernel,
        out_shape=pltpu.HBM((size_x, *shape), f32),
        in_specs=[hbm_spec()] * 3,
        out_specs=hbm_spec(),
        scratch_shapes=[
            pltpu.VMEM((rows, cols), f32),
            pltpu.VMEM((count, 8, K), f32),
            pltpu.VMEM((count, 8, K), f32),
            pltpu.VMEM((8, cols), f32),
            pltpu.VMEM(shape, f32),
            pltpu.SemaphoreType.DMA((3,)),
            pltpu.SemaphoreType.DMA((count,)),
            pltpu.SemaphoreType.DMA((size_x,)),
        ],
        compiler_params=pltpu.CompilerParams(vmem_limit_bytes=16 << 20),
        cost_estimate=cost(2 * rows * cols * 16, 2 << 20),
        name="ends_x",
    )(*in_hbm(adj, depth, block_x))


def ends_y_kernel(adj, depth, block_y, py, vy, first, last, dcol, sems, row_sems):
    rows, cols = vy.shape
    count = first.shape[0]
    small = block_ends(block_y, lax.axis_index("gy"), first, last, sems)
    side = pltpu.make_async_copy(depth.at[:, pl.ds(cols - K, K)], dcol, sems.at[2])
    big = []
    for r in range(rows // K):
        here = pl.ds(r * K, K)
        big.append(pltpu.make_async_copy(adj.at[2, here, :], vy.at[here, :], row_sems.at[r]))
    for copy in small + big + [side]:
        copy.start()
    for copy in small:
        copy.wait()
    weights = [stacked(first, last, c) for c in range(count)]
    for r in range(rows // K):
        big[r].wait()
        for c in range(count):
            field = vy[r * K : (r + 1) * K, c * K : (c + 1) * K]
            py[2 * c : 2 * c + 2, r * K : (r + 1) * K] = two_rows(weights[c], field, NT)
    side.wait()
    at_last = (iota((8, K), 1) == K - 1).astype(f32).astype(bf16)
    high, low = halves(dcol[...])
    line = mm(at_last, high, NT) + mm(at_last, low, NT)
    for part in range(rows // K):
        py[part : part + 1, rows:] = line[0:1, part * K : (part + 1) * K]
    py[rows // K :, rows:] = jnp.zeros((8 - rows // K, EXTRA), f32)


def ends_y(adj, depth, block_y, size_y):
    rows, cols = depth.shape
    count = block_y.shape[0] // size_y
    return pl.pallas_call(
        ends_y_kernel,
        out_shape=jax.ShapeDtypeStruct((2 * count, rows + EXTRA), f32),
        in_specs=[hbm_spec()] * 3,
        out_specs=vmem_spec(),
        scratch_shapes=[
            pltpu.VMEM((rows, cols), f32),
            pltpu.VMEM((count, 8, K), f32),
            pltpu.VMEM((count, 8, K), f32),
            pltpu.VMEM((rows, K), f32),
            pltpu.SemaphoreType.DMA((3,)),
            pltpu.SemaphoreType.DMA((rows // K,)),
        ],
        compiler_params=pltpu.CompilerParams(vmem_limit_bytes=16 << 20),
        cost_estimate=cost(2 * rows * cols * 16, 2 << 20),
        name="ends_y",
    )(*in_hbm(adj, depth, block_y))


def carry_kernel(
    block_x, block_y, reduced_x_hbm, reduced_y_hbm,
    gx_hbm, gy_hbm, gside_hbm,
    gx, gy, gside, wx, wy, wpx, wpy, reduced_x, reduced_y, sems, out_sems,
):
    u = lax.axis_index("gx")
    v = lax.axis_index("gy")
    nbx = wx.shape[0]
    nby = wy.shape[0]
    before_x = jnp.maximum(u * nbx - 1, 0)
    before_y = jnp.maximum(v * nby - 1, 0)
    copies = [
        pltpu.make_async_copy(reduced_x_hbm, reduced_x, sems.at[4]),
        pltpu.make_async_copy(reduced_y_hbm, reduced_y, sems.at[5]),
        pltpu.make_async_copy(block_y.at[pl.ds(v * nby, nby)], wy, sems.at[1]),
        pltpu.make_async_copy(block_x.at[before_x, pl.ds(K - 8, 8), :], wpx, sems.at[2]),
        pltpu.make_async_copy(block_y.at[before_y, pl.ds(K - 8, 8), :], wpy, sems.at[3]),
        pltpu.make_async_copy(block_x.at[pl.ds(u * nbx, nbx)], wx, sems.at[0]),
    ]
    for copy in copies:
        copy.start()
    for copy in copies[:3]:
        copy.wait()
    own_x = reduced_x[pl.ds(pl.multiple_of(u * 8, 8), 8), :]
    own_y = reduced_y[pl.ds(pl.multiple_of(v * 8, 8), 8), :]
    prev_x = reduced_x[pl.ds(pl.multiple_of(jnp.maximum(u - 1, 0) * 8, 8), 8), :]
    prev_y = reduced_y[pl.ds(pl.multiple_of(jnp.maximum(v - 1, 0) * 8, 8), 8), :]
    row = iota((8, K), 0)
    lane = iota((8, K), 1)
    own = halves(own_y)
    for c in range(nby):
        pick = ((row == 2 * c) & (lane == 0)) | ((row == 2 * c + 1) & (lane == K - 1))
        pick = pick.astype(f32).astype(bf16)
        high, low = halves(wy[c])
        across = mm(pick, high, NT) + mm(pick, low, NT)
        gy[:, c * K : (c + 1) * K] = mm3(own, halves(across), TN)
    for copy in copies[3:]:
        copy.wait()
    for c in range(nbx):
        w = wx[c]
        gx[c * K : (c + 1) * K, :] = (
            w[:, 0:1] * own_x[2 * c : 2 * c + 1, :] + w[:, K - 1 : K] * own_x[2 * c + 1 : 2 * c + 2, :]
        )

    def side(w, prev, index):
        width = prev.shape[1]
        g = w[7:8, 0:1] * prev[6:7, :] + w[7:8, K - 1 : K] * prev[7:8, :]
        g = g + (iota((1, width), 1) == index * 8 - 1).astype(f32)
        return jnp.where(index > 0, g, 0.0)

    gside[...] = jnp.zeros(gside.shape, f32)
    gside[0:1, :] = side(wpx[...], prev_x, u)
    gside[1:2, : reduced_y.shape[1]] = side(wpy[...], prev_y, v)
    outs = [
        pltpu.make_async_copy(gx, gx_hbm, out_sems.at[0]),
        pltpu.make_async_copy(gy, gy_hbm, out_sems.at[1]),
        pltpu.make_async_copy(gside, gside_hbm, out_sems.at[2]),
    ]
    for copy in outs:
        copy.start()
    for copy in outs:
        copy.wait()


def carry(block_x, block_y, reduced_x, reduced_y, size_x, size_y):
    nbx = block_x.shape[0] // size_x
    nby = block_y.shape[0] // size_y
    results = [
        ((nbx * K, reduced_x.shape[0]), f32),
        ((reduced_y.shape[0], nby * K), f32),
        ((8, reduced_x.shape[0]), f32),
    ]
    return pl.pallas_call(
        carry_kernel,
        out_shape=tuple(pltpu.HBM(*result) for result in results),
        in_specs=[hbm_spec()] * 4,
        out_specs=(hbm_spec(),) * 3,
        scratch_shapes=[pltpu.VMEM(*result) for result in results]
        + [
            pltpu.VMEM((nbx, K, K), f32),
            pltpu.VMEM((nby, K, K), f32),
            pltpu.VMEM((8, K), f32),
            pltpu.VMEM((8, K), f32),
            pltpu.VMEM(reduced_x.shape, f32),
            pltpu.VMEM(reduced_y.shape, f32),
            pltpu.SemaphoreType.DMA((6,)),
            pltpu.SemaphoreType.DMA((3,)),
        ],
        compiler_params=pltpu.CompilerParams(vmem_limit_bytes=16 << 20),
        cost_estimate=cost(1 << 36, 2 << 20),
        name="carry",
    )(*in_hbm(block_x, block_y, reduced_x, reduced_y))


def elev_kernel(
    tx, ta_in, tb_in, gside_in, gx_in, gy_in, block_x, block_y, adj, depth, basis_in,
    wet_in, coef_in, footprint_in, owner_in,
    elev_out, fx_out, fy_out, parts_out,
    ty, gside, gx, gy, wx, wy, planes, dep, basis, wet, coef, footprint, owner,
    elev, fx, fy, tyn, mom, parts, sems, row_sems, out_sems,
):
    u = lax.axis_index("gx")
    v = lax.axis_index("gy")
    rows, cols = dep.shape
    steps = rows // K
    half = ta_in.shape[0]
    nbx = wx.shape[0]
    nby = wy.shape[0]
    first = [
        pltpu.make_async_copy(ta_in, ty.at[pl.ds(0, half)], sems.at[0]),
        pltpu.make_async_copy(tb_in, ty.at[pl.ds(half, half)], sems.at[1]),
        pltpu.make_async_copy(gside_in, gside, sems.at[2]),
        pltpu.make_async_copy(gy_in, gy, sems.at[3]),
        pltpu.make_async_copy(block_y.at[pl.ds(v * nby, nby)], wy, sems.at[4]),
        pltpu.make_async_copy(gx_in, gx, sems.at[5]),
        pltpu.make_async_copy(block_x.at[pl.ds(u * nbx, nbx)], wx, sems.at[6]),
        pltpu.make_async_copy(basis_in, basis, sems.at[7]),
    ]
    last = [
        pltpu.make_async_copy(wet_in, wet, sems.at[8]),
        pltpu.make_async_copy(coef_in, coef, sems.at[9]),
        pltpu.make_async_copy(footprint_in, footprint, sems.at[10]),
        pltpu.make_async_copy(owner_in, owner, sems.at[11]),
    ]
    fields = []
    for r in range(steps):
        here = pl.ds(r * K, K)
        fields.append(
            [
                pltpu.make_async_copy(adj.at[:, here, :], planes.at[:, here, :], row_sems.at[r, 0]),
                pltpu.make_async_copy(depth.at[here, :], dep.at[here, :], row_sems.at[r, 1]),
            ]
        )
    for group in [first, *fields, last]:
        for copy in group:
            copy.start()
    for copy in first:
        copy.wait()
    tx_all = jnp.concatenate([tx[d][:, :cols] for d in range(tx.shape[0])], axis=0)
    for j in range(2 * half):
        tyn[j * 8 : (j + 1) * 8, :] = ty[j ^ v]
    ty_all = tyn[:, :rows]
    txs = halves(tx_all)
    tys = halves(ty_all)
    tyt = halves(ty_all.T)
    up = jnp.maximum(u - 1, 0)
    left = jnp.maximum(v - 1, 0)
    gs = gside[...]
    edge_x = mm3(halves(gs), txs, NN)[0:1, :]
    edge_y = mm3(halves(gs[:, : ty_all.shape[0]]), tys, NN)[1:2, :]
    drow = tx[up][:, cols:]
    drow = jnp.concatenate([drow[p : p + 1, :] for p in range(cols // K)], axis=1)
    dcol = tyn[pl.ds(pl.multiple_of(left * 8, 8), 8), rows:]
    dcol = jnp.concatenate([dcol[p : p + 1, :] for p in range(rows // K)], axis=1)
    carry = edge_x * drow
    side = halves(jnp.broadcast_to(edge_y * dcol, (8, rows)))
    row = iota((K, cols), 0)
    lane = iota((K, K), 1)
    corner = ((iota((8, K), 1) == 0) & (iota((8, K), 0) == 0)).astype(f32).astype(bf16)
    modes, tile_h, tile_w = basis.shape
    per = K // tile_h
    outs = []
    firsts = []
    to_y = []
    for c in range(nby):
        wh, wl = halves(wy[c].T)
        gh, gl = halves(gy[:, c * K : (c + 1) * K])
        to_y.append((jnp.concatenate([wh, gh], axis=0), jnp.concatenate([wl, gl], axis=0)))
    for r in range(steps):
        here = slice(r * K, (r + 1) * K)
        if r % 2 == 0:
            for copy in fields[r] + fields[r + 1]:
                copy.wait()
        d = dep[here, :]
        wh, wl = halves(wx[r])
        gh, gl = halves(gx[here, :])
        vh, vl = halves(planes[1, here, :])
        flux_x = mm3(
            (jnp.concatenate([wh, gh], axis=1), jnp.concatenate([wl, gl], axis=1)),
            (jnp.concatenate([vh, txs[0]], axis=0), jnp.concatenate([vl, txs[1]], axis=0)),
            NN,
        )
        pieces = []
        for c in range(nby):
            vh, vl = halves(planes[2, here, c * K : (c + 1) * K])
            lhs = (
                jnp.concatenate([vh, tyt[0][here, :]], axis=1),
                jnp.concatenate([vl, tyt[1][here, :]], axis=1),
            )
            pieces.append(mm3(lhs, to_y[c], NN))
        flux_y = jnp.concatenate(pieces, axis=1)
        fx[here, :] = flux_x
        fy[here, :] = flux_y
        weighted_x = d * flux_x
        weighted_y = d * flux_y
        before_x = jnp.where(row == 0, carry, pltpu.roll(weighted_x, 1, 0))
        carry = weighted_x[K - 1 : K, :]
        edge = mm(side[0][:, here], corner, TN) + mm(side[1][:, here], corner, TN)
        turned = [edge] + [
            pltpu.roll(weighted_y[:, c * K : (c + 1) * K], 1, 1) for c in range(cols // K)
        ]
        before_y = jnp.concatenate(
            [jnp.where(lane == 0, turned[c], turned[c + 1]) for c in range(cols // K)], axis=1
        )
        e = planes[0, here, :] + courant * ((weighted_x - before_x) + (weighted_y - before_y))
        elev[here, :] = e
        where = pl.ds(r * K, K)
        for i, (source, target) in enumerate(((elev, elev_out), (fx, fx_out), (fy, fy_out))):
            copy = pltpu.make_async_copy(source.at[where, :], target.at[where, :], out_sems.at[r, i])
            copy.start()
            outs.append(copy)
        if r == 0:
            top = e[0:1, :]
        eh, el = halves(e[:, :K])
        firsts.append((mm(corner, eh, NT) + mm(corner, el, NT))[0:1, :])
        for a in range(per):
            for w in range(cols // tile_w):
                tile = e[a * tile_h : (a + 1) * tile_h, w * tile_w : (w + 1) * tile_w]
                for b in range(modes):
                    at = b * (rows // tile_h) + r * per + a
                    mom[at : at + 1, w * tile_w : (w + 1) * tile_w] = jnp.sum(
                        tile * basis[b], axis=0, keepdims=True
                    )
    for copy in last:
        copy.wait()
    tiles_y, tiles_x = wet.shape
    count = footprint.shape[1]
    places = footprint.shape[0]
    ones = jnp.ones((8, tile_w), bf16)
    pieces = []
    for w in range(tiles_y):
        high, low = halves(mom[:, w * tile_w : (w + 1) * tile_w])
        line = (mm(ones, high, NT) + mm(ones, low, NT))[0:1, :]
        keep = wet[w : w + 1, :].astype(f32)
        for b in range(modes):
            pieces.append(line[:, b * tiles_x : (b + 1) * tiles_x] * keep)
    high, low = halves(jnp.concatenate(pieces, axis=0))
    table = jnp.concatenate([high, low], axis=0)
    number = footprint[...]
    total_cols = tiles_y * lax.axis_size("gy")
    local_row = lax.shift_right_logical(number, total_cols.bit_length() - 1) - u * tiles_x
    local_col = (number & (total_cols - 1)) - v * tiles_y
    lines = tiles_y * modes
    tile_row = iota((tiles_x, count), 0)
    tile_col = lax.shift_right_logical(iota((lines, count), 0), modes.bit_length() - 1)
    acc = jnp.zeros((lines, count), f32)
    for f in range(places):
        at_row = (tile_row == local_row[f : f + 1, :]).astype(f32).astype(bf16)
        both = mm(table, at_row, NN)
        four = coef[f]
        scale = jnp.concatenate([four] * tiles_y, axis=0)
        hit = tile_col == local_col[f : f + 1, :]
        acc = acc + jnp.where(hit, (both[:lines] + both[lines:]) * scale, 0.0)
    total = jnp.sum(acc, axis=0, keepdims=True)
    devices = parts.shape[0] // 5
    slots = count // devices
    own = owner[...]
    slot_of = (iota((slots, count), 0) == (own & (slots - 1))).astype(f32)
    device_of = iota((devices, count), 0) == lax.shift_right_logical(own, slots.bit_length() - 1)
    device_of = device_of.astype(f32).astype(bf16)
    high, low = halves(slot_of * total)
    sums = mm(device_of, high, NT) + mm(device_of, low, NT)
    parts[...] = jnp.zeros(parts.shape, f32)
    parts[pl.ds(0, devices, stride=5), :] = jnp.concatenate(
        [sums, jnp.zeros((devices, K - slots), f32)], axis=1
    )
    size_y = lax.axis_size("gy")

    def put(device, line):
        for p in range(4):
            parts[pl.ds(device * 5 + 1 + p, 1), :] = line[:, p * K : (p + 1) * K]

    @pl.when(u > 0)
    def _():
        put((u - 1) * size_y + v, top)

    @pl.when(v > 0)
    def _():
        put(u * size_y + v - 1, jnp.concatenate(firsts, axis=1))

    outs.append(pltpu.make_async_copy(parts, parts_out, sems.at[12]))
    outs[-1].start()
    for copy in outs:
        copy.wait()


def elevation(tx, ta, tb, gx, gy, gside, block_x, block_y, adj, depth, basis, wet, coef, footprint, owner):
    rows, cols = depth.shape
    modes, tile_h, tile_w = basis.shape
    devices = lax.axis_size("gx") * lax.axis_size("gy")
    steps = rows // K
    wet = wet.T
    coef = coef.transpose(1, 2, 0)
    footprint = footprint.T
    owner = owner.reshape(1, -1)
    field = ((rows, cols), f32)
    far = (2 * ta.shape[0], 8, rows + EXTRA)
    parts = ((devices * 5, K), f32)
    like = lambda *arrays: [pltpu.VMEM(a.shape, a.dtype) for a in arrays]
    return pl.pallas_call(
        elev_kernel,
        out_shape=(pltpu.HBM(*field),) * 3 + (pltpu.HBM(*parts),),
        in_specs=[vmem_spec()] + [pl.BlockSpec(memory_space=pl.ANY)] * 2 + [hbm_spec()] * 12,
        out_specs=(hbm_spec(),) * 4,
        scratch_shapes=[pltpu.VMEM(far, f32)]
        + like(gside, gx, gy)
        + [pltpu.VMEM((rows // K, K, K), f32), pltpu.VMEM((cols // K, K, K), f32)]
        + [pltpu.VMEM((3, rows, cols), f32), pltpu.VMEM(*field)]
        + like(basis, wet, coef, footprint, owner)
        + [pltpu.VMEM(*field)] * 3
        + [
            pltpu.VMEM((far[0] * 8, far[2]), f32),
            pltpu.VMEM((rows // tile_h * modes, cols), f32),
            pltpu.VMEM(*parts),
            pltpu.SemaphoreType.DMA((13,)),
            pltpu.SemaphoreType.DMA((steps, 2)),
            pltpu.SemaphoreType.DMA((steps, 3)),
        ],
        compiler_params=pltpu.CompilerParams(vmem_limit_bytes=32 << 20),
        cost_estimate=cost(12 * rows * cols * K, 10 << 20),
        name="elevation",
    )(
        tx,
        ta,
        tb,
        *in_hbm(gside, gx, gy, block_x, block_y, adj, depth, basis, wet, coef, footprint, owner),
    )


def fluxes_kernel(elev_in, fx_in, fy_in, out, e, x, y, sems, out_sems):
    rows, cols = e.shape
    steps = rows // K
    reads = []
    for r in range(steps):
        here = pl.ds(r * K, K)
        pairs = ((elev_in, e), (fx_in, x), (fy_in, y))
        reads.append(
            [
                pltpu.make_async_copy(source.at[here, :], target.at[here, :], sems.at[r, i])
                for i, (source, target) in enumerate(pairs)
            ]
        )
    for group in reads:
        for copy in group:
            copy.start()
    row = iota((K, cols), 0)
    lane = iota((K, cols), 1)
    writes = []
    for copy in reads[0]:
        copy.wait()
    for r in range(steps):
        here = slice(r * K, (r + 1) * K)
        after = 0.0
        if r + 1 < steps:
            for copy in reads[r + 1]:
                copy.wait()
            after = e[(r + 1) * K : (r + 1) * K + 1, :]
        now = e[here, :]
        below = jnp.where(row == K - 1, after, pltpu.roll(now, K - 1, 0))
        right = jnp.where(lane == cols - 1, 0.0, pltpu.roll(now, cols - 1, 1))
        x[here, :] = x[here, :] + courant * (below - now)
        y[here, :] = y[here, :] + courant * (right - now)
        where = pl.ds(r * K, K)
        for i, source in enumerate((e, x, y)):
            copy = pltpu.make_async_copy(source.at[where, :], out.at[i, where, :], out_sems.at[r, i])
            copy.start()
            writes.append(copy)
    for copy in writes:
        copy.wait()


def fluxes(elev, fx, fy):
    rows, cols = elev.shape
    return pl.pallas_call(
        fluxes_kernel,
        out_shape=pltpu.HBM((3, rows, cols), f32),
        in_specs=[hbm_spec()] * 3,
        out_specs=hbm_spec(),
        scratch_shapes=[
            pltpu.VMEM((rows, cols), f32),
            pltpu.VMEM((rows, cols), f32),
            pltpu.VMEM((rows, cols), f32),
            pltpu.SemaphoreType.DMA((rows // K, 3)),
            pltpu.SemaphoreType.DMA((rows // K, 3)),
        ],
        compiler_params=pltpu.CompilerParams(vmem_limit_bytes=16 << 20),
        cost_estimate=cost(10 * rows * cols, 6 << 20),
        name="fluxes",
    )(*in_hbm(elev, fx, fy))


def finish_kernel(fields_in, sums, fields, grad, bottom, edge, sems, out_sems):
    u = lax.axis_index("gx")
    v = lax.axis_index("gy")
    size_x = lax.axis_size("gx")
    size_y = lax.axis_size("gy")
    rows, cols = fields.shape[1:]
    reads = [
        pltpu.make_async_copy(fields.at[1, pl.ds(rows - 8, 8), :], bottom, sems.at[0]),
        pltpu.make_async_copy(fields.at[2, :, pl.ds(cols - K, K)], edge, sems.at[1]),
    ]
    for copy in reads:
        copy.start()

    def line(device):
        return jnp.concatenate([sums[pl.ds(device * 5 + 1 + p, 1), :] for p in range(4)], axis=1)

    below = line(jnp.minimum(u + 1, size_x - 1) * size_y + v) * jnp.where(u + 1 < size_x, courant, 0.0)
    right = line(u * size_y + jnp.minimum(v + 1, size_y - 1)) * jnp.where(v + 1 < size_y, courant, 0.0)
    devices = sums.shape[0] // 5
    total = jnp.sum(sums[pl.ds(0, devices, stride=5), :], axis=0, keepdims=True)
    grad[...] = total[:, : grad.shape[1]]
    corner = ((iota((8, K), 1) == K - 1) & (iota((8, K), 0) == 0)).astype(f32).astype(bf16)
    high, low = halves(jnp.broadcast_to(right, (8, rows)))
    for copy in reads:
        copy.wait()
    bottom[7:8, :] = bottom[7:8, :] + below
    edge[...] = edge[...] + (mm(high, corner, TN) + mm(low, corner, TN))
    writes = [
        pltpu.make_async_copy(bottom, fields.at[1, pl.ds(rows - 8, 8), :], out_sems.at[0]),
        pltpu.make_async_copy(edge, fields.at[2, :, pl.ds(cols - K, K)], out_sems.at[1]),
    ]
    for copy in writes:
        copy.start()
    for copy in writes:
        copy.wait()


def finish(fields, sums, slots):
    _, rows, cols = fields.shape
    return pl.pallas_call(
        finish_kernel,
        out_shape=(pltpu.HBM(fields.shape, f32), jax.ShapeDtypeStruct((1, slots), f32)),
        in_specs=[hbm_spec(), vmem_spec()],
        out_specs=(hbm_spec(), vmem_spec()),
        input_output_aliases={0: 0},
        scratch_shapes=[
            pltpu.VMEM((8, cols), f32),
            pltpu.VMEM((rows, K), f32),
            pltpu.SemaphoreType.DMA((2,)),
            pltpu.SemaphoreType.DMA((2,)),
        ],
        compiler_params=pltpu.CompilerParams(vmem_limit_bytes=16 << 20),
        cost_estimate=cost(1 << 20, 1 << 20),
        name="finish",
    )(*in_hbm(fields), sums)


def partner(axis, bit):
    return [(i, i ^ bit) for i in range(lax.axis_size(axis))]


def body(
    adj_fields, depth, block_x, reduced_x, block_y, reduced_y, basis, coef, footprint, owner, wet
):
    size_x = lax.axis_size("gx")
    size_y = lax.axis_size("gy")
    ty = ends_y(adj_fields, depth, block_y, size_y)[None]
    px = ends_x(adj_fields, depth, block_x, size_x)
    ty = jnp.concatenate([ty, lax.ppermute(ty, "gy", partner("gy", 1))], axis=0)
    px, ty = lax.optimization_barrier((px, ty))
    bit = 2
    while 2 * bit < size_y:
        ty = jnp.concatenate([ty, lax.ppermute(ty, "gy", partner("gy", bit))], axis=0)
        bit *= 2
    ty_far = lax.ppermute(ty, "gy", partner("gy", bit))
    tx = lax.all_to_all(px, "gx", split_axis=0, concat_axis=0, tiled=True)
    carried = carry(block_x, block_y, reduced_x, reduced_y, size_x, size_y)
    elev, fx, fy, parts = elevation(
        tx, ty, ty_far, *carried, block_x, block_y, adj_fields, depth, basis, wet, coef, footprint, owner
    )
    devices = size_x * size_y
    sums = lax.all_to_all(
        parts[:, None, :], ("gx", "gy"), split_axis=0, concat_axis=0, tiled=True
    )
    slots = owner.shape[0] // devices
    adj_before, grad = finish(fluxes(elev, fx, fy), sums[:, 0, :], slots)
    return adj_before, grad.reshape(slots)


def solution(mesh):
    in_specs = (
        P(None, "gx", "gy"),
        P("gx", "gy"),
        P(),
        P(),
        P(),
        P(),
        P(),
        P(),
        P(),
        P(),
        P("gx", "gy"),
    )
    out_specs = (P(None, "gx", "gy"), P(("gx", "gy")))
    return jax.shard_map(body, mesh=mesh, in_specs=in_specs, out_specs=out_specs, check_vma=False)
```

```python
import jax
import jax.numpy as jnp
from jax import lax
from jax.experimental import pallas as pl
from jax.experimental.pallas import tpu as pltpu
from jax.sharding import PartitionSpec as P

courant = 0.5
f32 = jnp.float32
bf16 = jnp.bfloat16
K = 128
EXTRA = 128

NN = (((1,), (0,)), ((), ()))
NT = (((1,), (1,)), ((), ()))
TN = (((0,), (0,)), ((), ()))


def halves(x):
    high = x.astype(bf16)
    return high, (x - high.astype(f32)).astype(bf16)


def mm(a, b, dims):
    return lax.dot_general(a, b, dims, preferred_element_type=f32)


def mm3(a, b, dims):
    ah, al = a
    bh, bl = b
    return mm(ah, bh, dims) + (mm(ah, bl, dims) + mm(al, bh, dims))


def exact(a, b, dims):
    return lax.dot_general(a, b, dims, precision=lax.Precision.HIGHEST, preferred_element_type=f32)


def iota(shape, dim):
    return lax.broadcasted_iota(jnp.int32, shape, dim)


def hbm_spec():
    return pl.BlockSpec(memory_space=pltpu.HBM)


def vmem_spec():
    return pl.BlockSpec(memory_space=pltpu.VMEM)


def in_hbm(*arrays):
    return tuple(pltpu.with_memory_space_constraint(a, pltpu.HBM) for a in arrays)


def in_vmem(*arrays):
    return tuple(pltpu.with_memory_space_constraint(a, pltpu.VMEM) for a in arrays)


def cost(flops, nbytes):
    return pl.CostEstimate(flops=flops, bytes_accessed=nbytes, transcendentals=0)


def stacked(first, last, c):
    high, low = halves(jnp.concatenate([first[c, 0:1, :], last[c, 7:8, :]], axis=0))
    return jnp.concatenate([high, low], axis=0)


def two_rows(weights, field, dims):
    high, low = halves(field)
    both = mm(weights, high, dims)
    return both[0:2] + both[2:4] + mm(weights[0:2], low, dims)


def block_ends(blocks, index, first, last, sems):
    here = pl.ds(index * first.shape[0], first.shape[0])
    return [
        pltpu.make_async_copy(blocks.at[here, pl.ds(0, 8), :], first, sems.at[0]),
        pltpu.make_async_copy(blocks.at[here, pl.ds(K - 8, 8), :], last, sems.at[1]),
    ]


def ends_kernel(
    adj, depth, block_x, block_y, px_hbm, py,
    vx, vy, first_x, last_x, first_y, last_y, drow, dcol, px, sems, out_sems,
):
    rows, cols = vx.shape
    nbx = first_x.shape[0]
    nby = first_y.shape[0]
    small = block_ends(block_x, lax.axis_index("gx"), first_x, last_x, sems)
    small += block_ends(block_y, lax.axis_index("gy"), first_y, last_y, sems.at[pl.ds(2, 2)])
    small.append(pltpu.make_async_copy(depth.at[pl.ds(rows - 8, 8), :], drow, sems.at[4]))
    side = pltpu.make_async_copy(depth.at[:, pl.ds(cols - K, K)], dcol, sems.at[5])
    field_x = pltpu.make_async_copy(adj.at[1], vx, sems.at[6])
    field_y = pltpu.make_async_copy(adj.at[2], vy, sems.at[7])
    for copy in small + [field_x, side, field_y]:
        copy.start()
    for copy in small:
        copy.wait()
    for part in range(cols // K):
        px[part : part + 1, cols:] = drow[7:8, part * K : (part + 1) * K]
    px[cols // K :, cols:] = jnp.zeros((8 - cols // K, EXTRA), f32)
    weights_x = [stacked(first_x, last_x, c) for c in range(nbx)]
    weights_y = [stacked(first_y, last_y, c) for c in range(nby)]
    field_x.wait()
    for c in range(nbx):
        px[2 * c : 2 * c + 2, :cols] = two_rows(weights_x[c], vx[c * K : (c + 1) * K, :], NN)
    outs = [pltpu.make_async_copy(px, px_hbm.at[d], out_sems.at[d]) for d in range(px_hbm.shape[0])]
    for copy in outs:
        copy.start()
    side.wait()
    field_y.wait()
    at_last = (iota((8, K), 1) == K - 1).astype(f32).astype(bf16)
    high, low = halves(dcol[...])
    line = mm(at_last, high, NT) + mm(at_last, low, NT)
    for part in range(rows // K):
        py[part : part + 1, rows:] = line[0:1, part * K : (part + 1) * K]
    py[rows // K :, rows:] = jnp.zeros((8 - rows // K, EXTRA), f32)
    for r in range(rows // K):
        for c in range(nby):
            field = vy[r * K : (r + 1) * K, c * K : (c + 1) * K]
            py[2 * c : 2 * c + 2, r * K : (r + 1) * K] = two_rows(weights_y[c], field, NT)
    for copy in outs:
        copy.wait()


def ends(adj, depth, block_x, block_y, size_x, size_y):
    rows, cols = depth.shape
    nbx = block_x.shape[0] // size_x
    nby = block_y.shape[0] // size_y
    shape = (2 * nbx, cols + EXTRA)
    return pl.pallas_call(
        ends_kernel,
        out_shape=(
            pltpu.HBM((size_x, *shape), f32),
            jax.ShapeDtypeStruct((2 * nby, rows + EXTRA), f32),
        ),
        in_specs=[hbm_spec()] * 4,
        out_specs=(hbm_spec(), vmem_spec()),
        scratch_shapes=[
            pltpu.VMEM((rows, cols), f32),
            pltpu.VMEM((rows, cols), f32),
            pltpu.VMEM((nbx, 8, K), f32),
            pltpu.VMEM((nbx, 8, K), f32),
            pltpu.VMEM((nby, 8, K), f32),
            pltpu.VMEM((nby, 8, K), f32),
            pltpu.VMEM((8, cols), f32),
            pltpu.VMEM((rows, K), f32),
            pltpu.VMEM(shape, f32),
            pltpu.SemaphoreType.DMA((8,)),
            pltpu.SemaphoreType.DMA((size_x,)),
        ],
        compiler_params=pltpu.CompilerParams(vmem_limit_bytes=16 << 20),
        cost_estimate=cost(2 * rows * cols * 32, 3 << 20),
        name="ends",
    )(*in_hbm(adj, depth, block_x, block_y))


def carry_kernel(
    block_x, block_y, reduced_x_hbm, reduced_y_hbm, mx_hbm, my_hbm,
    mx, my, wx, wy, reduced_x, reduced_y, sems, out_sems,
):
    u = lax.axis_index("gx")
    v = lax.axis_index("gy")
    nbx = wx.shape[0]
    nby = wy.shape[0]
    copies = [
        pltpu.make_async_copy(reduced_x_hbm, reduced_x, sems.at[0]),
        pltpu.make_async_copy(block_x.at[pl.ds(u * nbx, nbx)], wx, sems.at[1]),
        pltpu.make_async_copy(reduced_y_hbm, reduced_y, sems.at[2]),
        pltpu.make_async_copy(block_y.at[pl.ds(v * nby, nby)], wy, sems.at[3]),
    ]
    for copy in copies:
        copy.start()
    outs = [
        pltpu.make_async_copy(mx, mx_hbm, out_sems.at[0]),
        pltpu.make_async_copy(my, my_hbm, out_sems.at[1]),
    ]
    for copy in copies[:2]:
        copy.wait()
    own_x = reduced_x[pl.ds(pl.multiple_of(u * 8, 8), 8), :]
    for c in range(nbx):
        w = wx[c]
        g = w[:, 0:1] * own_x[2 * c : 2 * c + 1, :] + w[:, K - 1 : K] * own_x[2 * c + 1 : 2 * c + 2, :]
        for i, part in enumerate(zip(halves(w), halves(g))):
            mx[i, c * K : (c + 1) * K, :] = jnp.concatenate(part, axis=1)
    outs[0].start()
    for copy in copies[2:]:
        copy.wait()
    own_y = halves(reduced_y[pl.ds(pl.multiple_of(v * 8, 8), 8), :])
    sub = iota((8, K), 0)
    for c in range(nby):
        turned = wy[c].T
        across = jnp.where(sub == 2 * c, turned[0:1, :], 0.0)
        across = jnp.where(sub == 2 * c + 1, turned[K - 1 : K, :], across)
        g = mm3(own_y, halves(across), TN)
        for i, part in enumerate(zip(halves(turned), halves(g))):
            my[i, :, c * K : (c + 1) * K] = jnp.concatenate(part, axis=0)
    outs[1].start()
    for copy in outs:
        copy.wait()


def carry(block_x, block_y, reduced_x, reduced_y):
    nbx = block_x.shape[0] // lax.axis_size("gx")
    nby = block_y.shape[0] // lax.axis_size("gy")
    results = [
        ((2, nbx * K, K + reduced_x.shape[0]), bf16),
        ((2, K + reduced_y.shape[0], nby * K), bf16),
    ]
    return pl.pallas_call(
        carry_kernel,
        out_shape=tuple(pltpu.HBM(*result) for result in results),
        in_specs=[hbm_spec()] * 4,
        out_specs=(hbm_spec(),) * 2,
        scratch_shapes=[pltpu.VMEM(*result) for result in results]
        + [
            pltpu.VMEM((nbx, K, K), f32),
            pltpu.VMEM((nby, K, K), f32),
            pltpu.VMEM(reduced_x.shape, f32),
            pltpu.VMEM(reduced_y.shape, f32),
            pltpu.SemaphoreType.DMA((4,)),
            pltpu.SemaphoreType.DMA((2,)),
        ],
        compiler_params=pltpu.CompilerParams(vmem_limit_bytes=16 << 20),
        cost_estimate=cost(1 << 24, 2 << 20),
        name="carry",
    )(*in_hbm(block_x, block_y, reduced_x, reduced_y))


def shares_kernel(
    block_x, block_y, reduced_x_hbm, reduced_y_hbm, coef_hbm, footprint_hbm,
    gside_hbm, share_hbm, at_row_hbm,
    gside, share, at_row, wpx, wpy, reduced_x, reduced_y, coef, footprint, sems, out_sems,
):
    u = lax.axis_index("gx")
    v = lax.axis_index("gy")
    nbx = block_x.shape[0] // lax.axis_size("gx")
    nby = block_y.shape[0] // lax.axis_size("gy")
    before_x = jnp.maximum(u * nbx - 1, 0)
    before_y = jnp.maximum(v * nby - 1, 0)
    copies = [
        pltpu.make_async_copy(footprint_hbm, footprint, sems.at[0]),
        pltpu.make_async_copy(coef_hbm, coef, sems.at[1]),
        pltpu.make_async_copy(reduced_x_hbm, reduced_x, sems.at[2]),
        pltpu.make_async_copy(reduced_y_hbm, reduced_y, sems.at[3]),
        pltpu.make_async_copy(block_x.at[before_x, pl.ds(K - 8, 8), :], wpx, sems.at[4]),
        pltpu.make_async_copy(block_y.at[before_y, pl.ds(K - 8, 8), :], wpy, sems.at[5]),
    ]
    for copy in copies:
        copy.start()
    outs = [
        pltpu.make_async_copy(share, share_hbm, out_sems.at[0]),
        pltpu.make_async_copy(at_row, at_row_hbm, out_sems.at[1]),
        pltpu.make_async_copy(gside, gside_hbm, out_sems.at[2]),
    ]
    for copy in copies[:2]:
        copy.wait()
    places, modes, count = coef.shape
    tiles_y = share.shape[1] // modes
    tiles_x = at_row.shape[1]
    total_cols = tiles_y * lax.axis_size("gy")
    number = footprint[...]
    row = lax.shift_right_logical(number, total_cols.bit_length() - 1)
    col = (number & (total_cols - 1)) - v * tiles_y
    top = jnp.min(row, axis=0, keepdims=True)
    tile_row = iota((tiles_x, count), 0)
    tile_col = lax.shift_right_logical(iota((tiles_y * modes, count), 0), modes.bit_length() - 1)
    for step in range(2):
        at_row[step] = (tile_row == top + step - u * tiles_x).astype(f32).astype(bf16)
        index = jnp.where(row == top + step, col, -1)
        acc = jnp.zeros((tiles_y * modes, count), f32)
        for f in range(places):
            scale = jnp.concatenate([coef[f]] * tiles_y, axis=0)
            acc = acc + jnp.where(tile_col == index[f : f + 1, :], scale, 0.0)
        share[step] = acc
    for copy in outs[:2]:
        copy.start()
    for copy in copies[2:]:
        copy.wait()

    def side(w, reduced, index):
        prev = reduced[pl.ds(pl.multiple_of(jnp.maximum(index - 1, 0) * 8, 8), 8), :]
        width = prev.shape[1]
        g = w[7:8, 0:1] * prev[6:7, :] + w[7:8, K - 1 : K] * prev[7:8, :]
        g = g + (iota((1, width), 1) == index * 8 - 1).astype(f32)
        return jnp.where(index > 0, g, 0.0)

    gside[...] = jnp.zeros(gside.shape, f32)
    gside[0:1, :] = side(wpx[...], reduced_x, u)
    gside[1:2, : reduced_y.shape[1]] = side(wpy[...], reduced_y, v)
    outs[2].start()
    for copy in outs:
        copy.wait()


def shares(block_x, block_y, reduced_x, reduced_y, coef, footprint, wet):
    coef = coef.transpose(1, 2, 0)
    footprint = footprint.T
    _, modes, count = coef.shape
    tiles_x, tiles_y = wet.shape
    results = [
        ((8, reduced_x.shape[0]), f32),
        ((2, tiles_y * modes, count), f32),
        ((2, tiles_x, count), bf16),
    ]
    return pl.pallas_call(
        shares_kernel,
        out_shape=tuple(pltpu.HBM(*result) for result in results),
        in_specs=[hbm_spec()] * 6,
        out_specs=(hbm_spec(),) * 3,
        scratch_shapes=[pltpu.VMEM(*result) for result in results]
        + [
            pltpu.VMEM((8, K), f32),
            pltpu.VMEM((8, K), f32),
            pltpu.VMEM(reduced_x.shape, f32),
            pltpu.VMEM(reduced_y.shape, f32),
            pltpu.VMEM(coef.shape, f32),
            pltpu.VMEM(footprint.shape, jnp.int32),
            pltpu.SemaphoreType.DMA((6,)),
            pltpu.SemaphoreType.DMA((3,)),
        ],
        compiler_params=pltpu.CompilerParams(vmem_limit_bytes=16 << 20),
        cost_estimate=cost(1 << 24, 2 << 20),
        name="shares",
    )(*in_hbm(block_x, block_y, reduced_x, reduced_y, coef, footprint))


def elev_kernel(
    tx, ta_in, tb_in, mx_in, my_in, gside_in, share_in, at_row_in, adj, depth, basis_in, wet_in, owner_in,
    fields_out, parts_out,
    ty, mx, my, gside, share, at_row, planes, dep, basis, wet, owner,
    elev, fx, fy, tyn, mom, parts, sems, row_sems, out_sems,
):
    u = lax.axis_index("gx")
    v = lax.axis_index("gy")
    rows, cols = dep.shape
    steps = rows // K
    half = ta_in.shape[0]
    first = [
        pltpu.make_async_copy(ta_in, ty.at[pl.ds(0, half)], sems.at[0]),
        pltpu.make_async_copy(tb_in, ty.at[pl.ds(half, half)], sems.at[1]),
        pltpu.make_async_copy(gside_in, gside, sems.at[2]),
        pltpu.make_async_copy(owner_in, owner, sems.at[3]),
    ]
    second = [
        pltpu.make_async_copy(mx_in, mx, sems.at[4]),
        pltpu.make_async_copy(my_in, my, sems.at[5]),
    ]
    last = [
        pltpu.make_async_copy(basis_in, basis, sems.at[6]),
        pltpu.make_async_copy(wet_in, wet, sems.at[7]),
        pltpu.make_async_copy(share_in, share, sems.at[8]),
        pltpu.make_async_copy(at_row_in, at_row, sems.at[9]),
    ]
    fields = []
    for r in range(steps):
        here = pl.ds(r * K, K)
        fields.append(
            [
                pltpu.make_async_copy(adj.at[:, here, :], planes.at[:, here, :], row_sems.at[r, 0]),
                pltpu.make_async_copy(depth.at[here, :], dep.at[here, :], row_sems.at[r, 1]),
            ]
        )
    for group in [fields[0], first, second, fields[1], last[:1], fields[2], fields[3], last[1:]]:
        for copy in group:
            copy.start()
    txs = halves(jnp.concatenate([tx[d][:, :cols] for d in range(tx.shape[0])], axis=0))
    parts[...] = jnp.zeros(parts.shape, f32)
    for copy in first:
        copy.wait()
    devices = parts.shape[0] // 5
    count = owner.shape[1]
    slots = count // devices
    own = owner[...]
    device_of = iota((devices, count), 0) == lax.shift_right_logical(own, slots.bit_length() - 1)
    device_of = device_of.astype(f32).astype(bf16)
    slot_of = iota((slots, count), 0) == (own & (slots - 1))
    for j in range(2 * half):
        far = j ^ v
        place = 0
        for i, bit in enumerate(rounds(2 * half)):
            place = place | (((far // bit) & 1) << i)
        tyn[j * 8 : (j + 1) * 8, :] = ty[place]
    ty_all = tyn[:, :rows]
    tys = halves(ty_all)
    tyt = halves(ty_all.T)
    up = jnp.maximum(u - 1, 0)
    left = jnp.maximum(v - 1, 0)
    gs = gside[...]
    edge_x = mm3(halves(gs), txs, NN)[0:1, :]
    edge_y = mm3(halves(gs[:, : ty_all.shape[0]]), tys, NN)[1:2, :]
    drow = tx[up][:, cols:]
    drow = jnp.concatenate([drow[p : p + 1, :] for p in range(cols // K)], axis=1)
    dcol = tyn[pl.ds(pl.multiple_of(left * 8, 8), 8), rows:]
    dcol = jnp.concatenate([dcol[p : p + 1, :] for p in range(rows // K)], axis=1)
    carry = edge_x * drow
    side = jnp.broadcast_to(edge_y * dcol, (8, rows)).T
    row = iota((K, cols), 0)
    lane = iota((K, K), 1)
    modes, tile_h, tile_w = basis.shape
    per = K // tile_h
    outs = []
    firsts = []

    def send(plane, source, r):
        here = pl.ds(r * K, K)
        copy = pltpu.make_async_copy(
            source.at[here, :], fields_out.at[plane, here, :], out_sems.at[r, plane]
        )
        copy.start()
        outs.append(copy)

    for copy in second:
        copy.wait()
    for r in range(steps):
        here = slice(r * K, (r + 1) * K)
        if r == 0:
            for copy in fields[0] + fields[1] + last[:1]:
                copy.wait()
        if r == 2:
            for copy in fields[2] + fields[3]:
                copy.wait()
        d = dep[here, :]
        high, low = halves(planes[1, here, :])
        flux_x = mm3(
            (mx[0, here, :], mx[1, here, :]),
            (jnp.concatenate([high, txs[0]], axis=0), jnp.concatenate([low, txs[1]], axis=0)),
            NN,
        )
        if r % 2 == 0:
            pair = slice(r * K, (r + 2) * K)
            pieces = []
            for c in range(cols // K):
                block = slice(c * K, (c + 1) * K)
                high, low = halves(planes[2, pair, block])
                lhs = (
                    jnp.concatenate([high, tyt[0][pair, :]], axis=1),
                    jnp.concatenate([low, tyt[1][pair, :]], axis=1),
                )
                pieces.append(mm3(lhs, (my[0, :, block], my[1, :, block]), NN))
        flux_y = jnp.concatenate([piece[(r % 2) * K : (r % 2 + 1) * K] for piece in pieces], axis=1)
        weighted_x = d * flux_x
        weighted_y = d * flux_y
        before_x = jnp.where(row == 0, carry, pltpu.roll(weighted_x, 1, 0))
        carry = weighted_x[K - 1 : K, :]
        turned = [side[here, 0:1]] + [
            pltpu.roll(weighted_y[:, c * K : (c + 1) * K], 1, 1) for c in range(cols // K)
        ]
        before_y = jnp.concatenate(
            [jnp.where(lane == 0, turned[c], turned[c + 1]) for c in range(cols // K)], axis=1
        )
        e = planes[0, here, :] + courant * ((weighted_x - before_x) + (weighted_y - before_y))
        elev[here, :] = e
        send(0, elev, r)
        right = [pltpu.roll(e[:, c * K : (c + 1) * K], K - 1, 1) for c in range(cols // K)] + [0.0]
        right = jnp.concatenate(
            [jnp.where(lane == K - 1, right[c + 1], right[c]) for c in range(cols // K)], axis=1
        )
        fy[here, :] = flux_y + courant * (right - e)
        send(2, fy, r)
        fx[here, :] = flux_x + courant * (jnp.where(row == K - 1, 0.0, pltpu.roll(e, K - 1, 0)) - e)
        if r > 0:
            end = slice(r * K - 8, r * K)
            fx[end, :] = fx[end, :] + jnp.where(row[:8] == 7, courant * e[0:1, :], 0.0)
            send(1, fx, r - 1)
        if r == 0:
            top = e[0:1, :]
        firsts.append(e[:, :K].T[0:1, :])
        for a in range(per):
            for w in range(cols // tile_w):
                tile = e[a * tile_h : (a + 1) * tile_h, w * tile_w : (w + 1) * tile_w]
                for b in range(modes):
                    at = b * (rows // tile_h) + r * per + a
                    mom[at : at + 1, w * tile_w : (w + 1) * tile_w] = jnp.sum(
                        tile * basis[b], axis=0, keepdims=True
                    )
    send(1, fx, steps - 1)
    for copy in last[1:]:
        copy.wait()
    tiles_y, tiles_x = wet.shape
    ones = jnp.ones((8, tile_w), bf16)
    pieces = []
    for w in range(tiles_y):
        high, low = halves(mom[:, w * tile_w : (w + 1) * tile_w])
        line = (mm(ones, high, NT) + mm(ones, low, NT))[0:1, :]
        keep = wet[w : w + 1, :].astype(f32)
        for b in range(modes):
            pieces.append(line[:, b * tiles_x : (b + 1) * tiles_x] * keep)
    high, low = halves(jnp.concatenate(pieces, axis=0))
    table = jnp.concatenate([high, low], axis=0)
    lines = tiles_y * modes
    acc = jnp.zeros((lines, count), f32)
    for step in range(2):
        both = mm(table, at_row[step], NN)
        acc = acc + (both[:lines] + both[lines:]) * share[step]
    total = jnp.sum(acc, axis=0, keepdims=True)
    placed = jnp.concatenate(halves(jnp.where(slot_of, total, 0.0)), axis=0)
    both = mm(device_of, placed, NT)
    sums = both[:, :slots] + both[:, slots:]
    parts[pl.ds(0, devices, stride=5), :] = jnp.concatenate(
        [sums, jnp.zeros((devices, K - slots), f32)], axis=1
    )
    size_y = lax.axis_size("gy")

    def put(device, line):
        for p in range(4):
            parts[pl.ds(device * 5 + 1 + p, 1), :] = line[:, p * K : (p + 1) * K]

    @pl.when(u > 0)
    def _():
        put((u - 1) * size_y + v, top)

    @pl.when(v > 0)
    def _():
        put(u * size_y + v - 1, jnp.concatenate(firsts, axis=1))

    outs.append(pltpu.make_async_copy(parts, parts_out, sems.at[10]))
    outs[-1].start()
    for copy in outs:
        copy.wait()


def elevation(tx, ta, tb, carried, adj, depth, basis, wet, owner):
    rows, cols = depth.shape
    modes, tile_h, tile_w = basis.shape
    devices = lax.axis_size("gx") * lax.axis_size("gy")
    steps = rows // K
    wet = wet.T
    owner = owner.reshape(1, -1)
    field = ((rows, cols), f32)
    far = (2 * ta.shape[0], 8, rows + EXTRA)
    parts = ((devices * 5, K), f32)
    like = lambda *arrays: [pltpu.VMEM(a.shape, a.dtype) for a in arrays]
    return pl.pallas_call(
        elev_kernel,
        out_shape=(pltpu.HBM((3, rows, cols), f32), pltpu.HBM(*parts)),
        in_specs=[vmem_spec()] + [pl.BlockSpec(memory_space=pl.ANY)] * 2 + [hbm_spec()] * 10,
        out_specs=(hbm_spec(),) * 2,
        scratch_shapes=[pltpu.VMEM(far, f32)]
        + like(*carried)
        + [pltpu.VMEM((3, rows, cols), f32), pltpu.VMEM(*field)]
        + like(basis, wet, owner)
        + [pltpu.VMEM(*field)] * 3
        + [
            pltpu.VMEM((far[0] * 8, far[2]), f32),
            pltpu.VMEM((rows // tile_h * modes, cols), f32),
            pltpu.VMEM(*parts),
            pltpu.SemaphoreType.DMA((11,)),
            pltpu.SemaphoreType.DMA((steps, 2)),
            pltpu.SemaphoreType.DMA((steps, 3)),
        ],
        compiler_params=pltpu.CompilerParams(vmem_limit_bytes=32 << 20),
        cost_estimate=cost(12 * rows * cols * K, 10 << 20),
        name="elevation",
    )(tx, ta, tb, *in_hbm(*carried, adj, depth, basis, wet, owner))


def finish_kernel(fields_in, sums, bottom_in, edge_in, fields, grad, bottom, edge, out_sems):
    u = lax.axis_index("gx")
    v = lax.axis_index("gy")
    size_x = lax.axis_size("gx")
    size_y = lax.axis_size("gy")
    rows, cols = fields.shape[1:]

    def line(device):
        return jnp.concatenate([sums[pl.ds(device * 5 + 1 + p, 1), :] for p in range(4)], axis=1)

    below = line(jnp.minimum(u + 1, size_x - 1) * size_y + v) * jnp.where(u + 1 < size_x, courant, 0.0)
    right = line(u * size_y + jnp.minimum(v + 1, size_y - 1)) * jnp.where(v + 1 < size_y, courant, 0.0)
    right = jnp.broadcast_to(right, (8, rows)).T[:, 0:1]
    edge[...] = edge_in[...] + jnp.where(iota((rows, K), 1) == K - 1, right, 0.0)
    bottom[...] = bottom_in[...] + jnp.where(iota((8, cols), 0) == 7, below, 0.0)
    writes = [
        pltpu.make_async_copy(edge, fields.at[2, :, pl.ds(cols - K, K)], out_sems.at[0]),
        pltpu.make_async_copy(bottom, fields.at[1, pl.ds(rows - 8, 8), :], out_sems.at[1]),
    ]
    for copy in writes:
        copy.start()
    devices = sums.shape[0] // 5
    total = jnp.sum(sums[pl.ds(0, devices, stride=5), :], axis=0, keepdims=True)
    grad[...] = total[:, : grad.shape[1]]
    for copy in writes:
        copy.wait()


def finish(fields, sums, slots):
    _, rows, cols = fields.shape
    bottom = fields[1, rows - 8 :, :]
    edge = fields[2, :, cols - K :]
    return pl.pallas_call(
        finish_kernel,
        out_shape=(pltpu.HBM(fields.shape, f32), jax.ShapeDtypeStruct((1, slots), f32)),
        in_specs=[hbm_spec(), vmem_spec(), vmem_spec(), vmem_spec()],
        out_specs=(hbm_spec(), vmem_spec()),
        input_output_aliases={0: 0},
        scratch_shapes=[
            pltpu.VMEM((8, cols), f32),
            pltpu.VMEM((rows, K), f32),
            pltpu.SemaphoreType.DMA((2,)),
        ],
        compiler_params=pltpu.CompilerParams(vmem_limit_bytes=16 << 20),
        cost_estimate=cost(1 << 20, 1 << 20),
        name="finish",
    )(*in_hbm(fields), sums, bottom, edge)


def rounds(size):
    return [size >> i for i in range(1, size.bit_length())]


def partner(axis, bit):
    return [(i, i ^ bit) for i in range(lax.axis_size(axis))]


def body(
    adj_fields, depth, block_x, reduced_x, block_y, reduced_y, basis, coef, footprint, owner, wet
):
    size_x = lax.axis_size("gx")
    size_y = lax.axis_size("gy")
    px, py = ends(adj_fields, depth, block_x, block_y, size_x, size_y)
    tx = lax.all_to_all(px, "gx", split_axis=0, concat_axis=0, tiled=True)
    matrices = carry(block_x, block_y, reduced_x, reduced_y)
    sides = shares(block_x, block_y, reduced_x, reduced_y, coef, footprint, wet)
    ty = py[None]
    bits = rounds(size_y)
    for bit in bits[:-1]:
        ty = jnp.concatenate([ty, lax.ppermute(ty, "gy", partner("gy", bit))], axis=0)
    ty, matrices = lax.optimization_barrier((ty, matrices))
    ty_far = lax.ppermute(ty, "gy", partner("gy", bits[-1]))
    carried = (*matrices, *sides)
    fields, parts = elevation(tx, ty, ty_far, carried, adj_fields, depth, basis, wet, owner)
    devices = size_x * size_y
    sums = lax.all_to_all(
        parts[:, None, :], ("gx", "gy"), split_axis=0, concat_axis=0, tiled=True
    )
    slots = owner.shape[0] // devices
    adj_before, grad = finish(fields, sums[:, 0, :], slots)
    return adj_before, grad.reshape(slots)


def solution(mesh):
    in_specs = (
        P(None, "gx", "gy"),
        P("gx", "gy"),
        P(),
        P(),
        P(),
        P(),
        P(),
        P(),
        P(),
        P(),
        P("gx", "gy"),
    )
    out_specs = (P(None, "gx", "gy"), P(("gx", "gy")))
    return jax.shard_map(body, mesh=mesh, in_specs=in_specs, out_specs=out_specs, check_vma=False)
```

```python
import jax
import jax.numpy as jnp
from jax import lax
from jax.experimental import pallas as pl
from jax.experimental.pallas import tpu as pltpu
from jax.sharding import PartitionSpec as P

courant = 0.5
f32 = jnp.float32
bf16 = jnp.bfloat16
K = 128
EXTRA = 128

NN = (((1,), (0,)), ((), ()))
NT = (((1,), (1,)), ((), ()))
TN = (((0,), (0,)), ((), ()))


def halves(x):
    high = x.astype(bf16)
    return high, (x - high.astype(f32)).astype(bf16)


def mm(a, b, dims):
    return lax.dot_general(a, b, dims, preferred_element_type=f32)


def mm3(a, b, dims):
    ah, al = a
    bh, bl = b
    return mm(ah, bh, dims) + (mm(ah, bl, dims) + mm(al, bh, dims))


def exact(a, b, dims):
    return lax.dot_general(a, b, dims, precision=lax.Precision.HIGHEST, preferred_element_type=f32)


def iota(shape, dim):
    return lax.broadcasted_iota(jnp.int32, shape, dim)


def hbm_spec():
    return pl.BlockSpec(memory_space=pltpu.HBM)


def vmem_spec():
    return pl.BlockSpec(memory_space=pltpu.VMEM)


def in_hbm(*arrays):
    return tuple(pltpu.with_memory_space_constraint(a, pltpu.HBM) for a in arrays)


def in_vmem(*arrays):
    return tuple(pltpu.with_memory_space_constraint(a, pltpu.VMEM) for a in arrays)


def cost(flops, nbytes):
    return pl.CostEstimate(flops=flops, bytes_accessed=nbytes, transcendentals=0)


def stacked(first, last, c):
    high, low = halves(jnp.concatenate([first[c, 0:1, :], last[c, 7:8, :]], axis=0))
    return jnp.concatenate([high, low], axis=0)


def two_rows(weights, field, dims):
    high, low = halves(field)
    both = mm(weights, high, dims)
    return both[0:2] + both[2:4] + mm(weights[0:2], low, dims)


def block_ends(blocks, index, first, last, sems):
    here = pl.ds(index * first.shape[0], first.shape[0])
    return [
        pltpu.make_async_copy(blocks.at[here, pl.ds(0, 8), :], first, sems.at[0]),
        pltpu.make_async_copy(blocks.at[here, pl.ds(K - 8, 8), :], last, sems.at[1]),
    ]


def ends_kernel(
    adj, depth, block_x, block_y, px_hbm, py,
    vx, vy, first_x, last_x, first_y, last_y, drow, dcol, px, sems, out_sems,
):
    rows, cols = vx.shape
    nbx = first_x.shape[0]
    nby = first_y.shape[0]
    small = block_ends(block_x, lax.axis_index("gx"), first_x, last_x, sems)
    small += block_ends(block_y, lax.axis_index("gy"), first_y, last_y, sems.at[pl.ds(2, 2)])
    small.append(pltpu.make_async_copy(depth.at[pl.ds(rows - 8, 8), :], drow, sems.at[4]))
    side = pltpu.make_async_copy(depth.at[:, pl.ds(cols - K, K)], dcol, sems.at[5])
    field_x = pltpu.make_async_copy(adj.at[1], vx, sems.at[6])
    field_y = pltpu.make_async_copy(adj.at[2], vy, sems.at[7])
    for copy in small + [field_x, side, field_y]:
        copy.start()
    for copy in small:
        copy.wait()
    for part in range(cols // K):
        px[part : part + 1, cols:] = drow[7:8, part * K : (part + 1) * K]
    px[cols // K :, cols:] = jnp.zeros((8 - cols // K, EXTRA), f32)
    weights_x = [stacked(first_x, last_x, c) for c in range(nbx)]
    weights_y = [stacked(first_y, last_y, c) for c in range(nby)]
    field_x.wait()
    for c in range(nbx):
        px[2 * c : 2 * c + 2, :cols] = two_rows(weights_x[c], vx[c * K : (c + 1) * K, :], NN)
    outs = [pltpu.make_async_copy(px, px_hbm.at[d], out_sems.at[d]) for d in range(px_hbm.shape[0])]
    for copy in outs:
        copy.start()
    side.wait()
    field_y.wait()
    at_last = (iota((8, K), 1) == K - 1).astype(f32).astype(bf16)
    high, low = halves(dcol[...])
    line = mm(at_last, high, NT) + mm(at_last, low, NT)
    for part in range(rows // K):
        py[part : part + 1, rows:] = line[0:1, part * K : (part + 1) * K]
    py[rows // K :, rows:] = jnp.zeros((8 - rows // K, EXTRA), f32)
    for r in range(rows // K):
        for c in range(nby):
            field = vy[r * K : (r + 1) * K, c * K : (c + 1) * K]
            py[2 * c : 2 * c + 2, r * K : (r + 1) * K] = two_rows(weights_y[c], field, NT)
    for copy in outs:
        copy.wait()


def ends(adj, depth, block_x, block_y, size_x, size_y):
    rows, cols = depth.shape
    nbx = block_x.shape[0] // size_x
    nby = block_y.shape[0] // size_y
    shape = (2 * nbx, cols + EXTRA)
    return pl.pallas_call(
        ends_kernel,
        out_shape=(
            pltpu.HBM((size_x, *shape), f32),
            jax.ShapeDtypeStruct((2 * nby, rows + EXTRA), f32),
        ),
        in_specs=[hbm_spec()] * 4,
        out_specs=(hbm_spec(), vmem_spec()),
        scratch_shapes=[
            pltpu.VMEM((rows, cols), f32),
            pltpu.VMEM((rows, cols), f32),
            pltpu.VMEM((nbx, 8, K), f32),
            pltpu.VMEM((nbx, 8, K), f32),
            pltpu.VMEM((nby, 8, K), f32),
            pltpu.VMEM((nby, 8, K), f32),
            pltpu.VMEM((8, cols), f32),
            pltpu.VMEM((rows, K), f32),
            pltpu.VMEM(shape, f32),
            pltpu.SemaphoreType.DMA((8,)),
            pltpu.SemaphoreType.DMA((size_x,)),
        ],
        compiler_params=pltpu.CompilerParams(vmem_limit_bytes=16 << 20),
        cost_estimate=cost(2 * rows * cols * 32, 3 << 20),
        name="ends",
    )(*in_hbm(adj, depth, block_x, block_y))


def carry_kernel(
    block_x, block_y, reduced_x_hbm, reduced_y_hbm, coef_hbm, footprint_hbm,
    mx_hbm, my_hbm, gside_hbm, share_hbm, at_row_hbm,
    mx, my, gside, share, at_row, wx, wy, wpx, wpy, reduced_x, reduced_y, coef, footprint, sems, out_sems,
):
    u = lax.axis_index("gx")
    v = lax.axis_index("gy")
    nbx = wx.shape[0]
    nby = wy.shape[0]
    before_x = jnp.maximum(u * nbx - 1, 0)
    before_y = jnp.maximum(v * nby - 1, 0)
    copies = [
        pltpu.make_async_copy(footprint_hbm, footprint, sems.at[0]),
        pltpu.make_async_copy(coef_hbm, coef, sems.at[1]),
        pltpu.make_async_copy(reduced_x_hbm, reduced_x, sems.at[2]),
        pltpu.make_async_copy(block_x.at[pl.ds(u * nbx, nbx)], wx, sems.at[3]),
        pltpu.make_async_copy(reduced_y_hbm, reduced_y, sems.at[4]),
        pltpu.make_async_copy(block_y.at[pl.ds(v * nby, nby)], wy, sems.at[5]),
        pltpu.make_async_copy(block_x.at[before_x, pl.ds(K - 8, 8), :], wpx, sems.at[6]),
        pltpu.make_async_copy(block_y.at[before_y, pl.ds(K - 8, 8), :], wpy, sems.at[7]),
    ]
    for copy in copies:
        copy.start()
    outs = [
        pltpu.make_async_copy(share, share_hbm, out_sems.at[0]),
        pltpu.make_async_copy(at_row, at_row_hbm, out_sems.at[1]),
        pltpu.make_async_copy(mx, mx_hbm, out_sems.at[2]),
        pltpu.make_async_copy(my, my_hbm, out_sems.at[3]),
        pltpu.make_async_copy(gside, gside_hbm, out_sems.at[4]),
    ]
    for copy in copies[:2]:
        copy.wait()
    places, modes, count = coef.shape
    tiles_y = share.shape[1] // modes
    tiles_x = at_row.shape[1]
    total_cols = tiles_y * lax.axis_size("gy")
    number = footprint[...]
    row = lax.shift_right_logical(number, total_cols.bit_length() - 1)
    col = (number & (total_cols - 1)) - v * tiles_y
    top = jnp.min(row, axis=0, keepdims=True)
    tile_row = iota((tiles_x, count), 0)
    tile_col = lax.shift_right_logical(iota((tiles_y * modes, count), 0), modes.bit_length() - 1)
    for step in range(2):
        at_row[step] = (tile_row == top + step - u * tiles_x).astype(f32).astype(bf16)
        index = jnp.where(row == top + step, col, -1)
        acc = jnp.zeros((tiles_y * modes, count), f32)
        for f in range(places):
            scale = jnp.concatenate([coef[f]] * tiles_y, axis=0)
            acc = acc + jnp.where(tile_col == index[f : f + 1, :], scale, 0.0)
        share[step] = acc
    for copy in outs[:2]:
        copy.start()
    for copy in copies[2:4]:
        copy.wait()
    own_x = reduced_x[pl.ds(pl.multiple_of(u * 8, 8), 8), :]
    prev_x = reduced_x[pl.ds(pl.multiple_of(jnp.maximum(u - 1, 0) * 8, 8), 8), :]
    for c in range(nbx):
        w = wx[c]
        g = w[:, 0:1] * own_x[2 * c : 2 * c + 1, :] + w[:, K - 1 : K] * own_x[2 * c + 1 : 2 * c + 2, :]
        for i, part in enumerate(zip(halves(w), halves(g))):
            mx[i, c * K : (c + 1) * K, :] = jnp.concatenate(part, axis=1)
    outs[2].start()
    for copy in copies[4:]:
        copy.wait()
    own_y = halves(reduced_y[pl.ds(pl.multiple_of(v * 8, 8), 8), :])
    prev_y = reduced_y[pl.ds(pl.multiple_of(jnp.maximum(v - 1, 0) * 8, 8), 8), :]
    sub = iota((8, K), 0)
    for c in range(nby):
        turned = wy[c].T
        across = jnp.where(sub == 2 * c, turned[0:1, :], 0.0)
        across = jnp.where(sub == 2 * c + 1, turned[K - 1 : K, :], across)
        g = mm3(own_y, halves(across), TN)
        for i, part in enumerate(zip(halves(turned), halves(g))):
            my[i, :, c * K : (c + 1) * K] = jnp.concatenate(part, axis=0)
    outs[3].start()

    def side(w, prev, index):
        width = prev.shape[1]
        g = w[7:8, 0:1] * prev[6:7, :] + w[7:8, K - 1 : K] * prev[7:8, :]
        g = g + (iota((1, width), 1) == index * 8 - 1).astype(f32)
        return jnp.where(index > 0, g, 0.0)

    gside[...] = jnp.zeros(gside.shape, f32)
    gside[0:1, :] = side(wpx[...], prev_x, u)
    gside[1:2, : reduced_y.shape[1]] = side(wpy[...], prev_y, v)
    outs[4].start()
    for copy in outs:
        copy.wait()


def carry(block_x, block_y, reduced_x, reduced_y, coef, footprint, wet):
    nbx = block_x.shape[0] // lax.axis_size("gx")
    nby = block_y.shape[0] // lax.axis_size("gy")
    coef = coef.transpose(1, 2, 0)
    footprint = footprint.T
    _, modes, count = coef.shape
    tiles_x, tiles_y = wet.shape
    results = [
        ((2, nbx * K, K + reduced_x.shape[0]), bf16),
        ((2, K + reduced_y.shape[0], nby * K), bf16),
        ((8, reduced_x.shape[0]), f32),
        ((2, tiles_y * modes, count), f32),
        ((2, tiles_x, count), bf16),
    ]
    return pl.pallas_call(
        carry_kernel,
        out_shape=tuple(pltpu.HBM(*result) for result in results),
        in_specs=[hbm_spec()] * 6,
        out_specs=(hbm_spec(),) * 5,
        scratch_shapes=[pltpu.VMEM(*result) for result in results]
        + [
            pltpu.VMEM((nbx, K, K), f32),
            pltpu.VMEM((nby, K, K), f32),
            pltpu.VMEM((8, K), f32),
            pltpu.VMEM((8, K), f32),
            pltpu.VMEM(reduced_x.shape, f32),
            pltpu.VMEM(reduced_y.shape, f32),
            pltpu.VMEM(coef.shape, f32),
            pltpu.VMEM(footprint.shape, jnp.int32),
            pltpu.SemaphoreType.DMA((8,)),
            pltpu.SemaphoreType.DMA((5,)),
        ],
        compiler_params=pltpu.CompilerParams(vmem_limit_bytes=16 << 20),
        cost_estimate=cost(1 << 24, 2 << 20),
        name="carry",
    )(*in_hbm(block_x, block_y, reduced_x, reduced_y, coef, footprint))


def elev_kernel(
    tx, ta_in, tb_in, mx_in, my_in, gside_in, share_in, at_row_in, adj, depth, basis_in, wet_in, owner_in,
    fields_out, parts_out, erow_out, ecol_out,
    ty, mx, my, gside, share, at_row, planes, dep, basis, wet, owner,
    elev, fx, fy, tyn, mom, parts, erow, ecol, sems, row_sems, out_sems,
):
    u = lax.axis_index("gx")
    v = lax.axis_index("gy")
    rows, cols = dep.shape
    steps = rows // K
    half = ta_in.shape[0]
    first = [
        pltpu.make_async_copy(ta_in, ty.at[pl.ds(0, half)], sems.at[0]),
        pltpu.make_async_copy(tb_in, ty.at[pl.ds(half, half)], sems.at[1]),
        pltpu.make_async_copy(gside_in, gside, sems.at[2]),
        pltpu.make_async_copy(owner_in, owner, sems.at[3]),
    ]
    second = [
        pltpu.make_async_copy(mx_in, mx, sems.at[4]),
        pltpu.make_async_copy(my_in, my, sems.at[5]),
    ]
    last = [
        pltpu.make_async_copy(basis_in, basis, sems.at[6]),
        pltpu.make_async_copy(wet_in, wet, sems.at[7]),
        pltpu.make_async_copy(share_in, share, sems.at[8]),
        pltpu.make_async_copy(at_row_in, at_row, sems.at[9]),
    ]
    fields = []
    for r in range(steps):
        here = pl.ds(r * K, K)
        fields.append(
            [
                pltpu.make_async_copy(adj.at[:, here, :], planes.at[:, here, :], row_sems.at[r, 0]),
                pltpu.make_async_copy(depth.at[here, :], dep.at[here, :], row_sems.at[r, 1]),
            ]
        )
    for group in [fields[0], first, second, fields[1], last[:1], fields[2], fields[3], last[1:]]:
        for copy in group:
            copy.start()
    txs = halves(jnp.concatenate([tx[d][:, :cols] for d in range(tx.shape[0])], axis=0))
    for copy in first:
        copy.wait()
    devices = parts.shape[0]
    count = owner.shape[1]
    slots = count // devices
    own = owner[...]
    device_of = iota((devices, count), 0) == lax.shift_right_logical(own, slots.bit_length() - 1)
    device_of = device_of.astype(f32).astype(bf16)
    slot_of = iota((slots, count), 0) == (own & (slots - 1))
    for j in range(2 * half):
        far = j ^ v
        place = 0
        for i, bit in enumerate(rounds(2 * half)):
            place = place | (((far // bit) & 1) << i)
        tyn[j * 8 : (j + 1) * 8, :] = ty[place]
    ty_all = tyn[:, :rows]
    tys = halves(ty_all)
    tyt = halves(ty_all.T)
    up = jnp.maximum(u - 1, 0)
    left = jnp.maximum(v - 1, 0)
    gs = gside[...]
    edge_x = mm3(halves(gs), txs, NN)[0:1, :]
    edge_y = mm3(halves(gs[:, : ty_all.shape[0]]), tys, NN)[1:2, :]
    drow = tx[up][:, cols:]
    drow = jnp.concatenate([drow[p : p + 1, :] for p in range(cols // K)], axis=1)
    dcol = tyn[pl.ds(pl.multiple_of(left * 8, 8), 8), rows:]
    dcol = jnp.concatenate([dcol[p : p + 1, :] for p in range(rows // K)], axis=1)
    carry = edge_x * drow
    side = jnp.broadcast_to(edge_y * dcol, (8, rows)).T
    row = iota((K, cols), 0)
    lane = iota((K, K), 1)
    modes, tile_h, tile_w = basis.shape
    per = K // tile_h
    outs = []

    def send(plane, source, r):
        here = pl.ds(r * K, K)
        copy = pltpu.make_async_copy(
            source.at[here, :], fields_out.at[plane, here, :], out_sems.at[r, plane]
        )
        copy.start()
        outs.append(copy)

    for copy in second:
        copy.wait()
    for r in range(steps):
        here = slice(r * K, (r + 1) * K)
        if r == 0:
            for copy in fields[0] + fields[1] + last[:1]:
                copy.wait()
        if r == 2:
            for copy in fields[2] + fields[3]:
                copy.wait()
        d = dep[here, :]
        high, low = halves(planes[1, here, :])
        flux_x = mm3(
            (mx[0, here, :], mx[1, here, :]),
            (jnp.concatenate([high, txs[0]], axis=0), jnp.concatenate([low, txs[1]], axis=0)),
            NN,
        )
        if r % 2 == 0:
            pair = slice(r * K, (r + 2) * K)
            pieces = []
            for c in range(cols // K):
                block = slice(c * K, (c + 1) * K)
                high, low = halves(planes[2, pair, block])
                lhs = (
                    jnp.concatenate([high, tyt[0][pair, :]], axis=1),
                    jnp.concatenate([low, tyt[1][pair, :]], axis=1),
                )
                pieces.append(mm3(lhs, (my[0, :, block], my[1, :, block]), NN))
        flux_y = jnp.concatenate([piece[(r % 2) * K : (r % 2 + 1) * K] for piece in pieces], axis=1)
        weighted_x = d * flux_x
        weighted_y = d * flux_y
        before_x = jnp.where(row == 0, carry, pltpu.roll(weighted_x, 1, 0))
        carry = weighted_x[K - 1 : K, :]
        turned = [side[here, 0:1]] + [
            pltpu.roll(weighted_y[:, c * K : (c + 1) * K], 1, 1) for c in range(cols // K)
        ]
        before_y = jnp.concatenate(
            [jnp.where(lane == 0, turned[c], turned[c + 1]) for c in range(cols // K)], axis=1
        )
        e = planes[0, here, :] + courant * ((weighted_x - before_x) + (weighted_y - before_y))
        elev[here, :] = e
        send(0, elev, r)
        right = [pltpu.roll(e[:, c * K : (c + 1) * K], K - 1, 1) for c in range(cols // K)] + [0.0]
        right = jnp.concatenate(
            [jnp.where(lane == K - 1, right[c + 1], right[c]) for c in range(cols // K)], axis=1
        )
        fy[here, :] = flux_y + courant * (right - e)
        send(2, fy, r)
        fx[here, :] = flux_x + courant * (jnp.where(row == K - 1, 0.0, pltpu.roll(e, K - 1, 0)) - e)
        if r > 0:
            end = slice(r * K - 8, r * K)
            fx[end, :] = fx[end, :] + jnp.where(row[:8] == 7, courant * e[0:1, :], 0.0)
            send(1, fx, r - 1)
        if r == 0:
            erow[...] = e[0:1, :]
            outs.append(pltpu.make_async_copy(erow, erow_out, sems.at[11]))
            outs[-1].start()
        ecol[:, here] = e[:, :K].T[0:1, :]
        for a in range(per):
            for w in range(cols // tile_w):
                tile = e[a * tile_h : (a + 1) * tile_h, w * tile_w : (w + 1) * tile_w]
                for b in range(modes):
                    at = b * (rows // tile_h) + r * per + a
                    mom[at : at + 1, w * tile_w : (w + 1) * tile_w] = jnp.sum(
                        tile * basis[b], axis=0, keepdims=True
                    )
    send(1, fx, steps - 1)
    outs.append(pltpu.make_async_copy(ecol, ecol_out, sems.at[12]))
    outs[-1].start()
    for copy in last[1:]:
        copy.wait()
    tiles_y, tiles_x = wet.shape
    ones = jnp.ones((8, tile_w), bf16)
    pieces = []
    for w in range(tiles_y):
        high, low = halves(mom[:, w * tile_w : (w + 1) * tile_w])
        line = (mm(ones, high, NT) + mm(ones, low, NT))[0:1, :]
        keep = wet[w : w + 1, :].astype(f32)
        for b in range(modes):
            pieces.append(line[:, b * tiles_x : (b + 1) * tiles_x] * keep)
    high, low = halves(jnp.concatenate(pieces, axis=0))
    table = jnp.concatenate([high, low], axis=0)
    lines = tiles_y * modes
    acc = jnp.zeros((lines, count), f32)
    for step in range(2):
        both = mm(table, at_row[step], NN)
        acc = acc + (both[:lines] + both[lines:]) * share[step]
    total = jnp.sum(acc, axis=0, keepdims=True)
    placed = jnp.concatenate(halves(jnp.where(slot_of, total, 0.0)), axis=0)
    both = mm(device_of, placed, NT)
    sums = both[:, :slots] + both[:, slots:]
    parts[...] = jnp.concatenate([sums, jnp.zeros((devices, K - slots), f32)], axis=1)
    outs.append(pltpu.make_async_copy(parts, parts_out, sems.at[10]))
    outs[-1].start()
    for copy in outs:
        copy.wait()


def elevation(tx, ta, tb, carried, adj, depth, basis, wet, owner):
    rows, cols = depth.shape
    modes, tile_h, tile_w = basis.shape
    devices = lax.axis_size("gx") * lax.axis_size("gy")
    steps = rows // K
    wet = wet.T
    owner = owner.reshape(1, -1)
    field = ((rows, cols), f32)
    far = (2 * ta.shape[0], 8, rows + EXTRA)
    parts = ((devices, K), f32)
    halos = [((1, cols), f32), ((1, rows), f32)]
    like = lambda *arrays: [pltpu.VMEM(a.shape, a.dtype) for a in arrays]
    return pl.pallas_call(
        elev_kernel,
        out_shape=(pltpu.HBM((3, rows, cols), f32), pltpu.HBM(*parts), *(pltpu.HBM(*h) for h in halos)),
        in_specs=[vmem_spec()] + [pl.BlockSpec(memory_space=pl.ANY)] * 2 + [hbm_spec()] * 10,
        out_specs=(hbm_spec(),) * 4,
        scratch_shapes=[pltpu.VMEM(far, f32)]
        + like(*carried)
        + [pltpu.VMEM((3, rows, cols), f32), pltpu.VMEM(*field)]
        + like(basis, wet, owner)
        + [pltpu.VMEM(*field)] * 3
        + [
            pltpu.VMEM((far[0] * 8, far[2]), f32),
            pltpu.VMEM((rows // tile_h * modes, cols), f32),
            pltpu.VMEM(*parts),
            *(pltpu.VMEM(*h) for h in halos),
            pltpu.SemaphoreType.DMA((13,)),
            pltpu.SemaphoreType.DMA((steps, 2)),
            pltpu.SemaphoreType.DMA((steps, 3)),
        ],
        compiler_params=pltpu.CompilerParams(vmem_limit_bytes=32 << 20),
        cost_estimate=cost(12 * rows * cols * K, 10 << 20),
        name="elevation",
    )(tx, ta, tb, *in_hbm(*carried, adj, depth, basis, wet, owner))


def finish_kernel(fields_in, sums, hrow, hcol, bottom_in, edge_in, fields, grad, bottom, edge, out_sems):
    u = lax.axis_index("gx")
    v = lax.axis_index("gy")
    size_x = lax.axis_size("gx")
    size_y = lax.axis_size("gy")
    rows, cols = fields.shape[1:]

    below = hrow[...] * jnp.where(u + 1 < size_x, courant, 0.0)
    right = hcol[...] * jnp.where(v + 1 < size_y, courant, 0.0)
    right = jnp.broadcast_to(right, (8, rows)).T[:, 0:1]
    edge[...] = edge_in[...] + jnp.where(iota((rows, K), 1) == K - 1, right, 0.0)
    bottom[...] = bottom_in[...] + jnp.where(iota((8, cols), 0) == 7, below, 0.0)
    writes = [
        pltpu.make_async_copy(edge, fields.at[2, :, pl.ds(cols - K, K)], out_sems.at[0]),
        pltpu.make_async_copy(bottom, fields.at[1, pl.ds(rows - 8, 8), :], out_sems.at[1]),
    ]
    for copy in writes:
        copy.start()
    total = jnp.sum(sums[...], axis=0, keepdims=True)
    grad[...] = total[:, : grad.shape[1]]
    for copy in writes:
        copy.wait()


def finish(fields, sums, hrow, hcol, slots):
    _, rows, cols = fields.shape
    bottom = fields[1, rows - 8 :, :]
    edge = fields[2, :, cols - K :]
    return pl.pallas_call(
        finish_kernel,
        out_shape=(pltpu.HBM(fields.shape, f32), jax.ShapeDtypeStruct((1, slots), f32)),
        in_specs=[hbm_spec()] + [vmem_spec()] * 5,
        out_specs=(hbm_spec(), vmem_spec()),
        input_output_aliases={0: 0},
        scratch_shapes=[
            pltpu.VMEM((8, cols), f32),
            pltpu.VMEM((rows, K), f32),
            pltpu.SemaphoreType.DMA((2,)),
        ],
        compiler_params=pltpu.CompilerParams(vmem_limit_bytes=16 << 20),
        cost_estimate=cost(1 << 20, 1 << 20),
        name="finish",
    )(*in_hbm(fields), sums, hrow, hcol, bottom, edge)


def rounds(size):
    return [size >> i for i in range(1, size.bit_length())]


def partner(axis, bit):
    return [(i, i ^ bit) for i in range(lax.axis_size(axis))]


def previous(axis):
    size = lax.axis_size(axis)
    return [(i, (i - 1) % size) for i in range(size)]


def body(
    adj_fields, depth, block_x, reduced_x, block_y, reduced_y, basis, coef, footprint, owner, wet
):
    size_x = lax.axis_size("gx")
    size_y = lax.axis_size("gy")
    px, py = ends(adj_fields, depth, block_x, block_y, size_x, size_y)
    tx = lax.all_to_all(px, "gx", split_axis=0, concat_axis=0, tiled=True)
    carried = carry(block_x, block_y, reduced_x, reduced_y, coef, footprint, wet)
    ty = py[None]
    bits = rounds(size_y)
    for bit in bits[:-1]:
        ty = jnp.concatenate([ty, lax.ppermute(ty, "gy", partner("gy", bit))], axis=0)
    ty, carried = lax.optimization_barrier((ty, carried))
    ty_far = lax.ppermute(ty, "gy", partner("gy", bits[-1]))
    fields, parts, erow, ecol = elevation(tx, ty, ty_far, carried, adj_fields, depth, basis, wet, owner)
    devices = size_x * size_y
    hrow = lax.ppermute(erow, "gx", previous("gx"))
    hcol = lax.ppermute(ecol, "gy", previous("gy"))
    sums = lax.all_to_all(
        parts[:, None, :], ("gx", "gy"), split_axis=0, concat_axis=0, tiled=True
    )
    slots = owner.shape[0] // devices
    adj_before, grad = finish(fields, sums[:, 0, :], hrow, hcol, slots)
    return adj_before, grad.reshape(slots)


def solution(mesh):
    in_specs = (
        P(None, "gx", "gy"),
        P("gx", "gy"),
        P(),
        P(),
        P(),
        P(),
        P(),
        P(),
        P(),
        P(),
        P("gx", "gy"),
    )
    out_specs = (P(None, "gx", "gy"), P(("gx", "gy")))
    return jax.shard_map(body, mesh=mesh, in_specs=in_specs, out_specs=out_specs, check_vma=False)
```

```python
import jax
import jax.numpy as jnp
from jax import lax
from jax.experimental import pallas as pl
from jax.experimental.pallas import tpu as pltpu
from jax.sharding import PartitionSpec as P

courant = 0.5
f32 = jnp.float32
bf16 = jnp.bfloat16
K = 128
EXTRA = 128

NN = (((1,), (0,)), ((), ()))
NT = (((1,), (1,)), ((), ()))
TN = (((0,), (0,)), ((), ()))


def halves(x):
    high = x.astype(bf16)
    return high, (x - high.astype(f32)).astype(bf16)


def mm(a, b, dims):
    return lax.dot_general(a, b, dims, preferred_element_type=f32)


def mm3(a, b, dims):
    ah, al = a
    bh, bl = b
    return mm(ah, bh, dims) + (mm(ah, bl, dims) + mm(al, bh, dims))


def exact(a, b, dims):
    return lax.dot_general(a, b, dims, precision=lax.Precision.HIGHEST, preferred_element_type=f32)


def iota(shape, dim):
    return lax.broadcasted_iota(jnp.int32, shape, dim)


def hbm_spec():
    return pl.BlockSpec(memory_space=pltpu.HBM)


def vmem_spec():
    return pl.BlockSpec(memory_space=pltpu.VMEM)


def in_hbm(*arrays):
    return tuple(pltpu.with_memory_space_constraint(a, pltpu.HBM) for a in arrays)


def in_vmem(*arrays):
    return tuple(pltpu.with_memory_space_constraint(a, pltpu.VMEM) for a in arrays)


def cost(flops, nbytes):
    return pl.CostEstimate(flops=flops, bytes_accessed=nbytes, transcendentals=0)


def stacked(first, last, c):
    high, low = halves(jnp.concatenate([first[c, 0:1, :], last[c, 7:8, :]], axis=0))
    return jnp.concatenate([high, low], axis=0)


def two_rows(weights, field, dims):
    high, low = halves(field)
    both = mm(weights, high, dims)
    return both[0:2] + both[2:4] + mm(weights[0:2], low, dims)


def block_ends(blocks, index, first, last, sems):
    here = pl.ds(index * first.shape[0], first.shape[0])
    return [
        pltpu.make_async_copy(blocks.at[here, pl.ds(0, 8), :], first, sems.at[0]),
        pltpu.make_async_copy(blocks.at[here, pl.ds(K - 8, 8), :], last, sems.at[1]),
    ]


def ends_kernel(
    adj, depth, block_x, block_y, px_hbm, py,
    vx, vy, first_x, last_x, first_y, last_y, drow, dcol, px, sems, out_sems,
):
    rows, cols = vx.shape
    nbx = first_x.shape[0]
    nby = first_y.shape[0]
    small = block_ends(block_x, lax.axis_index("gx"), first_x, last_x, sems)
    small += block_ends(block_y, lax.axis_index("gy"), first_y, last_y, sems.at[pl.ds(2, 2)])
    small.append(pltpu.make_async_copy(depth.at[pl.ds(rows - 8, 8), :], drow, sems.at[4]))
    side = pltpu.make_async_copy(depth.at[:, pl.ds(cols - K, K)], dcol, sems.at[5])
    field_x = pltpu.make_async_copy(adj.at[1], vx, sems.at[6])
    field_y = pltpu.make_async_copy(adj.at[2], vy, sems.at[7])
    for copy in small + [field_x, side, field_y]:
        copy.start()
    for copy in small:
        copy.wait()
    for part in range(cols // K):
        px[part : part + 1, cols:] = drow[7:8, part * K : (part + 1) * K]
    px[cols // K :, cols:] = jnp.zeros((8 - cols // K, EXTRA), f32)
    weights_x = [stacked(first_x, last_x, c) for c in range(nbx)]
    weights_y = [stacked(first_y, last_y, c) for c in range(nby)]
    field_x.wait()
    for c in range(nbx):
        px[2 * c : 2 * c + 2, :cols] = two_rows(weights_x[c], vx[c * K : (c + 1) * K, :], NN)
    outs = [pltpu.make_async_copy(px, px_hbm.at[d], out_sems.at[d]) for d in range(px_hbm.shape[0])]
    for copy in outs:
        copy.start()
    side.wait()
    field_y.wait()
    at_last = (iota((8, K), 1) == K - 1).astype(f32).astype(bf16)
    high, low = halves(dcol[...])
    line = mm(at_last, high, NT) + mm(at_last, low, NT)
    for part in range(rows // K):
        py[part : part + 1, rows:] = line[0:1, part * K : (part + 1) * K]
    py[rows // K :, rows:] = jnp.zeros((8 - rows // K, EXTRA), f32)
    for r in range(rows // K):
        for c in range(nby):
            field = vy[r * K : (r + 1) * K, c * K : (c + 1) * K]
            py[2 * c : 2 * c + 2, r * K : (r + 1) * K] = two_rows(weights_y[c], field, NT)
    for copy in outs:
        copy.wait()


def ends(adj, depth, block_x, block_y, size_x, size_y):
    rows, cols = depth.shape
    nbx = block_x.shape[0] // size_x
    nby = block_y.shape[0] // size_y
    shape = (2 * nbx, cols + EXTRA)
    return pl.pallas_call(
        ends_kernel,
        out_shape=(
            pltpu.HBM((size_x, *shape), f32),
            jax.ShapeDtypeStruct((2 * nby, rows + EXTRA), f32),
        ),
        in_specs=[hbm_spec()] * 4,
        out_specs=(hbm_spec(), vmem_spec()),
        scratch_shapes=[
            pltpu.VMEM((rows, cols), f32),
            pltpu.VMEM((rows, cols), f32),
            pltpu.VMEM((nbx, 8, K), f32),
            pltpu.VMEM((nbx, 8, K), f32),
            pltpu.VMEM((nby, 8, K), f32),
            pltpu.VMEM((nby, 8, K), f32),
            pltpu.VMEM((8, cols), f32),
            pltpu.VMEM((rows, K), f32),
            pltpu.VMEM(shape, f32),
            pltpu.SemaphoreType.DMA((8,)),
            pltpu.SemaphoreType.DMA((size_x,)),
        ],
        compiler_params=pltpu.CompilerParams(vmem_limit_bytes=16 << 20),
        cost_estimate=cost(2 * rows * cols * 32, 3 << 20),
        name="ends",
    )(*in_hbm(adj, depth, block_x, block_y))


def carry_kernel(
    block_x, block_y, reduced_x_hbm, reduced_y_hbm, coef_hbm, footprint_hbm,
    mx_hbm, my_hbm, gside_hbm, share_hbm, at_row_hbm,
    mx, my, gside, share, at_row, wx, wy, wpx, wpy, reduced_x, reduced_y, coef, footprint, sems, out_sems,
):
    u = lax.axis_index("gx")
    v = lax.axis_index("gy")
    nbx = wx.shape[0]
    nby = wy.shape[0]
    before_x = jnp.maximum(u * nbx - 1, 0)
    before_y = jnp.maximum(v * nby - 1, 0)
    copies = [
        pltpu.make_async_copy(footprint_hbm, footprint, sems.at[0]),
        pltpu.make_async_copy(coef_hbm, coef, sems.at[1]),
        pltpu.make_async_copy(reduced_x_hbm, reduced_x, sems.at[2]),
        pltpu.make_async_copy(block_x.at[pl.ds(u * nbx, nbx)], wx, sems.at[3]),
        pltpu.make_async_copy(reduced_y_hbm, reduced_y, sems.at[4]),
        pltpu.make_async_copy(block_y.at[pl.ds(v * nby, nby)], wy, sems.at[5]),
        pltpu.make_async_copy(block_x.at[before_x, pl.ds(K - 8, 8), :], wpx, sems.at[6]),
        pltpu.make_async_copy(block_y.at[before_y, pl.ds(K - 8, 8), :], wpy, sems.at[7]),
    ]
    for copy in copies:
        copy.start()
    outs = [
        pltpu.make_async_copy(share, share_hbm, out_sems.at[0]),
        pltpu.make_async_copy(at_row, at_row_hbm, out_sems.at[1]),
        pltpu.make_async_copy(mx, mx_hbm, out_sems.at[2]),
        pltpu.make_async_copy(my, my_hbm, out_sems.at[3]),
        pltpu.make_async_copy(gside, gside_hbm, out_sems.at[4]),
    ]
    for copy in copies[:2]:
        copy.wait()
    places, modes, count = coef.shape
    tiles_y = share.shape[1] // modes
    tiles_x = at_row.shape[1]
    total_cols = tiles_y * lax.axis_size("gy")
    number = footprint[...]
    row = lax.shift_right_logical(number, total_cols.bit_length() - 1)
    col = (number & (total_cols - 1)) - v * tiles_y
    top = jnp.min(row, axis=0, keepdims=True)
    tile_row = iota((tiles_x, count), 0)
    tile_col = lax.shift_right_logical(iota((tiles_y * modes, count), 0), modes.bit_length() - 1)
    for step in range(2):
        at_row[step] = (tile_row == top + step - u * tiles_x).astype(f32).astype(bf16)
        index = jnp.where(row == top + step, col, -1)
        acc = jnp.zeros((tiles_y * modes, count), f32)
        for f in range(places):
            scale = jnp.concatenate([coef[f]] * tiles_y, axis=0)
            acc = acc + jnp.where(tile_col == index[f : f + 1, :], scale, 0.0)
        share[step] = acc
    for copy in outs[:2]:
        copy.start()
    for copy in copies[2:4]:
        copy.wait()
    own_x = reduced_x[pl.ds(pl.multiple_of(u * 8, 8), 8), :]
    prev_x = reduced_x[pl.ds(pl.multiple_of(jnp.maximum(u - 1, 0) * 8, 8), 8), :]
    for c in range(nbx):
        w = wx[c]
        g = w[:, 0:1] * own_x[2 * c : 2 * c + 1, :] + w[:, K - 1 : K] * own_x[2 * c + 1 : 2 * c + 2, :]
        for i, part in enumerate(zip(halves(w), halves(g))):
            mx[i, c * K : (c + 1) * K, :] = jnp.concatenate(part, axis=1)
    outs[2].start()
    for copy in copies[4:]:
        copy.wait()
    own_y = halves(reduced_y[pl.ds(pl.multiple_of(v * 8, 8), 8), :])
    prev_y = reduced_y[pl.ds(pl.multiple_of(jnp.maximum(v - 1, 0) * 8, 8), 8), :]
    sub = iota((8, K), 0)
    for c in range(nby):
        turned = wy[c].T
        across = jnp.where(sub == 2 * c, turned[0:1, :], 0.0)
        across = jnp.where(sub == 2 * c + 1, turned[K - 1 : K, :], across)
        g = mm3(own_y, halves(across), TN)
        for i, part in enumerate(zip(halves(turned), halves(g))):
            my[i, :, c * K : (c + 1) * K] = jnp.concatenate(part, axis=0)
    outs[3].start()

    def side(w, prev, index):
        width = prev.shape[1]
        g = w[7:8, 0:1] * prev[6:7, :] + w[7:8, K - 1 : K] * prev[7:8, :]
        g = g + (iota((1, width), 1) == index * 8 - 1).astype(f32)
        return jnp.where(index > 0, g, 0.0)

    gside[...] = jnp.zeros(gside.shape, f32)
    gside[0:1, :] = side(wpx[...], prev_x, u)
    gside[1:2, : reduced_y.shape[1]] = side(wpy[...], prev_y, v)
    outs[4].start()
    for copy in outs:
        copy.wait()


def carry(block_x, block_y, reduced_x, reduced_y, coef, footprint, wet):
    nbx = block_x.shape[0] // lax.axis_size("gx")
    nby = block_y.shape[0] // lax.axis_size("gy")
    coef = coef.transpose(1, 2, 0)
    footprint = footprint.T
    _, modes, count = coef.shape
    tiles_x, tiles_y = wet.shape
    results = [
        ((2, nbx * K, K + reduced_x.shape[0]), bf16),
        ((2, K + reduced_y.shape[0], nby * K), bf16),
        ((8, reduced_x.shape[0]), f32),
        ((2, tiles_y * modes, count), f32),
        ((2, tiles_x, count), bf16),
    ]
    return pl.pallas_call(
        carry_kernel,
        out_shape=tuple(pltpu.HBM(*result) for result in results),
        in_specs=[hbm_spec()] * 6,
        out_specs=(hbm_spec(),) * 5,
        scratch_shapes=[pltpu.VMEM(*result) for result in results]
        + [
            pltpu.VMEM((nbx, K, K), f32),
            pltpu.VMEM((nby, K, K), f32),
            pltpu.VMEM((8, K), f32),
            pltpu.VMEM((8, K), f32),
            pltpu.VMEM(reduced_x.shape, f32),
            pltpu.VMEM(reduced_y.shape, f32),
            pltpu.VMEM(coef.shape, f32),
            pltpu.VMEM(footprint.shape, jnp.int32),
            pltpu.SemaphoreType.DMA((8,)),
            pltpu.SemaphoreType.DMA((5,)),
        ],
        compiler_params=pltpu.CompilerParams(vmem_limit_bytes=16 << 20),
        cost_estimate=cost(1 << 36, 2 << 20),
        name="carry",
    )(*in_hbm(block_x, block_y, reduced_x, reduced_y, coef, footprint))


def elev_kernel(
    tx, t0, t1, t2, t3, mx_in, my_in, gside_in, share_in, at_row_in, adj, depth, basis_in, wet_in, owner_in,
    fields_out, parts_out, erow_out, ecol_out,
    ty, mx, my, gside, share, at_row, planes, dep, basis, wet, owner,
    elev, fx, fy, tyn, mom, parts, erow, ecol, sems, row_sems, out_sems,
):
    u = lax.axis_index("gx")
    v = lax.axis_index("gy")
    rows, cols = dep.shape
    steps = rows // K
    near = (t0, t1, t2, t3)
    first = [
        *(pltpu.make_async_copy(part, ty.at[i], sems.at[13 + i]) for i, part in enumerate(near)),
        pltpu.make_async_copy(gside_in, gside, sems.at[2]),
        pltpu.make_async_copy(owner_in, owner, sems.at[3]),
    ]
    second = [
        pltpu.make_async_copy(mx_in, mx, sems.at[4]),
        pltpu.make_async_copy(my_in, my, sems.at[5]),
    ]
    last = [
        pltpu.make_async_copy(basis_in, basis, sems.at[6]),
        pltpu.make_async_copy(wet_in, wet, sems.at[7]),
        pltpu.make_async_copy(share_in, share, sems.at[8]),
        pltpu.make_async_copy(at_row_in, at_row, sems.at[9]),
    ]
    fields = []
    for r in range(steps):
        here = pl.ds(r * K, K)
        fields.append(
            [
                pltpu.make_async_copy(adj.at[:, here, :], planes.at[:, here, :], row_sems.at[r, 0]),
                pltpu.make_async_copy(depth.at[here, :], dep.at[here, :], row_sems.at[r, 1]),
            ]
        )
    for group in [fields[0], first, second, fields[1], last[:1], fields[2], fields[3], last[1:]]:
        for copy in group:
            copy.start()
    txs = halves(jnp.concatenate([tx[d][:, :cols] for d in range(tx.shape[0])], axis=0))
    for copy in first:
        copy.wait()
    devices = parts.shape[0]
    count = owner.shape[1]
    slots = count // devices
    own = owner[...]
    device_of = iota((devices, count), 0) == lax.shift_right_logical(own, slots.bit_length() - 1)
    device_of = device_of.astype(f32).astype(bf16)
    slot_of = iota((slots, count), 0) == (own & (slots - 1))
    for j in range(ty.shape[0] * ty.shape[1]):
        far = j ^ v
        tyn[j * 8 : (j + 1) * 8, :] = ty[far & (ty.shape[0] - 1), far // ty.shape[0]]
    ty_all = tyn[:, :rows]
    tys = halves(ty_all)
    tyt = halves(ty_all.T)
    up = jnp.maximum(u - 1, 0)
    left = jnp.maximum(v - 1, 0)
    gs = gside[...]
    edge_x = mm3(halves(gs), txs, NN)[0:1, :]
    edge_y = mm3(halves(gs[:, : ty_all.shape[0]]), tys, NN)[1:2, :]
    drow = tx[up][:, cols:]
    drow = jnp.concatenate([drow[p : p + 1, :] for p in range(cols // K)], axis=1)
    dcol = tyn[pl.ds(pl.multiple_of(left * 8, 8), 8), rows:]
    dcol = jnp.concatenate([dcol[p : p + 1, :] for p in range(rows // K)], axis=1)
    carry = edge_x * drow
    side = jnp.broadcast_to(edge_y * dcol, (8, rows)).T
    row = iota((K, cols), 0)
    lane = iota((K, K), 1)
    modes, tile_h, tile_w = basis.shape
    per = K // tile_h
    outs = []

    def send(plane, source, r):
        here = pl.ds(r * K, K)
        copy = pltpu.make_async_copy(
            source.at[here, :], fields_out.at[plane, here, :], out_sems.at[r, plane]
        )
        copy.start()
        outs.append(copy)

    for copy in second:
        copy.wait()
    for r in range(steps):
        here = slice(r * K, (r + 1) * K)
        if r == 0:
            for copy in fields[0] + fields[1] + last[:1]:
                copy.wait()
        if r == 2:
            for copy in fields[2] + fields[3]:
                copy.wait()
        d = dep[here, :]
        high, low = halves(planes[1, here, :])
        flux_x = mm3(
            (mx[0, here, :], mx[1, here, :]),
            (jnp.concatenate([high, txs[0]], axis=0), jnp.concatenate([low, txs[1]], axis=0)),
            NN,
        )
        if r % 2 == 0:
            pair = slice(r * K, (r + 2) * K)
            pieces = []
            for c in range(cols // K):
                block = slice(c * K, (c + 1) * K)
                high, low = halves(planes[2, pair, block])
                lhs = (
                    jnp.concatenate([high, tyt[0][pair, :]], axis=1),
                    jnp.concatenate([low, tyt[1][pair, :]], axis=1),
                )
                pieces.append(mm3(lhs, (my[0, :, block], my[1, :, block]), NN))
        flux_y = jnp.concatenate([piece[(r % 2) * K : (r % 2 + 1) * K] for piece in pieces], axis=1)
        weighted_x = d * flux_x
        weighted_y = d * flux_y
        before_x = jnp.where(row == 0, carry, pltpu.roll(weighted_x, 1, 0))
        carry = weighted_x[K - 1 : K, :]
        turned = [side[here, 0:1]] + [
            pltpu.roll(weighted_y[:, c * K : (c + 1) * K], 1, 1) for c in range(cols // K)
        ]
        before_y = jnp.concatenate(
            [jnp.where(lane == 0, turned[c], turned[c + 1]) for c in range(cols // K)], axis=1
        )
        e = planes[0, here, :] + courant * ((weighted_x - before_x) + (weighted_y - before_y))
        elev[here, :] = e
        send(0, elev, r)
        right = [pltpu.roll(e[:, c * K : (c + 1) * K], K - 1, 1) for c in range(cols // K)] + [0.0]
        right = jnp.concatenate(
            [jnp.where(lane == K - 1, right[c + 1], right[c]) for c in range(cols // K)], axis=1
        )
        fy[here, :] = flux_y + courant * (right - e)
        send(2, fy, r)
        fx[here, :] = flux_x + courant * (jnp.where(row == K - 1, 0.0, pltpu.roll(e, K - 1, 0)) - e)
        if r > 0:
            end = slice(r * K - 8, r * K)
            fx[end, :] = fx[end, :] + jnp.where(row[:8] == 7, courant * e[0:1, :], 0.0)
            send(1, fx, r - 1)
        if r == 0:
            erow[...] = e[0:1, :]
            outs.append(pltpu.make_async_copy(erow, erow_out, sems.at[11]))
            outs[-1].start()
        ecol[:, here] = e[:, :K].T[0:1, :]
        for a in range(per):
            for w in range(cols // tile_w):
                tile = e[a * tile_h : (a + 1) * tile_h, w * tile_w : (w + 1) * tile_w]
                for b in range(modes):
                    at = b * (rows // tile_h) + r * per + a
                    mom[at : at + 1, w * tile_w : (w + 1) * tile_w] = jnp.sum(
                        tile * basis[b], axis=0, keepdims=True
                    )
    send(1, fx, steps - 1)
    outs.append(pltpu.make_async_copy(ecol, ecol_out, sems.at[12]))
    outs[-1].start()
    for copy in last[1:]:
        copy.wait()
    tiles_y, tiles_x = wet.shape
    ones = jnp.ones((8, tile_w), bf16)
    pieces = []
    for w in range(tiles_y):
        high, low = halves(mom[:, w * tile_w : (w + 1) * tile_w])
        line = (mm(ones, high, NT) + mm(ones, low, NT))[0:1, :]
        keep = wet[w : w + 1, :].astype(f32)
        for b in range(modes):
            pieces.append(line[:, b * tiles_x : (b + 1) * tiles_x] * keep)
    high, low = halves(jnp.concatenate(pieces, axis=0))
    table = jnp.concatenate([high, low], axis=0)
    lines = tiles_y * modes
    acc = jnp.zeros((lines, count), f32)
    for step in range(2):
        both = mm(table, at_row[step], NN)
        acc = acc + (both[:lines] + both[lines:]) * share[step]
    total = jnp.sum(acc, axis=0, keepdims=True)
    placed = jnp.concatenate(halves(jnp.where(slot_of, total, 0.0)), axis=0)
    both = mm(device_of, placed, NT)
    sums = both[:, :slots] + both[:, slots:]
    parts[...] = jnp.concatenate([sums, jnp.zeros((devices, K - slots), f32)], axis=1)
    outs.append(pltpu.make_async_copy(parts, parts_out, sems.at[10]))
    outs[-1].start()
    for copy in outs:
        copy.wait()


def elevation(tx, near, carried, adj, depth, basis, wet, owner):
    rows, cols = depth.shape
    modes, tile_h, tile_w = basis.shape
    devices = lax.axis_size("gx") * lax.axis_size("gy")
    steps = rows // K
    wet = wet.T
    owner = owner.reshape(1, -1)
    field = ((rows, cols), f32)
    far = (len(near), *near[0].shape)
    parts = ((devices, K), f32)
    halos = [((1, cols), f32), ((1, rows), f32)]
    like = lambda *arrays: [pltpu.VMEM(a.shape, a.dtype) for a in arrays]
    return pl.pallas_call(
        elev_kernel,
        out_shape=(pltpu.HBM((3, rows, cols), f32), pltpu.HBM(*parts), *(pltpu.HBM(*h) for h in halos)),
        in_specs=[vmem_spec()] + [pl.BlockSpec(memory_space=pl.ANY)] * 4 + [hbm_spec()] * 10,
        out_specs=(hbm_spec(),) * 4,
        scratch_shapes=[pltpu.VMEM(far, f32)]
        + like(*carried)
        + [pltpu.VMEM((3, rows, cols), f32), pltpu.VMEM(*field)]
        + like(basis, wet, owner)
        + [pltpu.VMEM(*field)] * 3
        + [
            pltpu.VMEM((far[0] * far[1] * 8, far[3]), f32),
            pltpu.VMEM((rows // tile_h * modes, cols), f32),
            pltpu.VMEM(*parts),
            *(pltpu.VMEM(*h) for h in halos),
            pltpu.SemaphoreType.DMA((17,)),
            pltpu.SemaphoreType.DMA((steps, 2)),
            pltpu.SemaphoreType.DMA((steps, 3)),
        ],
        compiler_params=pltpu.CompilerParams(vmem_limit_bytes=32 << 20),
        cost_estimate=cost(12 * rows * cols * K, 10 << 20),
        name="elevation",
    )(tx, *near, *in_hbm(*carried, adj, depth, basis, wet, owner))


def finish_kernel(fields_in, sums, hrow, hcol, bottom_in, edge_in, fields, grad, bottom, edge, out_sems):
    u = lax.axis_index("gx")
    v = lax.axis_index("gy")
    size_x = lax.axis_size("gx")
    size_y = lax.axis_size("gy")
    rows, cols = fields.shape[1:]

    below = hrow[...] * jnp.where(u + 1 < size_x, courant, 0.0)
    right = hcol[...] * jnp.where(v + 1 < size_y, courant, 0.0)
    right = jnp.broadcast_to(right, (8, rows)).T[:, 0:1]
    edge[...] = edge_in[...] + jnp.where(iota((rows, K), 1) == K - 1, right, 0.0)
    bottom[...] = bottom_in[...] + jnp.where(iota((8, cols), 0) == 7, below, 0.0)
    writes = [
        pltpu.make_async_copy(edge, fields.at[2, :, pl.ds(cols - K, K)], out_sems.at[0]),
        pltpu.make_async_copy(bottom, fields.at[1, pl.ds(rows - 8, 8), :], out_sems.at[1]),
    ]
    for copy in writes:
        copy.start()
    total = jnp.sum(sums[...], axis=0, keepdims=True)
    grad[...] = total[:, : grad.shape[1]]
    for copy in writes:
        copy.wait()


def finish(fields, sums, hrow, hcol, slots):
    _, rows, cols = fields.shape
    bottom = fields[1, rows - 8 :, :]
    edge = fields[2, :, cols - K :]
    return pl.pallas_call(
        finish_kernel,
        out_shape=(pltpu.HBM(fields.shape, f32), jax.ShapeDtypeStruct((1, slots), f32)),
        in_specs=[hbm_spec()] + [vmem_spec()] * 5,
        out_specs=(hbm_spec(), vmem_spec()),
        input_output_aliases={0: 0},
        scratch_shapes=[
            pltpu.VMEM((8, cols), f32),
            pltpu.VMEM((rows, K), f32),
            pltpu.SemaphoreType.DMA((2,)),
        ],
        compiler_params=pltpu.CompilerParams(vmem_limit_bytes=16 << 20),
        cost_estimate=cost(1 << 20, 1 << 20),
        name="finish",
    )(*in_hbm(fields), sums, hrow, hcol, bottom, edge)


def partner(axis, bit):
    return [(i, i ^ bit) for i in range(lax.axis_size(axis))]


def previous(axis):
    size = lax.axis_size(axis)
    return [(i, (i - 1) % size) for i in range(size)]


def body(
    adj_fields, depth, block_x, reduced_x, block_y, reduced_y, basis, coef, footprint, owner, wet
):
    size_x = lax.axis_size("gx")
    size_y = lax.axis_size("gy")
    px, py = ends(adj_fields, depth, block_x, block_y, size_x, size_y)
    tx = lax.all_to_all(px, "gx", split_axis=0, concat_axis=0, tiled=True)
    carried = carry(block_x, block_y, reduced_x, reduced_y, coef, footprint, wet)
    ty = py[None]
    ty = jnp.concatenate([ty, lax.ppermute(ty, "gy", partner("gy", size_y // 2))], axis=0)
    near = [ty] + [lax.ppermute(ty, "gy", partner("gy", bits)) for bits in range(1, size_y // 2)]
    fields, parts, erow, ecol = elevation(tx, near, carried, adj_fields, depth, basis, wet, owner)
    devices = size_x * size_y
    hrow = lax.ppermute(erow, "gx", previous("gx"))
    hcol = lax.ppermute(ecol, "gy", previous("gy"))
    sums = lax.all_to_all(
        parts[:, None, :], ("gx", "gy"), split_axis=0, concat_axis=0, tiled=True
    )
    slots = owner.shape[0] // devices
    adj_before, grad = finish(fields, sums[:, 0, :], hrow, hcol, slots)
    return adj_before, grad.reshape(slots)


def solution(mesh):
    in_specs = (
        P(None, "gx", "gy"),
        P("gx", "gy"),
        P(),
        P(),
        P(),
        P(),
        P(),
        P(),
        P(),
        P(),
        P("gx", "gy"),
    )
    out_specs = (P(None, "gx", "gy"), P(("gx", "gy")))
    return jax.shard_map(body, mesh=mesh, in_specs=in_specs, out_specs=out_specs, check_vma=False)
```

```python
import jax
import jax.numpy as jnp
from jax import lax
from jax.experimental import pallas as pl
from jax.experimental.pallas import tpu as pltpu
from jax.sharding import PartitionSpec as P

courant = 0.5
f32 = jnp.float32
bf16 = jnp.bfloat16
K = 128
EXTRA = 128

NN = (((1,), (0,)), ((), ()))
NT = (((1,), (1,)), ((), ()))
TN = (((0,), (0,)), ((), ()))


def halves(x):
    high = x.astype(bf16)
    return high, (x - high.astype(f32)).astype(bf16)


def mm(a, b, dims):
    return lax.dot_general(a, b, dims, preferred_element_type=f32)


def mm3(a, b, dims):
    ah, al = a
    bh, bl = b
    return mm(ah, bh, dims) + (mm(ah, bl, dims) + mm(al, bh, dims))


def exact(a, b, dims):
    return lax.dot_general(a, b, dims, precision=lax.Precision.HIGHEST, preferred_element_type=f32)


def iota(shape, dim):
    return lax.broadcasted_iota(jnp.int32, shape, dim)


def hbm_spec():
    return pl.BlockSpec(memory_space=pltpu.HBM)


def vmem_spec():
    return pl.BlockSpec(memory_space=pltpu.VMEM)


def in_hbm(*arrays):
    return tuple(pltpu.with_memory_space_constraint(a, pltpu.HBM) for a in arrays)


def in_vmem(*arrays):
    return tuple(pltpu.with_memory_space_constraint(a, pltpu.VMEM) for a in arrays)


def cost(flops, nbytes):
    return pl.CostEstimate(flops=flops, bytes_accessed=nbytes, transcendentals=0)


def stacked(first, last, c):
    high, low = halves(jnp.concatenate([first[c, 0:1, :], last[c, 7:8, :]], axis=0))
    return jnp.concatenate([high, low], axis=0)


def two_rows(weights, field, dims):
    high, low = halves(field)
    both = mm(weights, high, dims)
    return both[0:2] + both[2:4] + mm(weights[0:2], low, dims)


def block_ends(blocks, index, first, last, sems):
    here = pl.ds(index * first.shape[0], first.shape[0])
    return [
        pltpu.make_async_copy(blocks.at[here, pl.ds(0, 8), :], first, sems.at[0]),
        pltpu.make_async_copy(blocks.at[here, pl.ds(K - 8, 8), :], last, sems.at[1]),
    ]


def ends_kernel(
    adj, depth, block_x, block_y, px_hbm, py,
    vx, vy, first_x, last_x, first_y, last_y, drow, dcol, px, sems, out_sems,
):
    rows, cols = vx.shape
    nbx = first_x.shape[0]
    nby = first_y.shape[0]
    small = block_ends(block_x, lax.axis_index("gx"), first_x, last_x, sems)
    small += block_ends(block_y, lax.axis_index("gy"), first_y, last_y, sems.at[pl.ds(2, 2)])
    small.append(pltpu.make_async_copy(depth.at[pl.ds(rows - 8, 8), :], drow, sems.at[4]))
    side = pltpu.make_async_copy(depth.at[:, pl.ds(cols - K, K)], dcol, sems.at[5])
    field_x = pltpu.make_async_copy(adj.at[1], vx, sems.at[6])
    field_y = pltpu.make_async_copy(adj.at[2], vy, sems.at[7])
    for copy in small + [field_x, side, field_y]:
        copy.start()
    for copy in small:
        copy.wait()
    for part in range(cols // K):
        px[part : part + 1, cols:] = drow[7:8, part * K : (part + 1) * K]
    px[cols // K :, cols:] = jnp.zeros((8 - cols // K, EXTRA), f32)
    weights_x = [stacked(first_x, last_x, c) for c in range(nbx)]
    weights_y = [stacked(first_y, last_y, c) for c in range(nby)]
    field_x.wait()
    for c in range(nbx):
        px[2 * c : 2 * c + 2, :cols] = two_rows(weights_x[c], vx[c * K : (c + 1) * K, :], NN)
    outs = [pltpu.make_async_copy(px, px_hbm.at[d], out_sems.at[d]) for d in range(px_hbm.shape[0])]
    for copy in outs:
        copy.start()
    side.wait()
    field_y.wait()
    at_last = (iota((8, K), 1) == K - 1).astype(f32).astype(bf16)
    high, low = halves(dcol[...])
    line = mm(at_last, high, NT) + mm(at_last, low, NT)
    for part in range(rows // K):
        py[part : part + 1, rows:] = line[0:1, part * K : (part + 1) * K]
    py[rows // K :, rows:] = jnp.zeros((8 - rows // K, EXTRA), f32)
    for c in range(nby):
        py[2 * c : 2 * c + 2, :rows] = two_rows(weights_y[c], vy[:, c * K : (c + 1) * K], NT)
    for copy in outs:
        copy.wait()


def ends(adj, depth, block_x, block_y, size_x, size_y):
    rows, cols = depth.shape
    nbx = block_x.shape[0] // size_x
    nby = block_y.shape[0] // size_y
    shape = (2 * nbx, cols + EXTRA)
    return pl.pallas_call(
        ends_kernel,
        out_shape=(
            pltpu.HBM((size_x, *shape), f32),
            jax.ShapeDtypeStruct((2 * nby, rows + EXTRA), f32),
        ),
        in_specs=[hbm_spec()] * 4,
        out_specs=(hbm_spec(), vmem_spec()),
        scratch_shapes=[
            pltpu.VMEM((rows, cols), f32),
            pltpu.VMEM((rows, cols), f32),
            pltpu.VMEM((nbx, 8, K), f32),
            pltpu.VMEM((nbx, 8, K), f32),
            pltpu.VMEM((nby, 8, K), f32),
            pltpu.VMEM((nby, 8, K), f32),
            pltpu.VMEM((8, cols), f32),
            pltpu.VMEM((rows, K), f32),
            pltpu.VMEM(shape, f32),
            pltpu.SemaphoreType.DMA((8,)),
            pltpu.SemaphoreType.DMA((size_x,)),
        ],
        compiler_params=pltpu.CompilerParams(vmem_limit_bytes=16 << 20),
        cost_estimate=cost(2 * rows * cols * 32, 3 << 20),
        name="ends",
    )(*in_hbm(adj, depth, block_x, block_y))


def carry_kernel(
    block_x, block_y, reduced_x_hbm, reduced_y_hbm, coef_hbm, footprint_hbm,
    mx_hbm, my_hbm, gside_hbm, share_hbm, at_row_hbm,
    mx, my, gside, share, at_row, wx, wy, wpx, wpy, reduced_x, reduced_y, coef, footprint, sems, out_sems,
):
    u = lax.axis_index("gx")
    v = lax.axis_index("gy")
    nbx = wx.shape[0]
    nby = wy.shape[0]
    before_x = jnp.maximum(u * nbx - 1, 0)
    before_y = jnp.maximum(v * nby - 1, 0)
    copies = [
        pltpu.make_async_copy(footprint_hbm, footprint, sems.at[0]),
        pltpu.make_async_copy(coef_hbm, coef, sems.at[1]),
        pltpu.make_async_copy(reduced_x_hbm, reduced_x, sems.at[2]),
        pltpu.make_async_copy(block_x.at[pl.ds(u * nbx, nbx)], wx, sems.at[3]),
        pltpu.make_async_copy(reduced_y_hbm, reduced_y, sems.at[4]),
        pltpu.make_async_copy(block_y.at[pl.ds(v * nby, nby)], wy, sems.at[5]),
        pltpu.make_async_copy(block_x.at[before_x, pl.ds(K - 8, 8), :], wpx, sems.at[6]),
        pltpu.make_async_copy(block_y.at[before_y, pl.ds(K - 8, 8), :], wpy, sems.at[7]),
    ]
    for copy in copies:
        copy.start()
    outs = [
        pltpu.make_async_copy(share, share_hbm, out_sems.at[0]),
        pltpu.make_async_copy(at_row, at_row_hbm, out_sems.at[1]),
        pltpu.make_async_copy(mx, mx_hbm, out_sems.at[2]),
        pltpu.make_async_copy(my, my_hbm, out_sems.at[3]),
        pltpu.make_async_copy(gside, gside_hbm, out_sems.at[4]),
    ]
    for copy in copies[:2]:
        copy.wait()
    places, modes, count = coef.shape
    tiles_y = share.shape[1] // modes
    tiles_x = at_row.shape[1]
    total_cols = tiles_y * lax.axis_size("gy")
    number = footprint[...]
    row = lax.shift_right_logical(number, total_cols.bit_length() - 1)
    col = (number & (total_cols - 1)) - v * tiles_y
    top = jnp.min(row, axis=0, keepdims=True)
    tile_row = iota((tiles_x, count), 0)
    tile_col = lax.shift_right_logical(iota((tiles_y * modes, count), 0), modes.bit_length() - 1)
    for step in range(2):
        at_row[step] = (tile_row == top + step - u * tiles_x).astype(f32).astype(bf16)
        index = jnp.where(row == top + step, col, -1)
        acc = jnp.zeros((tiles_y * modes, count), f32)
        for f in range(places):
            scale = jnp.concatenate([coef[f]] * tiles_y, axis=0)
            acc = acc + jnp.where(tile_col == index[f : f + 1, :], scale, 0.0)
        share[step] = acc
    for copy in outs[:2]:
        copy.start()
    for copy in copies[2:4]:
        copy.wait()
    own_x = reduced_x[pl.ds(pl.multiple_of(u * 8, 8), 8), :]
    prev_x = reduced_x[pl.ds(pl.multiple_of(jnp.maximum(u - 1, 0) * 8, 8), 8), :]
    for c in range(nbx):
        w = wx[c]
        g = w[:, 0:1] * own_x[2 * c : 2 * c + 1, :] + w[:, K - 1 : K] * own_x[2 * c + 1 : 2 * c + 2, :]
        for i, part in enumerate(zip(halves(w), halves(g))):
            mx[i, c * K : (c + 1) * K, :] = jnp.concatenate(part, axis=1)
    outs[2].start()
    for copy in copies[4:]:
        copy.wait()
    own_y = halves(reduced_y[pl.ds(pl.multiple_of(v * 8, 8), 8), :])
    prev_y = reduced_y[pl.ds(pl.multiple_of(jnp.maximum(v - 1, 0) * 8, 8), 8), :]
    sub = iota((8, K), 0)
    for c in range(nby):
        turned = wy[c].T
        across = jnp.where(sub == 2 * c, turned[0:1, :], 0.0)
        across = jnp.where(sub == 2 * c + 1, turned[K - 1 : K, :], across)
        g = mm3(own_y, halves(across), TN)
        for i, part in enumerate(zip(halves(turned), halves(g))):
            my[i, :, c * K : (c + 1) * K] = jnp.concatenate(part, axis=0)
    outs[3].start()

    def side(w, prev, index):
        width = prev.shape[1]
        g = w[7:8, 0:1] * prev[6:7, :] + w[7:8, K - 1 : K] * prev[7:8, :]
        g = g + (iota((1, width), 1) == index * 8 - 1).astype(f32)
        return jnp.where(index > 0, g, 0.0)

    gside[...] = jnp.zeros(gside.shape, f32)
    gside[0:1, :] = side(wpx[...], prev_x, u)
    gside[1:2, : reduced_y.shape[1]] = side(wpy[...], prev_y, v)
    outs[4].start()
    for copy in outs:
        copy.wait()


def carry(block_x, block_y, reduced_x, reduced_y, coef, footprint, wet):
    nbx = block_x.shape[0] // lax.axis_size("gx")
    nby = block_y.shape[0] // lax.axis_size("gy")
    coef = coef.transpose(1, 2, 0)
    footprint = footprint.T
    _, modes, count = coef.shape
    tiles_x, tiles_y = wet.shape
    results = [
        ((2, nbx * K, K + reduced_x.shape[0]), bf16),
        ((2, K + reduced_y.shape[0], nby * K), bf16),
        ((8, reduced_x.shape[0]), f32),
        ((2, tiles_y * modes, count), f32),
        ((2, tiles_x, count), bf16),
    ]
    return pl.pallas_call(
        carry_kernel,
        out_shape=tuple(pltpu.HBM(*result) for result in results),
        in_specs=[hbm_spec()] * 6,
        out_specs=(hbm_spec(),) * 5,
        scratch_shapes=[pltpu.VMEM(*result) for result in results]
        + [
            pltpu.VMEM((nbx, K, K), f32),
            pltpu.VMEM((nby, K, K), f32),
            pltpu.VMEM((8, K), f32),
            pltpu.VMEM((8, K), f32),
            pltpu.VMEM(reduced_x.shape, f32),
            pltpu.VMEM(reduced_y.shape, f32),
            pltpu.VMEM(coef.shape, f32),
            pltpu.VMEM(footprint.shape, jnp.int32),
            pltpu.SemaphoreType.DMA((8,)),
            pltpu.SemaphoreType.DMA((5,)),
        ],
        compiler_params=pltpu.CompilerParams(vmem_limit_bytes=16 << 20),
        cost_estimate=cost(1 << 36, 2 << 20),
        name="carry",
    )(*in_hbm(block_x, block_y, reduced_x, reduced_y, coef, footprint))


def elev_kernel(
    tx, t0, t1, t2, t3, mx_in, my_in, gside_in, share_in, at_row_in, adj, depth, basis_in, wet_in, owner_in,
    fields_out, parts_out, erow_out, ecol_out,
    ty, mx, my, gside, share, at_row, planes, dep, basis, wet, owner,
    elev, fx, fy, tyn, mom, parts, erow, ecol, sems, row_sems, out_sems,
):
    u = lax.axis_index("gx")
    v = lax.axis_index("gy")
    rows, cols = dep.shape
    steps = rows // K
    near = (t0, t1, t2, t3)
    first = [
        *(pltpu.make_async_copy(part, ty.at[i], sems.at[13 + i]) for i, part in enumerate(near)),
        pltpu.make_async_copy(gside_in, gside, sems.at[2]),
        pltpu.make_async_copy(owner_in, owner, sems.at[3]),
    ]
    second = [
        pltpu.make_async_copy(mx_in, mx, sems.at[4]),
        pltpu.make_async_copy(my_in, my, sems.at[5]),
    ]
    last = [
        pltpu.make_async_copy(basis_in, basis, sems.at[6]),
        pltpu.make_async_copy(wet_in, wet, sems.at[7]),
        pltpu.make_async_copy(share_in, share, sems.at[8]),
        pltpu.make_async_copy(at_row_in, at_row, sems.at[9]),
    ]
    fields = []
    for r in range(steps):
        here = pl.ds(r * K, K)
        fields.append(
            [
                pltpu.make_async_copy(adj.at[:, here, :], planes.at[:, here, :], row_sems.at[r, 0]),
                pltpu.make_async_copy(depth.at[here, :], dep.at[here, :], row_sems.at[r, 1]),
            ]
        )
    for group in [fields[0], first, second, fields[1], last[:1], fields[2], fields[3], last[1:]]:
        for copy in group:
            copy.start()
    txs = halves(jnp.concatenate([tx[d][:, :cols] for d in range(tx.shape[0])], axis=0))
    for copy in first:
        copy.wait()
    devices = parts.shape[0]
    count = owner.shape[1]
    slots = count // devices
    own = owner[...]
    device_of = iota((devices, count), 0) == lax.shift_right_logical(own, slots.bit_length() - 1)
    device_of = device_of.astype(f32).astype(bf16)
    slot_of = iota((slots, count), 0) == (own & (slots - 1))
    for j in range(ty.shape[0] * ty.shape[1]):
        far = j ^ v
        tyn[j * 8 : (j + 1) * 8, :] = ty[far & (ty.shape[0] - 1), far // ty.shape[0]]
    ty_all = tyn[:, :rows]
    tys = halves(ty_all)
    tyt = halves(ty_all.T)
    up = jnp.maximum(u - 1, 0)
    left = jnp.maximum(v - 1, 0)
    gs = gside[...]
    edge_x = mm3(halves(gs), txs, NN)[0:1, :]
    edge_y = mm3(halves(gs[:, : ty_all.shape[0]]), tys, NN)[1:2, :]
    drow = tx[up][:, cols:]
    drow = jnp.concatenate([drow[p : p + 1, :] for p in range(cols // K)], axis=1)
    dcol = tyn[pl.ds(pl.multiple_of(left * 8, 8), 8), rows:]
    dcol = jnp.concatenate([dcol[p : p + 1, :] for p in range(rows // K)], axis=1)
    carry = edge_x * drow
    side = jnp.broadcast_to(edge_y * dcol, (8, rows)).T
    row = iota((K, cols), 0)
    lane = iota((K, K), 1)
    modes, tile_h, tile_w = basis.shape
    per = K // tile_h
    outs = []

    def send(plane, source, r):
        here = pl.ds(r * K, K)
        copy = pltpu.make_async_copy(
            source.at[here, :], fields_out.at[plane, here, :], out_sems.at[r, plane]
        )
        copy.start()
        outs.append(copy)

    for copy in second:
        copy.wait()
    for r in range(steps):
        here = slice(r * K, (r + 1) * K)
        if r == 0:
            for copy in fields[0] + fields[1] + last[:1]:
                copy.wait()
        if r == 2:
            for copy in fields[2] + fields[3]:
                copy.wait()
        d = dep[here, :]
        high, low = halves(planes[1, here, :])
        flux_x = mm3(
            (mx[0, here, :], mx[1, here, :]),
            (jnp.concatenate([high, txs[0]], axis=0), jnp.concatenate([low, txs[1]], axis=0)),
            NN,
        )
        if r % 2 == 0:
            pair = slice(r * K, (r + 2) * K)
            pieces = []
            for c in range(cols // K):
                block = slice(c * K, (c + 1) * K)
                high, low = halves(planes[2, pair, block])
                lhs = (
                    jnp.concatenate([high, tyt[0][pair, :]], axis=1),
                    jnp.concatenate([low, tyt[1][pair, :]], axis=1),
                )
                pieces.append(mm3(lhs, (my[0, :, block], my[1, :, block]), NN))
        flux_y = jnp.concatenate([piece[(r % 2) * K : (r % 2 + 1) * K] for piece in pieces], axis=1)
        weighted_x = d * flux_x
        weighted_y = d * flux_y
        before_x = jnp.where(row == 0, carry, pltpu.roll(weighted_x, 1, 0))
        carry = weighted_x[K - 1 : K, :]
        turned = [side[here, 0:1]] + [
            pltpu.roll(weighted_y[:, c * K : (c + 1) * K], 1, 1) for c in range(cols // K)
        ]
        before_y = jnp.concatenate(
            [jnp.where(lane == 0, turned[c], turned[c + 1]) for c in range(cols // K)], axis=1
        )
        e = planes[0, here, :] + courant * ((weighted_x - before_x) + (weighted_y - before_y))
        elev[here, :] = e
        send(0, elev, r)
        right = [pltpu.roll(e[:, c * K : (c + 1) * K], K - 1, 1) for c in range(cols // K)] + [0.0]
        right = jnp.concatenate(
            [jnp.where(lane == K - 1, right[c + 1], right[c]) for c in range(cols // K)], axis=1
        )
        fy[here, :] = flux_y + courant * (right - e)
        send(2, fy, r)
        fx[here, :] = flux_x + courant * (jnp.where(row == K - 1, 0.0, pltpu.roll(e, K - 1, 0)) - e)
        if r > 0:
            end = slice(r * K - 8, r * K)
            fx[end, :] = fx[end, :] + jnp.where(row[:8] == 7, courant * e[0:1, :], 0.0)
            send(1, fx, r - 1)
        if r == 0:
            erow[...] = e[0:1, :]
            outs.append(pltpu.make_async_copy(erow, erow_out, sems.at[11]))
            outs[-1].start()
        ecol[:, here] = e[:, :K].T[0:1, :]
        for a in range(per):
            for w in range(cols // tile_w):
                tile = e[a * tile_h : (a + 1) * tile_h, w * tile_w : (w + 1) * tile_w]
                for b in range(modes):
                    at = b * (rows // tile_h) + r * per + a
                    mom[at : at + 1, w * tile_w : (w + 1) * tile_w] = jnp.sum(
                        tile * basis[b], axis=0, keepdims=True
                    )
    send(1, fx, steps - 1)
    outs.append(pltpu.make_async_copy(ecol, ecol_out, sems.at[12]))
    outs[-1].start()
    for copy in last[1:]:
        copy.wait()
    tiles_y, tiles_x = wet.shape
    ones = jnp.ones((8, tile_w), bf16)
    pieces = []
    for w in range(tiles_y):
        high, low = halves(mom[:, w * tile_w : (w + 1) * tile_w])
        line = (mm(ones, high, NT) + mm(ones, low, NT))[0:1, :]
        keep = wet[w : w + 1, :].astype(f32)
        for b in range(modes):
            pieces.append(line[:, b * tiles_x : (b + 1) * tiles_x] * keep)
    high, low = halves(jnp.concatenate(pieces, axis=0))
    table = jnp.concatenate([high, low], axis=0)
    lines = tiles_y * modes
    acc = jnp.zeros((lines, count), f32)
    for step in range(2):
        both = mm(table, at_row[step], NN)
        acc = acc + (both[:lines] + both[lines:]) * share[step]
    total = jnp.sum(acc, axis=0, keepdims=True)
    placed = jnp.concatenate(halves(jnp.where(slot_of, total, 0.0)), axis=0)
    both = mm(device_of, placed, NT)
    sums = both[:, :slots] + both[:, slots:]
    parts[...] = jnp.concatenate([sums, jnp.zeros((devices, K - slots), f32)], axis=1)
    outs.append(pltpu.make_async_copy(parts, parts_out, sems.at[10]))
    outs[-1].start()
    for copy in outs:
        copy.wait()


def elevation(tx, near, carried, adj, depth, basis, wet, owner):
    rows, cols = depth.shape
    modes, tile_h, tile_w = basis.shape
    devices = lax.axis_size("gx") * lax.axis_size("gy")
    steps = rows // K
    wet = wet.T
    owner = owner.reshape(1, -1)
    field = ((rows, cols), f32)
    far = (len(near), *near[0].shape)
    parts = ((devices, K), f32)
    halos = [((1, cols), f32), ((1, rows), f32)]
    like = lambda *arrays: [pltpu.VMEM(a.shape, a.dtype) for a in arrays]
    return pl.pallas_call(
        elev_kernel,
        out_shape=(pltpu.HBM((3, rows, cols), f32), pltpu.HBM(*parts), *(pltpu.HBM(*h) for h in halos)),
        in_specs=[vmem_spec()] + [pl.BlockSpec(memory_space=pl.ANY)] * 4 + [hbm_spec()] * 10,
        out_specs=(hbm_spec(),) * 4,
        scratch_shapes=[pltpu.VMEM(far, f32)]
        + like(*carried)
        + [pltpu.VMEM((3, rows, cols), f32), pltpu.VMEM(*field)]
        + like(basis, wet, owner)
        + [pltpu.VMEM(*field)] * 3
        + [
            pltpu.VMEM((far[0] * far[1] * 8, far[3]), f32),
            pltpu.VMEM((rows // tile_h * modes, cols), f32),
            pltpu.VMEM(*parts),
            *(pltpu.VMEM(*h) for h in halos),
            pltpu.SemaphoreType.DMA((17,)),
            pltpu.SemaphoreType.DMA((steps, 2)),
            pltpu.SemaphoreType.DMA((steps, 3)),
        ],
        compiler_params=pltpu.CompilerParams(vmem_limit_bytes=32 << 20),
        cost_estimate=cost(12 * rows * cols * K, 10 << 20),
        name="elevation",
    )(tx, *near, *in_hbm(*carried, adj, depth, basis, wet, owner))


def finish_kernel(
    fields_in, sums, hrow, hcol, bottom_in, edge_in, fields, grad_out, bottom, edge, grad, out_sems
):
    u = lax.axis_index("gx")
    v = lax.axis_index("gy")
    size_x = lax.axis_size("gx")
    size_y = lax.axis_size("gy")
    rows, cols = fields.shape[1:]

    right = hcol[...] * jnp.where(v + 1 < size_y, courant, 0.0)
    right = jnp.broadcast_to(right, (8, rows)).T[:, 0:1]
    edge[...] = edge_in[...] + jnp.where(iota((rows, K), 1) == K - 1, right, 0.0)
    below = hrow[...] * jnp.where(u + 1 < size_x, courant, 0.0)
    bottom[...] = bottom_in[...] + jnp.where(iota((8, cols), 0) == 7, below, 0.0)
    total = jnp.sum(sums[...], axis=0, keepdims=True)
    grad[...] = total[:, : grad.shape[1]]
    writes = [
        pltpu.make_async_copy(edge, fields.at[2, :, pl.ds(cols - K, K)], out_sems.at[0]),
        pltpu.make_async_copy(bottom, fields.at[1, pl.ds(rows - 8, 8), :], out_sems.at[1]),
        pltpu.make_async_copy(grad, grad_out, out_sems.at[2]),
    ]
    for copy in writes:
        copy.start()
    for copy in writes:
        copy.wait()


def finish(fields, sums, hrow, hcol, slots):
    _, rows, cols = fields.shape
    bottom = fields[1, rows - 8 :, :]
    edge = fields[2, :, cols - K :]
    return pl.pallas_call(
        finish_kernel,
        out_shape=(pltpu.HBM(fields.shape, f32), pltpu.HBM((1, slots), f32)),
        in_specs=[hbm_spec()] + [vmem_spec()] * 5,
        out_specs=(hbm_spec(), hbm_spec()),
        input_output_aliases={0: 0},
        scratch_shapes=[
            pltpu.VMEM((8, cols), f32),
            pltpu.VMEM((rows, K), f32),
            pltpu.VMEM((1, slots), f32),
            pltpu.SemaphoreType.DMA((3,)),
        ],
        compiler_params=pltpu.CompilerParams(vmem_limit_bytes=16 << 20),
        cost_estimate=cost(1 << 20, 1 << 20),
        name="finish",
    )(*in_hbm(fields), sums, hrow, hcol, bottom, edge)


def partner(axis, bit):
    return [(i, i ^ bit) for i in range(lax.axis_size(axis))]


def previous(axis):
    size = lax.axis_size(axis)
    return [(i, (i - 1) % size) for i in range(size)]


def body(
    adj_fields, depth, block_x, reduced_x, block_y, reduced_y, basis, coef, footprint, owner, wet
):
    size_x = lax.axis_size("gx")
    size_y = lax.axis_size("gy")
    px, py = ends(adj_fields, depth, block_x, block_y, size_x, size_y)
    tx = lax.all_to_all(px, "gx", split_axis=0, concat_axis=0, tiled=True)
    carried = carry(block_x, block_y, reduced_x, reduced_y, coef, footprint, wet)
    ty = py[None]
    ty = jnp.concatenate([ty, lax.ppermute(ty, "gy", partner("gy", size_y // 2))], axis=0)
    near = [ty] + [lax.ppermute(ty, "gy", partner("gy", bits)) for bits in range(1, size_y // 2)]
    fields, parts, erow, ecol = elevation(tx, near, carried, adj_fields, depth, basis, wet, owner)
    devices = size_x * size_y
    hrow = lax.ppermute(erow, "gx", previous("gx"))
    hcol = lax.ppermute(ecol, "gy", previous("gy"))
    sums = lax.all_to_all(
        parts[:, None, :], ("gx", "gy"), split_axis=0, concat_axis=0, tiled=True
    )
    slots = owner.shape[0] // devices
    adj_before, grad = finish(fields, sums[:, 0, :], hrow, hcol, slots)
    return adj_before, grad.reshape(slots)


def solution(mesh):
    in_specs = (
        P(None, "gx", "gy"),
        P("gx", "gy"),
        P(),
        P(),
        P(),
        P(),
        P(),
        P(),
        P(),
        P(),
        P("gx", "gy"),
    )
    out_specs = (P(None, "gx", "gy"), P(("gx", "gy")))
    return jax.shard_map(body, mesh=mesh, in_specs=in_specs, out_specs=out_specs, check_vma=False)
```

```python
import jax
import jax.numpy as jnp
from jax import lax
from jax.experimental import pallas as pl
from jax.experimental.pallas import tpu as pltpu
from jax.sharding import PartitionSpec as P

courant = 0.5
f32 = jnp.float32
bf16 = jnp.bfloat16
K = 128
EXTRA = 128

NN = (((1,), (0,)), ((), ()))
NT = (((1,), (1,)), ((), ()))
TN = (((0,), (0,)), ((), ()))


def halves(x):
    high = x.astype(bf16)
    return high, (x - high.astype(f32)).astype(bf16)


def mm(a, b, dims):
    return lax.dot_general(a, b, dims, preferred_element_type=f32)


def mm3(a, b, dims):
    ah, al = a
    bh, bl = b
    return mm(ah, bh, dims) + (mm(ah, bl, dims) + mm(al, bh, dims))


def exact(a, b, dims):
    return lax.dot_general(a, b, dims, precision=lax.Precision.HIGHEST, preferred_element_type=f32)


def iota(shape, dim):
    return lax.broadcasted_iota(jnp.int32, shape, dim)


def hbm_spec():
    return pl.BlockSpec(memory_space=pltpu.HBM)


def vmem_spec():
    return pl.BlockSpec(memory_space=pltpu.VMEM)


def in_hbm(*arrays):
    return tuple(pltpu.with_memory_space_constraint(a, pltpu.HBM) for a in arrays)


def in_vmem(*arrays):
    return tuple(pltpu.with_memory_space_constraint(a, pltpu.VMEM) for a in arrays)


def cost(flops, nbytes):
    return pl.CostEstimate(flops=flops, bytes_accessed=nbytes, transcendentals=0)


def stacked(first, last, c):
    high, low = halves(jnp.concatenate([first[c, 0:1, :], last[c, 7:8, :]], axis=0))
    return jnp.concatenate([high, low], axis=0)


def two_rows(weights, field, dims):
    high, low = halves(field)
    both = mm(weights, high, dims)
    return both[0:2] + both[2:4] + mm(weights[0:2], low, dims)


def block_ends(blocks, index, first, last, sems):
    here = pl.ds(index * first.shape[0], first.shape[0])
    return [
        pltpu.make_async_copy(blocks.at[here, pl.ds(0, 8), :], first, sems.at[0]),
        pltpu.make_async_copy(blocks.at[here, pl.ds(K - 8, 8), :], last, sems.at[1]),
    ]


def ends_kernel(
    adj, depth, block_x, block_y, px_hbm, py,
    vx, vy, first_x, last_x, first_y, last_y, drow, dcol, px, sems, out_sems,
):
    rows, cols = vx.shape
    nbx = first_x.shape[0]
    nby = first_y.shape[0]
    small = block_ends(block_x, lax.axis_index("gx"), first_x, last_x, sems)
    small += block_ends(block_y, lax.axis_index("gy"), first_y, last_y, sems.at[pl.ds(2, 2)])
    small.append(pltpu.make_async_copy(depth.at[pl.ds(rows - 8, 8), :], drow, sems.at[4]))
    side = pltpu.make_async_copy(depth.at[:, pl.ds(cols - K, K)], dcol, sems.at[5])
    field_x = pltpu.make_async_copy(adj.at[1], vx, sems.at[6])
    field_y = pltpu.make_async_copy(adj.at[2], vy, sems.at[7])
    for copy in small + [field_x, side, field_y]:
        copy.start()
    for copy in small:
        copy.wait()
    for part in range(cols // K):
        px[part : part + 1, cols:] = drow[7:8, part * K : (part + 1) * K]
    px[cols // K :, cols:] = jnp.zeros((8 - cols // K, EXTRA), f32)
    weights_x = [stacked(first_x, last_x, c) for c in range(nbx)]
    weights_y = [stacked(first_y, last_y, c) for c in range(nby)]
    field_x.wait()
    for c in range(nbx):
        px[2 * c : 2 * c + 2, :cols] = two_rows(weights_x[c], vx[c * K : (c + 1) * K, :], NN)
    outs = [pltpu.make_async_copy(px, px_hbm.at[d], out_sems.at[d]) for d in range(px_hbm.shape[0])]
    for copy in outs:
        copy.start()
    side.wait()
    field_y.wait()
    at_last = (iota((8, K), 1) == K - 1).astype(f32).astype(bf16)
    high, low = halves(dcol[...])
    line = mm(at_last, high, NT) + mm(at_last, low, NT)
    for part in range(rows // K):
        py[part : part + 1, rows:] = line[0:1, part * K : (part + 1) * K]
    py[rows // K :, rows:] = jnp.zeros((8 - rows // K, EXTRA), f32)
    for c in range(nby):
        py[2 * c : 2 * c + 2, :rows] = two_rows(weights_y[c], vy[:, c * K : (c + 1) * K], NT)
    for copy in outs:
        copy.wait()


def ends(adj, depth, block_x, block_y, size_x, size_y):
    rows, cols = depth.shape
    nbx = block_x.shape[0] // size_x
    nby = block_y.shape[0] // size_y
    shape = (2 * nbx, cols + EXTRA)
    return pl.pallas_call(
        ends_kernel,
        out_shape=(
            pltpu.HBM((size_x, *shape), f32),
            jax.ShapeDtypeStruct((2 * nby, rows + EXTRA), f32),
        ),
        in_specs=[hbm_spec()] * 4,
        out_specs=(hbm_spec(), vmem_spec()),
        scratch_shapes=[
            pltpu.VMEM((rows, cols), f32),
            pltpu.VMEM((rows, cols), f32),
            pltpu.VMEM((nbx, 8, K), f32),
            pltpu.VMEM((nbx, 8, K), f32),
            pltpu.VMEM((nby, 8, K), f32),
            pltpu.VMEM((nby, 8, K), f32),
            pltpu.VMEM((8, cols), f32),
            pltpu.VMEM((rows, K), f32),
            pltpu.VMEM(shape, f32),
            pltpu.SemaphoreType.DMA((8,)),
            pltpu.SemaphoreType.DMA((size_x,)),
        ],
        compiler_params=pltpu.CompilerParams(vmem_limit_bytes=16 << 20),
        cost_estimate=cost(2 * rows * cols * 32, 3 << 20),
        name="ends",
    )(*in_hbm(adj, depth, block_x, block_y))


def carry_kernel(
    block_x, block_y, reduced_x_hbm, reduced_y_hbm, coef_hbm, footprint_hbm,
    mx_hbm, my_hbm, gside_hbm, share_hbm, at_row_hbm,
    mx, my, gside, share, at_row, wx, wy, wpx, wpy, reduced_x, reduced_y, coef, footprint, sems, out_sems,
):
    u = lax.axis_index("gx")
    v = lax.axis_index("gy")
    nbx = wx.shape[0]
    nby = wy.shape[0]
    before_x = jnp.maximum(u * nbx - 1, 0)
    before_y = jnp.maximum(v * nby - 1, 0)
    copies = [
        pltpu.make_async_copy(footprint_hbm, footprint, sems.at[0]),
        pltpu.make_async_copy(coef_hbm, coef, sems.at[1]),
        pltpu.make_async_copy(reduced_x_hbm, reduced_x, sems.at[2]),
        pltpu.make_async_copy(block_x.at[pl.ds(u * nbx, nbx)], wx, sems.at[3]),
        pltpu.make_async_copy(reduced_y_hbm, reduced_y, sems.at[4]),
        pltpu.make_async_copy(block_y.at[pl.ds(v * nby, nby)], wy, sems.at[5]),
        pltpu.make_async_copy(block_x.at[before_x, pl.ds(K - 8, 8), :], wpx, sems.at[6]),
        pltpu.make_async_copy(block_y.at[before_y, pl.ds(K - 8, 8), :], wpy, sems.at[7]),
    ]
    for copy in copies:
        copy.start()
    outs = [
        pltpu.make_async_copy(share, share_hbm, out_sems.at[0]),
        pltpu.make_async_copy(at_row, at_row_hbm, out_sems.at[1]),
        pltpu.make_async_copy(mx, mx_hbm, out_sems.at[2]),
        pltpu.make_async_copy(my, my_hbm, out_sems.at[3]),
        pltpu.make_async_copy(gside, gside_hbm, out_sems.at[4]),
    ]
    for copy in copies[:2]:
        copy.wait()
    places, modes, count = coef.shape
    tiles_y = share.shape[1] // modes
    tiles_x = at_row.shape[1]
    total_cols = tiles_y * lax.axis_size("gy")
    number = footprint[...]
    row = lax.shift_right_logical(number, total_cols.bit_length() - 1)
    col = (number & (total_cols - 1)) - v * tiles_y
    top = jnp.min(row, axis=0, keepdims=True)
    tile_row = iota((tiles_x, count), 0)
    tile_col = lax.shift_right_logical(iota((tiles_y * modes, count), 0), modes.bit_length() - 1)
    for step in range(2):
        at_row[step] = (tile_row == top + step - u * tiles_x).astype(f32).astype(bf16)
        index = jnp.where(row == top + step, col, -1)
        acc = jnp.zeros((tiles_y * modes, count), f32)
        for f in range(places):
            scale = jnp.concatenate([coef[f]] * tiles_y, axis=0)
            acc = acc + jnp.where(tile_col == index[f : f + 1, :], scale, 0.0)
        share[step] = acc
    for copy in outs[:2]:
        copy.start()
    for copy in copies[2:4]:
        copy.wait()
    own_x = reduced_x[pl.ds(pl.multiple_of(u * 8, 8), 8), :]
    prev_x = reduced_x[pl.ds(pl.multiple_of(jnp.maximum(u - 1, 0) * 8, 8), 8), :]
    for c in range(nbx):
        w = wx[c]
        g = w[:, 0:1] * own_x[2 * c : 2 * c + 1, :] + w[:, K - 1 : K] * own_x[2 * c + 1 : 2 * c + 2, :]
        for i, part in enumerate(zip(halves(w), halves(g))):
            mx[i, c * K : (c + 1) * K, :] = jnp.concatenate(part, axis=1)
    outs[2].start()
    for copy in copies[4:]:
        copy.wait()
    own_y = halves(reduced_y[pl.ds(pl.multiple_of(v * 8, 8), 8), :])
    prev_y = reduced_y[pl.ds(pl.multiple_of(jnp.maximum(v - 1, 0) * 8, 8), 8), :]
    sub = iota((8, K), 0)
    for c in range(nby):
        turned = wy[c].T
        across = jnp.where(sub == 2 * c, turned[0:1, :], 0.0)
        across = jnp.where(sub == 2 * c + 1, turned[K - 1 : K, :], across)
        g = mm3(own_y, halves(across), TN)
        for i, part in enumerate(zip(halves(turned), halves(g))):
            my[i, :, c * K : (c + 1) * K] = jnp.concatenate(part, axis=0)
    outs[3].start()

    def side(w, prev, index):
        width = prev.shape[1]
        g = w[7:8, 0:1] * prev[6:7, :] + w[7:8, K - 1 : K] * prev[7:8, :]
        g = g + (iota((1, width), 1) == index * 8 - 1).astype(f32)
        return jnp.where(index > 0, g, 0.0)

    gside[...] = jnp.zeros(gside.shape, f32)
    gside[0:1, :] = side(wpx[...], prev_x, u)
    gside[1:2, : reduced_y.shape[1]] = side(wpy[...], prev_y, v)
    outs[4].start()
    for copy in outs:
        copy.wait()


def carry(block_x, block_y, reduced_x, reduced_y, coef, footprint, wet):
    nbx = block_x.shape[0] // lax.axis_size("gx")
    nby = block_y.shape[0] // lax.axis_size("gy")
    coef = coef.transpose(1, 2, 0)
    footprint = footprint.T
    _, modes, count = coef.shape
    tiles_x, tiles_y = wet.shape
    results = [
        ((2, nbx * K, K + reduced_x.shape[0]), bf16),
        ((2, K + reduced_y.shape[0], nby * K), bf16),
        ((8, reduced_x.shape[0]), f32),
        ((2, tiles_y * modes, count), f32),
        ((2, tiles_x, count), bf16),
    ]
    return pl.pallas_call(
        carry_kernel,
        out_shape=tuple(pltpu.HBM(*result) for result in results),
        in_specs=[hbm_spec()] * 6,
        out_specs=(hbm_spec(),) * 5,
        scratch_shapes=[pltpu.VMEM(*result) for result in results]
        + [
            pltpu.VMEM((nbx, K, K), f32),
            pltpu.VMEM((nby, K, K), f32),
            pltpu.VMEM((8, K), f32),
            pltpu.VMEM((8, K), f32),
            pltpu.VMEM(reduced_x.shape, f32),
            pltpu.VMEM(reduced_y.shape, f32),
            pltpu.VMEM(coef.shape, f32),
            pltpu.VMEM(footprint.shape, jnp.int32),
            pltpu.SemaphoreType.DMA((8,)),
            pltpu.SemaphoreType.DMA((5,)),
        ],
        compiler_params=pltpu.CompilerParams(vmem_limit_bytes=16 << 20),
        cost_estimate=cost(1 << 36, 2 << 20),
        name="carry",
    )(*in_hbm(block_x, block_y, reduced_x, reduced_y, coef, footprint))


def elev_kernel(
    tx, t0, t1, t2, t3, mx_in, my_in, gside_in, share_in, at_row_in, adj, depth, basis_in, wet_in, owner_in,
    fields_out, parts_out, erow_out, ecol_out,
    ty, mx, my, gside, share, at_row, planes, dep, basis, wet, owner,
    elev, fx, fy, tyn, mom, parts, erow, ecol, sems, row_sems, out_sems,
):
    u = lax.axis_index("gx")
    v = lax.axis_index("gy")
    rows, cols = dep.shape
    steps = rows // K
    near = (t0, t1, t2, t3)
    first = [
        *(pltpu.make_async_copy(part, ty.at[i], sems.at[13 + i]) for i, part in enumerate(near)),
        pltpu.make_async_copy(gside_in, gside, sems.at[2]),
        pltpu.make_async_copy(owner_in, owner, sems.at[3]),
    ]
    second = [
        pltpu.make_async_copy(mx_in, mx, sems.at[4]),
        pltpu.make_async_copy(my_in, my, sems.at[5]),
    ]
    last = [
        pltpu.make_async_copy(basis_in, basis, sems.at[6]),
        pltpu.make_async_copy(wet_in, wet, sems.at[7]),
        pltpu.make_async_copy(share_in, share, sems.at[8]),
        pltpu.make_async_copy(at_row_in, at_row, sems.at[9]),
    ]
    fields = []
    for r in range(steps // 2):
        here = pl.ds(r * 2 * K, 2 * K)
        fields.append(
            [
                pltpu.make_async_copy(adj.at[:, here, :], planes.at[:, here, :], row_sems.at[r, 0]),
                pltpu.make_async_copy(depth.at[here, :], dep.at[here, :], row_sems.at[r, 1]),
            ]
        )
    for group in [fields[0], first, second, last[:1], fields[1], last[1:]]:
        for copy in group:
            copy.start()
    txs = halves(jnp.concatenate([tx[d][:, :cols] for d in range(tx.shape[0])], axis=0))
    for copy in first:
        copy.wait()
    devices = parts.shape[0]
    count = owner.shape[1]
    slots = count // devices
    for j in range(ty.shape[0] * ty.shape[1]):
        far = j ^ v
        tyn[j * 8 : (j + 1) * 8, :] = ty[far & (ty.shape[0] - 1), far // ty.shape[0]]
    ty_all = tyn[:, :rows]
    tys = halves(ty_all)
    tyt = halves(ty_all.T)
    up = jnp.maximum(u - 1, 0)
    left = jnp.maximum(v - 1, 0)
    gs = gside[...]
    edge_x = mm3(halves(gs), txs, NN)[0:1, :]
    edge_y = mm3(halves(gs[:, : ty_all.shape[0]]), tys, NN)[1:2, :]
    drow = tx[up][:, cols:]
    drow = jnp.concatenate([drow[p : p + 1, :] for p in range(cols // K)], axis=1)
    dcol = tyn[pl.ds(pl.multiple_of(left * 8, 8), 8), rows:]
    dcol = jnp.concatenate([dcol[p : p + 1, :] for p in range(rows // K)], axis=1)
    carry = edge_x * drow
    side = jnp.broadcast_to(edge_y * dcol, (8, rows)).T
    row = iota((K, cols), 0)
    lane = iota((K, K), 1)
    modes, tile_h, tile_w = basis.shape
    per = K // tile_h
    outs = []

    def send(plane, source, r):
        here = pl.ds(r * K, K)
        copy = pltpu.make_async_copy(
            source.at[here, :], fields_out.at[plane, here, :], out_sems.at[r, plane]
        )
        copy.start()
        outs.append(copy)

    for copy in second:
        copy.wait()
    for r in range(steps):
        here = slice(r * K, (r + 1) * K)
        if r == 0:
            for copy in fields[0] + last[:1]:
                copy.wait()
        if r == 2:
            for copy in fields[1]:
                copy.wait()
        d = dep[here, :]
        high, low = halves(planes[1, here, :])
        flux_x = mm3(
            (mx[0, here, :], mx[1, here, :]),
            (jnp.concatenate([high, txs[0]], axis=0), jnp.concatenate([low, txs[1]], axis=0)),
            NN,
        )
        if r % 2 == 0:
            pair = slice(r * K, (r + 2) * K)
            pieces = []
            for c in range(cols // K):
                block = slice(c * K, (c + 1) * K)
                high, low = halves(planes[2, pair, block])
                lhs = (
                    jnp.concatenate([high, tyt[0][pair, :]], axis=1),
                    jnp.concatenate([low, tyt[1][pair, :]], axis=1),
                )
                pieces.append(mm3(lhs, (my[0, :, block], my[1, :, block]), NN))
        flux_y = jnp.concatenate([piece[(r % 2) * K : (r % 2 + 1) * K] for piece in pieces], axis=1)
        weighted_x = d * flux_x
        weighted_y = d * flux_y
        before_x = jnp.where(row == 0, carry, pltpu.roll(weighted_x, 1, 0))
        carry = weighted_x[K - 1 : K, :]
        turned = [side[here, 0:1]] + [
            pltpu.roll(weighted_y[:, c * K : (c + 1) * K], 1, 1) for c in range(cols // K)
        ]
        before_y = jnp.concatenate(
            [jnp.where(lane == 0, turned[c], turned[c + 1]) for c in range(cols // K)], axis=1
        )
        e = planes[0, here, :] + courant * ((weighted_x - before_x) + (weighted_y - before_y))
        elev[here, :] = e
        send(0, elev, r)
        right = [pltpu.roll(e[:, c * K : (c + 1) * K], K - 1, 1) for c in range(cols // K)] + [0.0]
        right = jnp.concatenate(
            [jnp.where(lane == K - 1, right[c + 1], right[c]) for c in range(cols // K)], axis=1
        )
        fy[here, :] = flux_y + courant * (right - e)
        send(2, fy, r)
        fx[here, :] = flux_x + courant * (jnp.where(row == K - 1, 0.0, pltpu.roll(e, K - 1, 0)) - e)
        if r > 0:
            end = slice(r * K - 8, r * K)
            fx[end, :] = fx[end, :] + jnp.where(row[:8] == 7, courant * e[0:1, :], 0.0)
            send(1, fx, r - 1)
        if r == 0:
            erow[...] = e[0:1, :]
            outs.append(pltpu.make_async_copy(erow, erow_out, sems.at[11]))
            outs[-1].start()
        ecol[:, here] = e[:, :K].T[0:1, :]
        for a in range(per):
            for w in range(cols // tile_w):
                tile = e[a * tile_h : (a + 1) * tile_h, w * tile_w : (w + 1) * tile_w]
                for b in range(modes):
                    at = b * (rows // tile_h) + r * per + a
                    mom[at : at + 1, w * tile_w : (w + 1) * tile_w] = jnp.sum(
                        tile * basis[b], axis=0, keepdims=True
                    )
    send(1, fx, steps - 1)
    outs.append(pltpu.make_async_copy(ecol, ecol_out, sems.at[12]))
    outs[-1].start()
    for copy in last[1:]:
        copy.wait()
    tiles_y, tiles_x = wet.shape
    ones = jnp.ones((8, tile_w), bf16)
    pieces = []
    for w in range(tiles_y):
        high, low = halves(mom[:, w * tile_w : (w + 1) * tile_w])
        line = (mm(ones, high, NT) + mm(ones, low, NT))[0:1, :]
        keep = wet[w : w + 1, :].astype(f32)
        for b in range(modes):
            pieces.append(line[:, b * tiles_x : (b + 1) * tiles_x] * keep)
    high, low = halves(jnp.concatenate(pieces, axis=0))
    table = jnp.concatenate([high, low], axis=0)
    own = owner[...]
    device_of = iota((devices, count), 0) == lax.shift_right_logical(own, slots.bit_length() - 1)
    device_of = device_of.astype(f32).astype(bf16)
    slot_of = iota((slots, count), 0) == (own & (slots - 1))
    lines = tiles_y * modes
    acc = jnp.zeros((lines, count), f32)
    for step in range(2):
        both = mm(table, at_row[step], NN)
        acc = acc + (both[:lines] + both[lines:]) * share[step]
    total = jnp.sum(acc, axis=0, keepdims=True)
    placed = jnp.concatenate(halves(jnp.where(slot_of, total, 0.0)), axis=0)
    both = mm(device_of, placed, NT)
    sums = both[:, :slots] + both[:, slots:]
    parts[...] = jnp.concatenate([sums, jnp.zeros((devices, K - slots), f32)], axis=1)
    outs.append(pltpu.make_async_copy(parts, parts_out, sems.at[10]))
    outs[-1].start()
    for copy in outs:
        copy.wait()


def elevation(tx, near, carried, adj, depth, basis, wet, owner):
    rows, cols = depth.shape
    modes, tile_h, tile_w = basis.shape
    devices = lax.axis_size("gx") * lax.axis_size("gy")
    steps = rows // K
    wet = wet.T
    owner = owner.reshape(1, -1)
    field = ((rows, cols), f32)
    far = (len(near), *near[0].shape)
    parts = ((devices, K), f32)
    halos = [((1, cols), f32), ((1, rows), f32)]
    like = lambda *arrays: [pltpu.VMEM(a.shape, a.dtype) for a in arrays]
    return pl.pallas_call(
        elev_kernel,
        out_shape=(pltpu.HBM((3, rows, cols), f32), pltpu.HBM(*parts), *(pltpu.HBM(*h) for h in halos)),
        in_specs=[vmem_spec()] + [pl.BlockSpec(memory_space=pl.ANY)] * 4 + [hbm_spec()] * 10,
        out_specs=(hbm_spec(),) * 4,
        scratch_shapes=[pltpu.VMEM(far, f32)]
        + like(*carried)
        + [pltpu.VMEM((3, rows, cols), f32), pltpu.VMEM(*field)]
        + like(basis, wet, owner)
        + [pltpu.VMEM(*field)] * 3
        + [
            pltpu.VMEM((far[0] * far[1] * 8, far[3]), f32),
            pltpu.VMEM((rows // tile_h * modes, cols), f32),
            pltpu.VMEM(*parts),
            *(pltpu.VMEM(*h) for h in halos),
            pltpu.SemaphoreType.DMA((17,)),
            pltpu.SemaphoreType.DMA((steps // 2, 2)),
            pltpu.SemaphoreType.DMA((steps, 3)),
        ],
        compiler_params=pltpu.CompilerParams(vmem_limit_bytes=32 << 20),
        cost_estimate=cost(12 * rows * cols * K, 10 << 20),
        name="elevation",
    )(tx, *near, *in_hbm(*carried, adj, depth, basis, wet, owner))


def finish_kernel(
    fields_in, sums, hrow, hcol, bottom_in, edge_in, fields, grad_out, bottom, edge, grad, out_sems
):
    u = lax.axis_index("gx")
    v = lax.axis_index("gy")
    size_x = lax.axis_size("gx")
    size_y = lax.axis_size("gy")
    rows, cols = fields.shape[1:]

    right = hcol[...] * jnp.where(v + 1 < size_y, courant, 0.0)
    right = jnp.broadcast_to(right, (8, rows)).T[:, 0:1]
    edge[...] = edge_in[...] + jnp.where(iota((rows, K), 1) == K - 1, right, 0.0)
    below = hrow[...] * jnp.where(u + 1 < size_x, courant, 0.0)
    bottom[...] = bottom_in[...] + jnp.where(iota((8, cols), 0) == 7, below, 0.0)
    total = jnp.sum(sums[...], axis=0, keepdims=True)
    grad[...] = total[:, : grad.shape[1]]
    writes = [
        pltpu.make_async_copy(edge, fields.at[2, :, pl.ds(cols - K, K)], out_sems.at[0]),
        pltpu.make_async_copy(bottom, fields.at[1, pl.ds(rows - 8, 8), :], out_sems.at[1]),
        pltpu.make_async_copy(grad, grad_out, out_sems.at[2]),
    ]
    for copy in writes:
        copy.start()
    for copy in writes:
        copy.wait()


def finish(fields, sums, hrow, hcol, slots):
    _, rows, cols = fields.shape
    bottom = fields[1, rows - 8 :, :]
    edge = fields[2, :, cols - K :]
    return pl.pallas_call(
        finish_kernel,
        out_shape=(pltpu.HBM(fields.shape, f32), pltpu.HBM((1, slots), f32)),
        in_specs=[hbm_spec()] + [vmem_spec()] * 5,
        out_specs=(hbm_spec(), hbm_spec()),
        input_output_aliases={0: 0},
        scratch_shapes=[
            pltpu.VMEM((8, cols), f32),
            pltpu.VMEM((rows, K), f32),
            pltpu.VMEM((1, slots), f32),
            pltpu.SemaphoreType.DMA((3,)),
        ],
        compiler_params=pltpu.CompilerParams(vmem_limit_bytes=16 << 20),
        cost_estimate=cost(1 << 20, 1 << 20),
        name="finish",
    )(*in_hbm(fields), sums, hrow, hcol, bottom, edge)


def partner(axis, bit):
    return [(i, i ^ bit) for i in range(lax.axis_size(axis))]


def previous(axis):
    size = lax.axis_size(axis)
    return [(i, (i - 1) % size) for i in range(size)]


def body(
    adj_fields, depth, block_x, reduced_x, block_y, reduced_y, basis, coef, footprint, owner, wet
):
    size_x = lax.axis_size("gx")
    size_y = lax.axis_size("gy")
    px, py = ends(adj_fields, depth, block_x, block_y, size_x, size_y)
    tx = lax.all_to_all(px, "gx", split_axis=0, concat_axis=0, tiled=True)
    carried = carry(block_x, block_y, reduced_x, reduced_y, coef, footprint, wet)
    ty = py[None]
    ty = jnp.concatenate([ty, lax.ppermute(ty, "gy", partner("gy", size_y // 2))], axis=0)
    near = [ty] + [lax.ppermute(ty, "gy", partner("gy", bits)) for bits in range(1, size_y // 2)]
    fields, parts, erow, ecol = elevation(tx, near, carried, adj_fields, depth, basis, wet, owner)
    devices = size_x * size_y
    hrow = lax.ppermute(erow, "gx", previous("gx"))
    hcol = lax.ppermute(ecol, "gy", previous("gy"))
    sums = lax.all_to_all(
        parts[:, None, :], ("gx", "gy"), split_axis=0, concat_axis=0, tiled=True
    )
    slots = owner.shape[0] // devices
    adj_before, grad = finish(fields, sums[:, 0, :], hrow, hcol, slots)
    return adj_before, grad.reshape(slots)


def solution(mesh):
    in_specs = (
        P(None, "gx", "gy"),
        P("gx", "gy"),
        P(),
        P(),
        P(),
        P(),
        P(),
        P(),
        P(),
        P(),
        P("gx", "gy"),
    )
    out_specs = (P(None, "gx", "gy"), P(("gx", "gy")))
    return jax.shard_map(body, mesh=mesh, in_specs=in_specs, out_specs=out_specs, check_vma=False)
```

```python
import jax
import jax.numpy as jnp
from jax import lax
from jax.experimental import pallas as pl
from jax.experimental.pallas import tpu as pltpu
from jax.sharding import PartitionSpec as P

courant = 0.5
f32 = jnp.float32
bf16 = jnp.bfloat16
K = 128
EXTRA = 128

NN = (((1,), (0,)), ((), ()))
NT = (((1,), (1,)), ((), ()))
TN = (((0,), (0,)), ((), ()))


def halves(x):
    high = x.astype(bf16)
    return high, (x - high.astype(f32)).astype(bf16)


def mm(a, b, dims):
    return lax.dot_general(a, b, dims, preferred_element_type=f32)


def mm3(a, b, dims):
    ah, al = a
    bh, bl = b
    return mm(ah, bh, dims) + (mm(ah, bl, dims) + mm(al, bh, dims))


def exact(a, b, dims):
    return lax.dot_general(a, b, dims, precision=lax.Precision.HIGHEST, preferred_element_type=f32)


def iota(shape, dim):
    return lax.broadcasted_iota(jnp.int32, shape, dim)


def hbm_spec():
    return pl.BlockSpec(memory_space=pltpu.HBM)


def vmem_spec():
    return pl.BlockSpec(memory_space=pltpu.VMEM)


def in_hbm(*arrays):
    return tuple(pltpu.with_memory_space_constraint(a, pltpu.HBM) for a in arrays)


def in_vmem(*arrays):
    return tuple(pltpu.with_memory_space_constraint(a, pltpu.VMEM) for a in arrays)


def cost(flops, nbytes):
    return pl.CostEstimate(flops=flops, bytes_accessed=nbytes, transcendentals=0)


def stacked(first, last, c):
    high, low = halves(jnp.concatenate([first[c, 0:1, :], last[c, 7:8, :]], axis=0))
    return jnp.concatenate([high, low], axis=0)


def two_rows(weights, field, dims):
    high, low = halves(field)
    both = mm(weights, high, dims)
    return both[0:2] + both[2:4] + mm(weights[0:2], low, dims)


def block_ends(blocks, index, first, last, sems):
    here = pl.ds(index * first.shape[0], first.shape[0])
    return [
        pltpu.make_async_copy(blocks.at[here, pl.ds(0, 8), :], first, sems.at[0]),
        pltpu.make_async_copy(blocks.at[here, pl.ds(K - 8, 8), :], last, sems.at[1]),
    ]


def ends_kernel(
    adj, depth, block_x, block_y, px_hbm, py,
    vx, vy, first_x, last_x, first_y, last_y, drow, dcol, px, sems, out_sems,
):
    rows, cols = vx.shape
    nbx = first_x.shape[0]
    nby = first_y.shape[0]
    small = block_ends(block_x, lax.axis_index("gx"), first_x, last_x, sems)
    small += block_ends(block_y, lax.axis_index("gy"), first_y, last_y, sems.at[pl.ds(2, 2)])
    small.append(pltpu.make_async_copy(depth.at[pl.ds(rows - 8, 8), :], drow, sems.at[4]))
    side = pltpu.make_async_copy(depth.at[:, pl.ds(cols - K, K)], dcol, sems.at[5])
    field_x = pltpu.make_async_copy(adj.at[1], vx, sems.at[6])
    field_y = pltpu.make_async_copy(adj.at[2], vy, sems.at[7])
    for copy in small + [field_x, side, field_y]:
        copy.start()
    for copy in small:
        copy.wait()
    for part in range(cols // K):
        px[part : part + 1, cols:] = drow[7:8, part * K : (part + 1) * K]
    px[cols // K :, cols:] = jnp.zeros((8 - cols // K, EXTRA), f32)
    weights_x = [stacked(first_x, last_x, c) for c in range(nbx)]
    weights_y = [stacked(first_y, last_y, c) for c in range(nby)]
    field_x.wait()
    for c in range(nbx):
        px[2 * c : 2 * c + 2, :cols] = two_rows(weights_x[c], vx[c * K : (c + 1) * K, :], NN)
    outs = [pltpu.make_async_copy(px, px_hbm.at[d], out_sems.at[d]) for d in range(px_hbm.shape[0])]
    for copy in outs:
        copy.start()
    side.wait()
    field_y.wait()
    at_last = (iota((8, K), 1) == K - 1).astype(f32).astype(bf16)
    high, low = halves(dcol[...])
    line = mm(at_last, high, NT) + mm(at_last, low, NT)
    for part in range(rows // K):
        py[part : part + 1, rows:] = line[0:1, part * K : (part + 1) * K]
    py[rows // K :, rows:] = jnp.zeros((8 - rows // K, EXTRA), f32)
    for c in range(nby):
        py[2 * c : 2 * c + 2, :rows] = two_rows(weights_y[c], vy[:, c * K : (c + 1) * K], NT)
    for copy in outs:
        copy.wait()


def ends(adj, depth, block_x, block_y, size_x, size_y):
    rows, cols = depth.shape
    nbx = block_x.shape[0] // size_x
    nby = block_y.shape[0] // size_y
    shape = (2 * nbx, cols + EXTRA)
    return pl.pallas_call(
        ends_kernel,
        out_shape=(
            pltpu.HBM((size_x, *shape), f32),
            jax.ShapeDtypeStruct((2 * nby, rows + EXTRA), f32),
        ),
        in_specs=[hbm_spec()] * 4,
        out_specs=(hbm_spec(), vmem_spec()),
        scratch_shapes=[
            pltpu.VMEM((rows, cols), f32),
            pltpu.VMEM((rows, cols), f32),
            pltpu.VMEM((nbx, 8, K), f32),
            pltpu.VMEM((nbx, 8, K), f32),
            pltpu.VMEM((nby, 8, K), f32),
            pltpu.VMEM((nby, 8, K), f32),
            pltpu.VMEM((8, cols), f32),
            pltpu.VMEM((rows, K), f32),
            pltpu.VMEM(shape, f32),
            pltpu.SemaphoreType.DMA((8,)),
            pltpu.SemaphoreType.DMA((size_x,)),
        ],
        compiler_params=pltpu.CompilerParams(vmem_limit_bytes=16 << 20),
        cost_estimate=cost(2 * rows * cols * 32, 3 << 20),
        name="ends",
    )(*in_hbm(adj, depth, block_x, block_y))


def carry_kernel(
    block_x, block_y, reduced_x_hbm, reduced_y_hbm, coef_hbm, footprint_hbm,
    mx_hbm, my_hbm, gside_hbm, share_hbm, at_row_hbm,
    mx, my, gside, share, at_row, wx, wy, wpx, wpy, reduced_x, reduced_y, coef, footprint, sems, out_sems,
):
    u = lax.axis_index("gx")
    v = lax.axis_index("gy")
    nbx = wx.shape[0]
    nby = wy.shape[0]
    before_x = jnp.maximum(u * nbx - 1, 0)
    before_y = jnp.maximum(v * nby - 1, 0)
    copies = [
        pltpu.make_async_copy(footprint_hbm, footprint, sems.at[0]),
        pltpu.make_async_copy(coef_hbm, coef, sems.at[1]),
        pltpu.make_async_copy(reduced_x_hbm, reduced_x, sems.at[2]),
        pltpu.make_async_copy(block_x.at[pl.ds(u * nbx, nbx)], wx, sems.at[3]),
        pltpu.make_async_copy(reduced_y_hbm, reduced_y, sems.at[4]),
        pltpu.make_async_copy(block_y.at[pl.ds(v * nby, nby)], wy, sems.at[5]),
        pltpu.make_async_copy(block_x.at[before_x, pl.ds(K - 8, 8), :], wpx, sems.at[6]),
        pltpu.make_async_copy(block_y.at[before_y, pl.ds(K - 8, 8), :], wpy, sems.at[7]),
    ]
    for copy in copies:
        copy.start()
    outs = [
        pltpu.make_async_copy(share, share_hbm, out_sems.at[0]),
        pltpu.make_async_copy(at_row, at_row_hbm, out_sems.at[1]),
        pltpu.make_async_copy(mx, mx_hbm, out_sems.at[2]),
        pltpu.make_async_copy(my, my_hbm, out_sems.at[3]),
        pltpu.make_async_copy(gside, gside_hbm, out_sems.at[4]),
    ]
    for copy in copies[:2]:
        copy.wait()
    places, modes, count = coef.shape
    tiles_y = share.shape[1] // modes
    tiles_x = at_row.shape[1]
    total_cols = tiles_y * lax.axis_size("gy")
    number = footprint[...]
    row = lax.shift_right_logical(number, total_cols.bit_length() - 1)
    col = (number & (total_cols - 1)) - v * tiles_y
    top = jnp.min(row, axis=0, keepdims=True)
    tile_row = iota((tiles_x, count), 0)
    tile_col = lax.shift_right_logical(iota((tiles_y * modes, count), 0), modes.bit_length() - 1)
    for step in range(2):
        at_row[step] = (tile_row == top + step - u * tiles_x).astype(f32).astype(bf16)
        index = jnp.where(row == top + step, col, -1)
        acc = jnp.zeros((tiles_y * modes, count), f32)
        for f in range(places):
            scale = jnp.concatenate([coef[f]] * tiles_y, axis=0)
            acc = acc + jnp.where(tile_col == index[f : f + 1, :], scale, 0.0)
        share[step] = acc
    for copy in outs[:2]:
        copy.start()
    for copy in copies[2:4]:
        copy.wait()
    own_x = reduced_x[pl.ds(pl.multiple_of(u * 8, 8), 8), :]
    prev_x = reduced_x[pl.ds(pl.multiple_of(jnp.maximum(u - 1, 0) * 8, 8), 8), :]
    for c in range(nbx):
        w = wx[c]
        g = w[:, 0:1] * own_x[2 * c : 2 * c + 1, :] + w[:, K - 1 : K] * own_x[2 * c + 1 : 2 * c + 2, :]
        for i, part in enumerate(zip(halves(w), halves(g))):
            mx[i, c * K : (c + 1) * K, :] = jnp.concatenate(part, axis=1)
    outs[2].start()
    for copy in copies[4:]:
        copy.wait()
    own_y = halves(reduced_y[pl.ds(pl.multiple_of(v * 8, 8), 8), :])
    prev_y = reduced_y[pl.ds(pl.multiple_of(jnp.maximum(v - 1, 0) * 8, 8), 8), :]
    sub = iota((8, K), 0)
    for c in range(nby):
        turned = wy[c].T
        across = jnp.where(sub == 2 * c, turned[0:1, :], 0.0)
        across = jnp.where(sub == 2 * c + 1, turned[K - 1 : K, :], across)
        g = mm3(own_y, halves(across), TN)
        for i, part in enumerate(zip(halves(turned), halves(g))):
            my[i, :, c * K : (c + 1) * K] = jnp.concatenate(part, axis=0)
    outs[3].start()

    def side(w, prev, index):
        width = prev.shape[1]
        g = w[7:8, 0:1] * prev[6:7, :] + w[7:8, K - 1 : K] * prev[7:8, :]
        g = g + (iota((1, width), 1) == index * 8 - 1).astype(f32)
        return jnp.where(index > 0, g, 0.0)

    gside[...] = jnp.zeros(gside.shape, f32)
    gside[0:1, :] = side(wpx[...], prev_x, u)
    gside[1:2, : reduced_y.shape[1]] = side(wpy[...], prev_y, v)
    outs[4].start()
    for copy in outs:
        copy.wait()


def carry(block_x, block_y, reduced_x, reduced_y, coef, footprint, wet):
    nbx = block_x.shape[0] // lax.axis_size("gx")
    nby = block_y.shape[0] // lax.axis_size("gy")
    coef = coef.transpose(1, 2, 0)
    footprint = footprint.T
    _, modes, count = coef.shape
    tiles_x, tiles_y = wet.shape
    results = [
        ((2, nbx * K, K + reduced_x.shape[0]), bf16),
        ((2, K + reduced_y.shape[0], nby * K), bf16),
        ((8, reduced_x.shape[0]), f32),
        ((2, tiles_y * modes, count), f32),
        ((2, tiles_x, count), bf16),
    ]
    return pl.pallas_call(
        carry_kernel,
        out_shape=tuple(pltpu.HBM(*result) for result in results),
        in_specs=[hbm_spec()] * 6,
        out_specs=(hbm_spec(),) * 5,
        scratch_shapes=[pltpu.VMEM(*result) for result in results]
        + [
            pltpu.VMEM((nbx, K, K), f32),
            pltpu.VMEM((nby, K, K), f32),
            pltpu.VMEM((8, K), f32),
            pltpu.VMEM((8, K), f32),
            pltpu.VMEM(reduced_x.shape, f32),
            pltpu.VMEM(reduced_y.shape, f32),
            pltpu.VMEM(coef.shape, f32),
            pltpu.VMEM(footprint.shape, jnp.int32),
            pltpu.SemaphoreType.DMA((8,)),
            pltpu.SemaphoreType.DMA((5,)),
        ],
        compiler_params=pltpu.CompilerParams(vmem_limit_bytes=16 << 20),
        cost_estimate=cost(1 << 36, 2 << 20),
        name="carry",
    )(*in_hbm(block_x, block_y, reduced_x, reduced_y, coef, footprint))


def elev_kernel(
    tx, t0, t1, t2, t3, mx_in, my_in, gside_in, share_in, at_row_in, adj, depth, basis_in, wet_in, owner_in,
    fields_out, parts_out, erow, ecol,
    ty, mx, my, gside, share, at_row, planes, dep, basis, wet, owner,
    elev, fx, fy, tyn, mom, parts, sems, row_sems, out_sems,
):
    u = lax.axis_index("gx")
    v = lax.axis_index("gy")
    rows, cols = dep.shape
    steps = rows // K
    near = (t0, t1, t2, t3)
    first = [
        *(pltpu.make_async_copy(part, ty.at[i], sems.at[13 + i]) for i, part in enumerate(near)),
        pltpu.make_async_copy(gside_in, gside, sems.at[2]),
        pltpu.make_async_copy(owner_in, owner, sems.at[3]),
    ]
    second = [
        pltpu.make_async_copy(mx_in, mx, sems.at[4]),
        pltpu.make_async_copy(my_in, my, sems.at[5]),
    ]
    last = [
        pltpu.make_async_copy(basis_in, basis, sems.at[6]),
        pltpu.make_async_copy(wet_in, wet, sems.at[7]),
        pltpu.make_async_copy(share_in, share, sems.at[8]),
        pltpu.make_async_copy(at_row_in, at_row, sems.at[9]),
    ]
    fields = []
    for r in range(steps // 2):
        here = pl.ds(r * 2 * K, 2 * K)
        fields.append(
            [
                pltpu.make_async_copy(adj.at[:, here, :], planes.at[:, here, :], row_sems.at[r, 0]),
                pltpu.make_async_copy(depth.at[here, :], dep.at[here, :], row_sems.at[r, 1]),
            ]
        )
    for group in [fields[0], first, second, last[:1], fields[1], last[1:]]:
        for copy in group:
            copy.start()
    txs = halves(jnp.concatenate([tx[d][:, :cols] for d in range(tx.shape[0])], axis=0))
    for copy in first:
        copy.wait()
    devices = parts.shape[0]
    count = owner.shape[1]
    slots = count // devices
    for j in range(ty.shape[0] * ty.shape[1]):
        far = j ^ v
        tyn[j * 8 : (j + 1) * 8, :] = ty[far & (ty.shape[0] - 1), far // ty.shape[0]]
    ty_all = tyn[:, :rows]
    tys = halves(ty_all)
    tyt = halves(ty_all.T)
    up = jnp.maximum(u - 1, 0)
    left = jnp.maximum(v - 1, 0)
    gs = gside[...]
    edge_x = mm3(halves(gs), txs, NN)[0:1, :]
    edge_y = mm3(halves(gs[:, : ty_all.shape[0]]), tys, NN)[1:2, :]
    drow = tx[up][:, cols:]
    drow = jnp.concatenate([drow[p : p + 1, :] for p in range(cols // K)], axis=1)
    dcol = tyn[pl.ds(pl.multiple_of(left * 8, 8), 8), rows:]
    dcol = jnp.concatenate([dcol[p : p + 1, :] for p in range(rows // K)], axis=1)
    carry = edge_x * drow
    side = jnp.broadcast_to(edge_y * dcol, (8, rows)).T
    row = iota((K, cols), 0)
    lane = iota((K, K), 1)
    modes, tile_h, tile_w = basis.shape
    per = K // tile_h
    outs = []

    def send(plane, source, r):
        here = pl.ds(r * K, K)
        copy = pltpu.make_async_copy(
            source.at[here, :], fields_out.at[plane, here, :], out_sems.at[r, plane]
        )
        copy.start()
        outs.append(copy)

    for copy in second:
        copy.wait()
    for r in range(steps):
        here = slice(r * K, (r + 1) * K)
        if r == 0:
            for copy in fields[0] + last[:1]:
                copy.wait()
        if r == 2:
            for copy in fields[1]:
                copy.wait()
        d = dep[here, :]
        high, low = halves(planes[1, here, :])
        flux_x = mm3(
            (mx[0, here, :], mx[1, here, :]),
            (jnp.concatenate([high, txs[0]], axis=0), jnp.concatenate([low, txs[1]], axis=0)),
            NN,
        )
        if r % 2 == 0:
            pair = slice(r * K, (r + 2) * K)
            pieces = []
            for c in range(cols // K):
                block = slice(c * K, (c + 1) * K)
                high, low = halves(planes[2, pair, block])
                lhs = (
                    jnp.concatenate([high, tyt[0][pair, :]], axis=1),
                    jnp.concatenate([low, tyt[1][pair, :]], axis=1),
                )
                pieces.append(mm3(lhs, (my[0, :, block], my[1, :, block]), NN))
        flux_y = jnp.concatenate([piece[(r % 2) * K : (r % 2 + 1) * K] for piece in pieces], axis=1)
        weighted_x = d * flux_x
        weighted_y = d * flux_y
        before_x = jnp.where(row == 0, carry, pltpu.roll(weighted_x, 1, 0))
        carry = weighted_x[K - 1 : K, :]
        turned = [side[here, 0:1]] + [
            pltpu.roll(weighted_y[:, c * K : (c + 1) * K], 1, 1) for c in range(cols // K)
        ]
        before_y = jnp.concatenate(
            [jnp.where(lane == 0, turned[c], turned[c + 1]) for c in range(cols // K)], axis=1
        )
        e = planes[0, here, :] + courant * ((weighted_x - before_x) + (weighted_y - before_y))
        elev[here, :] = e
        send(0, elev, r)
        right = [pltpu.roll(e[:, c * K : (c + 1) * K], K - 1, 1) for c in range(cols // K)] + [0.0]
        right = jnp.concatenate(
            [jnp.where(lane == K - 1, right[c + 1], right[c]) for c in range(cols // K)], axis=1
        )
        fy[here, :] = flux_y + courant * (right - e)
        send(2, fy, r)
        fx[here, :] = flux_x + courant * (jnp.where(row == K - 1, 0.0, pltpu.roll(e, K - 1, 0)) - e)
        if r > 0:
            end = slice(r * K - 8, r * K)
            fx[end, :] = fx[end, :] + jnp.where(row[:8] == 7, courant * e[0:1, :], 0.0)
            send(1, fx, r - 1)
        if r == 0:
            erow[...] = e[0:1, :]
        ecol[:, here] = e[:, :K].T[0:1, :]
        for a in range(per):
            for w in range(cols // tile_w):
                tile = e[a * tile_h : (a + 1) * tile_h, w * tile_w : (w + 1) * tile_w]
                for b in range(modes):
                    at = b * (rows // tile_h) + r * per + a
                    mom[at : at + 1, w * tile_w : (w + 1) * tile_w] = jnp.sum(
                        tile * basis[b], axis=0, keepdims=True
                    )
    send(1, fx, steps - 1)
    for copy in last[1:]:
        copy.wait()
    tiles_y, tiles_x = wet.shape
    ones = jnp.ones((8, tile_w), bf16)
    pieces = []
    for w in range(tiles_y):
        high, low = halves(mom[:, w * tile_w : (w + 1) * tile_w])
        line = (mm(ones, high, NT) + mm(ones, low, NT))[0:1, :]
        keep = wet[w : w + 1, :].astype(f32)
        for b in range(modes):
            pieces.append(line[:, b * tiles_x : (b + 1) * tiles_x] * keep)
    high, low = halves(jnp.concatenate(pieces, axis=0))
    table = jnp.concatenate([high, low], axis=0)
    own = owner[...]
    device_of = iota((devices, count), 0) == lax.shift_right_logical(own, slots.bit_length() - 1)
    device_of = device_of.astype(f32).astype(bf16)
    slot_of = iota((slots, count), 0) == (own & (slots - 1))
    lines = tiles_y * modes
    acc = jnp.zeros((lines, count), f32)
    for step in range(2):
        both = mm(table, at_row[step], NN)
        acc = acc + (both[:lines] + both[lines:]) * share[step]
    total = jnp.sum(acc, axis=0, keepdims=True)
    placed = jnp.concatenate(halves(jnp.where(slot_of, total, 0.0)), axis=0)
    both = mm(device_of, placed, NT)
    sums = both[:, :slots] + both[:, slots:]
    parts[...] = jnp.concatenate([sums, jnp.zeros((devices, K - slots), f32)], axis=1)
    outs.append(pltpu.make_async_copy(parts, parts_out, sems.at[10]))
    outs[-1].start()
    for copy in outs:
        copy.wait()


def elevation(tx, near, carried, adj, depth, basis, wet, owner):
    rows, cols = depth.shape
    modes, tile_h, tile_w = basis.shape
    devices = lax.axis_size("gx") * lax.axis_size("gy")
    steps = rows // K
    wet = wet.T
    owner = owner.reshape(1, -1)
    field = ((rows, cols), f32)
    far = (len(near), *near[0].shape)
    parts = ((devices, K), f32)
    halos = [((1, cols), f32), ((1, rows), f32)]
    like = lambda *arrays: [pltpu.VMEM(a.shape, a.dtype) for a in arrays]
    return pl.pallas_call(
        elev_kernel,
        out_shape=(
            pltpu.HBM((3, rows, cols), f32),
            pltpu.HBM(*parts),
            *(jax.ShapeDtypeStruct(*h) for h in halos),
        ),
        in_specs=[vmem_spec()] + [pl.BlockSpec(memory_space=pl.ANY)] * 4 + [hbm_spec()] * 10,
        out_specs=(hbm_spec(), hbm_spec(), vmem_spec(), vmem_spec()),
        scratch_shapes=[pltpu.VMEM(far, f32)]
        + like(*carried)
        + [pltpu.VMEM((3, rows, cols), f32), pltpu.VMEM(*field)]
        + like(basis, wet, owner)
        + [pltpu.VMEM(*field)] * 3
        + [
            pltpu.VMEM((far[0] * far[1] * 8, far[3]), f32),
            pltpu.VMEM((rows // tile_h * modes, cols), f32),
            pltpu.VMEM(*parts),
            pltpu.SemaphoreType.DMA((17,)),
            pltpu.SemaphoreType.DMA((steps // 2, 2)),
            pltpu.SemaphoreType.DMA((steps, 3)),
        ],
        compiler_params=pltpu.CompilerParams(vmem_limit_bytes=32 << 20),
        cost_estimate=cost(12 * rows * cols * K, 10 << 20),
        name="elevation",
    )(tx, *near, *in_hbm(*carried, adj, depth, basis, wet, owner))


def finish_kernel(
    fields_in, sums, hrow, hcol, bottom_in, edge_in, fields, grad_out, bottom, edge, grad, out_sems
):
    u = lax.axis_index("gx")
    v = lax.axis_index("gy")
    size_x = lax.axis_size("gx")
    size_y = lax.axis_size("gy")
    rows, cols = fields.shape[1:]

    right = hcol[...] * jnp.where(v + 1 < size_y, courant, 0.0)
    right = jnp.broadcast_to(right, (8, rows)).T[:, 0:1]
    edge[...] = edge_in[...] + jnp.where(iota((rows, K), 1) == K - 1, right, 0.0)
    below = hrow[...] * jnp.where(u + 1 < size_x, courant, 0.0)
    bottom[...] = bottom_in[...] + jnp.where(iota((8, cols), 0) == 7, below, 0.0)
    total = jnp.sum(sums[...], axis=0, keepdims=True)
    grad[...] = total[:, : grad.shape[1]]
    writes = [
        pltpu.make_async_copy(edge, fields.at[2, :, pl.ds(cols - K, K)], out_sems.at[0]),
        pltpu.make_async_copy(bottom, fields.at[1, pl.ds(rows - 8, 8), :], out_sems.at[1]),
        pltpu.make_async_copy(grad, grad_out, out_sems.at[2]),
    ]
    for copy in writes:
        copy.start()
    for copy in writes:
        copy.wait()


def finish(fields, sums, hrow, hcol, slots):
    _, rows, cols = fields.shape
    bottom = fields[1, rows - 8 :, :]
    edge = fields[2, :, cols - K :]
    return pl.pallas_call(
        finish_kernel,
        out_shape=(pltpu.HBM(fields.shape, f32), pltpu.HBM((1, slots), f32)),
        in_specs=[hbm_spec()] + [vmem_spec()] * 5,
        out_specs=(hbm_spec(), hbm_spec()),
        input_output_aliases={0: 0},
        scratch_shapes=[
            pltpu.VMEM((8, cols), f32),
            pltpu.VMEM((rows, K), f32),
            pltpu.VMEM((1, slots), f32),
            pltpu.SemaphoreType.DMA((3,)),
        ],
        compiler_params=pltpu.CompilerParams(vmem_limit_bytes=16 << 20),
        cost_estimate=cost(1 << 20, 1 << 20),
        name="finish",
    )(*in_hbm(fields), sums, hrow, hcol, bottom, edge)


def partner(axis, bit):
    return [(i, i ^ bit) for i in range(lax.axis_size(axis))]


def previous(axis):
    size = lax.axis_size(axis)
    return [(i, (i - 1) % size) for i in range(size)]


def body(
    adj_fields, depth, block_x, reduced_x, block_y, reduced_y, basis, coef, footprint, owner, wet
):
    size_x = lax.axis_size("gx")
    size_y = lax.axis_size("gy")
    px, py = ends(adj_fields, depth, block_x, block_y, size_x, size_y)
    tx = lax.all_to_all(px, "gx", split_axis=0, concat_axis=0, tiled=True)
    carried = carry(block_x, block_y, reduced_x, reduced_y, coef, footprint, wet)
    ty = py[None]
    ty = jnp.concatenate([ty, lax.ppermute(ty, "gy", partner("gy", size_y // 2))], axis=0)
    near = [ty] + [lax.ppermute(ty, "gy", partner("gy", bits)) for bits in range(1, size_y // 2)]
    fields, parts, erow, ecol = elevation(tx, near, carried, adj_fields, depth, basis, wet, owner)
    devices = size_x * size_y
    hrow = lax.ppermute(erow, "gx", previous("gx"))
    hcol = lax.ppermute(ecol, "gy", previous("gy"))
    sums = lax.all_to_all(
        parts[:, None, :], ("gx", "gy"), split_axis=0, concat_axis=0, tiled=True
    )
    slots = owner.shape[0] // devices
    adj_before, grad = finish(fields, sums[:, 0, :], hrow, hcol, slots)
    return adj_before, grad.reshape(slots)


def solution(mesh):
    in_specs = (
        P(None, "gx", "gy"),
        P("gx", "gy"),
        P(),
        P(),
        P(),
        P(),
        P(),
        P(),
        P(),
        P(),
        P("gx", "gy"),
    )
    out_specs = (P(None, "gx", "gy"), P(("gx", "gy")))
    return jax.shard_map(body, mesh=mesh, in_specs=in_specs, out_specs=out_specs, check_vma=False)
```

```python
import jax
import jax.numpy as jnp
from jax import lax
from jax.experimental import pallas as pl
from jax.experimental.pallas import tpu as pltpu
from jax.sharding import PartitionSpec as P

courant = 0.5
f32 = jnp.float32
bf16 = jnp.bfloat16
K = 128
EXTRA = 128

NN = (((1,), (0,)), ((), ()))
NT = (((1,), (1,)), ((), ()))
TN = (((0,), (0,)), ((), ()))


def halves(x):
    high = x.astype(bf16)
    return high, (x - high.astype(f32)).astype(bf16)


def mm(a, b, dims):
    return lax.dot_general(a, b, dims, preferred_element_type=f32)


def mm3(a, b, dims):
    ah, al = a
    bh, bl = b
    return mm(ah, bh, dims) + (mm(ah, bl, dims) + mm(al, bh, dims))


def exact(a, b, dims):
    return lax.dot_general(a, b, dims, precision=lax.Precision.HIGHEST, preferred_element_type=f32)


def iota(shape, dim):
    return lax.broadcasted_iota(jnp.int32, shape, dim)


def hbm_spec():
    return pl.BlockSpec(memory_space=pltpu.HBM)


def vmem_spec():
    return pl.BlockSpec(memory_space=pltpu.VMEM)


def in_hbm(*arrays):
    return tuple(pltpu.with_memory_space_constraint(a, pltpu.HBM) for a in arrays)


def in_vmem(*arrays):
    return tuple(pltpu.with_memory_space_constraint(a, pltpu.VMEM) for a in arrays)


def cost(flops, nbytes):
    return pl.CostEstimate(flops=flops, bytes_accessed=nbytes, transcendentals=0)


def stacked(first, last, c):
    high, low = halves(jnp.concatenate([first[c, 0:1, :], last[c, 7:8, :]], axis=0))
    return jnp.concatenate([high, low], axis=0)


def two_rows(weights, field, dims):
    high, low = halves(field)
    both = mm(weights, high, dims)
    return both[0:2] + both[2:4] + mm(weights[0:2], low, dims)


def block_ends(blocks, index, first, last, sems):
    here = pl.ds(index * first.shape[0], first.shape[0])
    return [
        pltpu.make_async_copy(blocks.at[here, pl.ds(0, 8), :], first, sems.at[0]),
        pltpu.make_async_copy(blocks.at[here, pl.ds(K - 8, 8), :], last, sems.at[1]),
    ]


def ends_kernel(
    adj, depth, block_x, block_y, px_hbm, py,
    vx, vy, first_x, last_x, first_y, last_y, drow, dcol, px, sems, out_sems,
):
    rows, cols = vx.shape
    nbx = first_x.shape[0]
    nby = first_y.shape[0]
    small = block_ends(block_x, lax.axis_index("gx"), first_x, last_x, sems)
    small += block_ends(block_y, lax.axis_index("gy"), first_y, last_y, sems.at[pl.ds(2, 2)])
    small.append(pltpu.make_async_copy(depth.at[pl.ds(rows - 8, 8), :], drow, sems.at[4]))
    side = pltpu.make_async_copy(depth.at[:, pl.ds(cols - K, K)], dcol, sems.at[5])
    field_x = pltpu.make_async_copy(adj.at[1], vx, sems.at[6])
    field_y = pltpu.make_async_copy(adj.at[2], vy, sems.at[7])
    for copy in small + [field_x, side, field_y]:
        copy.start()
    for copy in small:
        copy.wait()
    for part in range(cols // K):
        px[part : part + 1, cols:] = drow[7:8, part * K : (part + 1) * K]
    px[cols // K :, cols:] = jnp.zeros((8 - cols // K, EXTRA), f32)
    weights_x = [stacked(first_x, last_x, c) for c in range(nbx)]
    weights_y = [stacked(first_y, last_y, c) for c in range(nby)]
    field_x.wait()
    for c in range(nbx):
        px[2 * c : 2 * c + 2, :cols] = two_rows(weights_x[c], vx[c * K : (c + 1) * K, :], NN)
    outs = [pltpu.make_async_copy(px, px_hbm.at[d], out_sems.at[d]) for d in range(px_hbm.shape[0])]
    for copy in outs:
        copy.start()
    side.wait()
    field_y.wait()
    at_last = (iota((8, K), 1) == K - 1).astype(f32).astype(bf16)
    high, low = halves(dcol[...])
    line = mm(at_last, high, NT) + mm(at_last, low, NT)
    for part in range(rows // K):
        py[part : part + 1, rows:] = line[0:1, part * K : (part + 1) * K]
    py[rows // K :, rows:] = jnp.zeros((8 - rows // K, EXTRA), f32)
    for c in range(nby):
        py[2 * c : 2 * c + 2, :rows] = two_rows(weights_y[c], vy[:, c * K : (c + 1) * K], NT)
    for copy in outs:
        copy.wait()


def ends(adj, depth, block_x, block_y, size_x, size_y):
    rows, cols = depth.shape
    nbx = block_x.shape[0] // size_x
    nby = block_y.shape[0] // size_y
    shape = (2 * nbx, cols + EXTRA)
    return pl.pallas_call(
        ends_kernel,
        out_shape=(
            pltpu.HBM((size_x, *shape), f32),
            jax.ShapeDtypeStruct((2 * nby, rows + EXTRA), f32),
        ),
        in_specs=[hbm_spec()] * 4,
        out_specs=(hbm_spec(), vmem_spec()),
        scratch_shapes=[
            pltpu.VMEM((rows, cols), f32),
            pltpu.VMEM((rows, cols), f32),
            pltpu.VMEM((nbx, 8, K), f32),
            pltpu.VMEM((nbx, 8, K), f32),
            pltpu.VMEM((nby, 8, K), f32),
            pltpu.VMEM((nby, 8, K), f32),
            pltpu.VMEM((8, cols), f32),
            pltpu.VMEM((rows, K), f32),
            pltpu.VMEM(shape, f32),
            pltpu.SemaphoreType.DMA((8,)),
            pltpu.SemaphoreType.DMA((size_x,)),
        ],
        compiler_params=pltpu.CompilerParams(vmem_limit_bytes=16 << 20),
        cost_estimate=cost(2 * rows * cols * 32, 3 << 20),
        name="ends",
    )(*in_hbm(adj, depth, block_x, block_y))


def carry_kernel(
    block_x, block_y, reduced_x_hbm, reduced_y_hbm, coef_hbm, footprint_hbm,
    mx_hbm, my_hbm, gside_hbm, share_hbm, at_row_hbm,
    mx, my, gside, share, at_row, wx, wy, wpx, wpy, reduced_x, reduced_y, coef, footprint, sems, out_sems,
):
    u = lax.axis_index("gx")
    v = lax.axis_index("gy")
    nbx = wx.shape[0]
    nby = wy.shape[0]
    before_x = jnp.maximum(u * nbx - 1, 0)
    before_y = jnp.maximum(v * nby - 1, 0)
    copies = [
        pltpu.make_async_copy(footprint_hbm, footprint, sems.at[0]),
        pltpu.make_async_copy(coef_hbm, coef, sems.at[1]),
        pltpu.make_async_copy(reduced_x_hbm, reduced_x, sems.at[2]),
        pltpu.make_async_copy(block_x.at[pl.ds(u * nbx, nbx)], wx, sems.at[3]),
        pltpu.make_async_copy(reduced_y_hbm, reduced_y, sems.at[4]),
        pltpu.make_async_copy(block_y.at[pl.ds(v * nby, nby)], wy, sems.at[5]),
        pltpu.make_async_copy(block_x.at[before_x, pl.ds(K - 8, 8), :], wpx, sems.at[6]),
        pltpu.make_async_copy(block_y.at[before_y, pl.ds(K - 8, 8), :], wpy, sems.at[7]),
    ]
    for copy in copies:
        copy.start()
    outs = [
        pltpu.make_async_copy(share, share_hbm, out_sems.at[0]),
        pltpu.make_async_copy(at_row, at_row_hbm, out_sems.at[1]),
        pltpu.make_async_copy(mx, mx_hbm, out_sems.at[2]),
        pltpu.make_async_copy(my, my_hbm, out_sems.at[3]),
        pltpu.make_async_copy(gside, gside_hbm, out_sems.at[4]),
    ]
    for copy in copies[:2]:
        copy.wait()
    places, modes, count = coef.shape
    tiles_y = share.shape[1] // modes
    tiles_x = at_row.shape[1]
    total_cols = tiles_y * lax.axis_size("gy")
    number = footprint[...]
    row = lax.shift_right_logical(number, total_cols.bit_length() - 1)
    col = (number & (total_cols - 1)) - v * tiles_y
    top = jnp.min(row, axis=0, keepdims=True)
    tile_row = iota((tiles_x, count), 0)
    tile_col = lax.shift_right_logical(iota((tiles_y * modes, count), 0), modes.bit_length() - 1)
    for step in range(2):
        at_row[step] = (tile_row == top + step - u * tiles_x).astype(f32).astype(bf16)
        index = jnp.where(row == top + step, col, -1)
        acc = jnp.zeros((tiles_y * modes, count), f32)
        for f in range(places):
            scale = jnp.concatenate([coef[f]] * tiles_y, axis=0)
            acc = acc + jnp.where(tile_col == index[f : f + 1, :], scale, 0.0)
        share[step] = acc
    for copy in outs[:2]:
        copy.start()
    for copy in copies[2:]:
        copy.wait()
    own_x = reduced_x[pl.ds(pl.multiple_of(u * 8, 8), 8), :]
    prev_x = reduced_x[pl.ds(pl.multiple_of(jnp.maximum(u - 1, 0) * 8, 8), 8), :]
    for c in range(nbx):
        w = wx[c]
        g = w[:, 0:1] * own_x[2 * c : 2 * c + 1, :] + w[:, K - 1 : K] * own_x[2 * c + 1 : 2 * c + 2, :]
        for i, part in enumerate(zip(halves(w), halves(g))):
            mx[i, c * K : (c + 1) * K, :] = jnp.concatenate(part, axis=1)
    outs[2].start()
    own_y = halves(reduced_y[pl.ds(pl.multiple_of(v * 8, 8), 8), :])
    prev_y = reduced_y[pl.ds(pl.multiple_of(jnp.maximum(v - 1, 0) * 8, 8), 8), :]
    sub = iota((8, K), 0)
    for c in range(nby):
        turned = wy[c].T
        across = jnp.where(sub == 2 * c, turned[0:1, :], 0.0)
        across = jnp.where(sub == 2 * c + 1, turned[K - 1 : K, :], across)
        g = mm3(own_y, halves(across), TN)
        for i, part in enumerate(zip(halves(turned), halves(g))):
            my[i, :, c * K : (c + 1) * K] = jnp.concatenate(part, axis=0)
    outs[3].start()

    def side(w, prev, index):
        width = prev.shape[1]
        g = w[7:8, 0:1] * prev[6:7, :] + w[7:8, K - 1 : K] * prev[7:8, :]
        g = g + (iota((1, width), 1) == index * 8 - 1).astype(f32)
        return jnp.where(index > 0, g, 0.0)

    gside[...] = jnp.zeros(gside.shape, f32)
    gside[0:1, :] = side(wpx[...], prev_x, u)
    gside[1:2, : reduced_y.shape[1]] = side(wpy[...], prev_y, v)
    outs[4].start()
    for copy in outs:
        copy.wait()


def carry(block_x, block_y, reduced_x, reduced_y, coef, footprint, wet):
    nbx = block_x.shape[0] // lax.axis_size("gx")
    nby = block_y.shape[0] // lax.axis_size("gy")
    coef = coef.transpose(1, 2, 0)
    footprint = footprint.T
    _, modes, count = coef.shape
    tiles_x, tiles_y = wet.shape
    results = [
        ((2, nbx * K, K + reduced_x.shape[0]), bf16),
        ((2, K + reduced_y.shape[0], nby * K), bf16),
        ((8, reduced_x.shape[0]), f32),
        ((2, tiles_y * modes, count), f32),
        ((2, tiles_x, count), bf16),
    ]
    return pl.pallas_call(
        carry_kernel,
        out_shape=tuple(pltpu.HBM(*result) for result in results),
        in_specs=[hbm_spec()] * 6,
        out_specs=(hbm_spec(),) * 5,
        scratch_shapes=[pltpu.VMEM(*result) for result in results]
        + [
            pltpu.VMEM((nbx, K, K), f32),
            pltpu.VMEM((nby, K, K), f32),
            pltpu.VMEM((8, K), f32),
            pltpu.VMEM((8, K), f32),
            pltpu.VMEM(reduced_x.shape, f32),
            pltpu.VMEM(reduced_y.shape, f32),
            pltpu.VMEM(coef.shape, f32),
            pltpu.VMEM(footprint.shape, jnp.int32),
            pltpu.SemaphoreType.DMA((8,)),
            pltpu.SemaphoreType.DMA((5,)),
        ],
        compiler_params=pltpu.CompilerParams(vmem_limit_bytes=16 << 20),
        cost_estimate=cost(1 << 36, 2 << 20),
        name="carry",
    )(*in_hbm(block_x, block_y, reduced_x, reduced_y, coef, footprint))


def elev_kernel(
    tx, t0, t1, t2, t3, mx_in, my_in, gside_in, share_in, at_row_in, adj, depth, basis_in, wet_in, owner_in,
    fields_out, parts_out, erow, ecol,
    ty, mx, my, gside, share, at_row, planes, dep, basis, wet, owner,
    elev, fx, fy, tyn, mom, parts, sems, row_sems, out_sems,
):
    u = lax.axis_index("gx")
    v = lax.axis_index("gy")
    rows, cols = dep.shape
    steps = rows // K
    near = (t0, t1, t2, t3)
    first = [
        *(pltpu.make_async_copy(part, ty.at[i], sems.at[13 + i]) for i, part in enumerate(near)),
        pltpu.make_async_copy(gside_in, gside, sems.at[2]),
        pltpu.make_async_copy(owner_in, owner, sems.at[3]),
    ]
    second = [
        pltpu.make_async_copy(mx_in, mx, sems.at[4]),
        pltpu.make_async_copy(my_in, my, sems.at[5]),
    ]
    last = [
        pltpu.make_async_copy(basis_in, basis, sems.at[6]),
        pltpu.make_async_copy(wet_in, wet, sems.at[7]),
        pltpu.make_async_copy(share_in, share, sems.at[8]),
        pltpu.make_async_copy(at_row_in, at_row, sems.at[9]),
    ]
    fields = []
    for r in range(steps // 2):
        here = pl.ds(r * 2 * K, 2 * K)
        fields.append(
            [
                pltpu.make_async_copy(adj.at[:, here, :], planes.at[:, here, :], row_sems.at[r, 0]),
                pltpu.make_async_copy(depth.at[here, :], dep.at[here, :], row_sems.at[r, 1]),
            ]
        )
    for group in [fields[0], first, second, last[:1], fields[1], last[1:]]:
        for copy in group:
            copy.start()
    txs = halves(jnp.concatenate([tx[d][:, :cols] for d in range(tx.shape[0])], axis=0))
    for copy in first:
        copy.wait()
    devices = parts.shape[0]
    count = owner.shape[1]
    slots = count // devices
    for j in range(ty.shape[0] * ty.shape[1]):
        far = j ^ v
        tyn[j * 8 : (j + 1) * 8, :] = ty[far & (ty.shape[0] - 1), far // ty.shape[0]]
    ty_all = tyn[:, :rows]
    tys = halves(ty_all)
    tyt = halves(ty_all.T)
    up = jnp.maximum(u - 1, 0)
    left = jnp.maximum(v - 1, 0)
    gs = gside[...]
    edge_x = mm3(halves(gs), txs, NN)[0:1, :]
    edge_y = mm3(halves(gs[:, : ty_all.shape[0]]), tys, NN)[1:2, :]
    drow = tx[up][:, cols:]
    drow = jnp.concatenate([drow[p : p + 1, :] for p in range(cols // K)], axis=1)
    dcol = tyn[pl.ds(pl.multiple_of(left * 8, 8), 8), rows:]
    dcol = jnp.concatenate([dcol[p : p + 1, :] for p in range(rows // K)], axis=1)
    carry = edge_x * drow
    side = jnp.broadcast_to(edge_y * dcol, (8, rows)).T
    row = iota((K, cols), 0)
    lane = iota((K, K), 1)
    modes, tile_h, tile_w = basis.shape
    per = K // tile_h
    outs = []

    def send(plane, source, r):
        here = pl.ds(r * K, K)
        copy = pltpu.make_async_copy(
            source.at[here, :], fields_out.at[plane, here, :], out_sems.at[r, plane]
        )
        copy.start()
        outs.append(copy)

    for copy in second:
        copy.wait()
    for r in range(steps):
        here = slice(r * K, (r + 1) * K)
        if r == 0:
            for copy in fields[0] + last[:1]:
                copy.wait()
        if r == 2:
            for copy in fields[1]:
                copy.wait()
        d = dep[here, :]
        high, low = halves(planes[1, here, :])
        flux_x = mm3(
            (mx[0, here, :], mx[1, here, :]),
            (jnp.concatenate([high, txs[0]], axis=0), jnp.concatenate([low, txs[1]], axis=0)),
            NN,
        )
        if r % 2 == 0:
            pair = slice(r * K, (r + 2) * K)
            pieces = []
            for c in range(cols // K):
                block = slice(c * K, (c + 1) * K)
                high, low = halves(planes[2, pair, block])
                lhs = (
                    jnp.concatenate([high, tyt[0][pair, :]], axis=1),
                    jnp.concatenate([low, tyt[1][pair, :]], axis=1),
                )
                pieces.append(mm3(lhs, (my[0, :, block], my[1, :, block]), NN))
        flux_y = jnp.concatenate([piece[(r % 2) * K : (r % 2 + 1) * K] for piece in pieces], axis=1)
        weighted_x = d * flux_x
        weighted_y = d * flux_y
        before_x = jnp.where(row == 0, carry, pltpu.roll(weighted_x, 1, 0))
        carry = weighted_x[K - 1 : K, :]
        turned = [side[here, 0:1]] + [
            pltpu.roll(weighted_y[:, c * K : (c + 1) * K], 1, 1) for c in range(cols // K)
        ]
        before_y = jnp.concatenate(
            [jnp.where(lane == 0, turned[c], turned[c + 1]) for c in range(cols // K)], axis=1
        )
        e = planes[0, here, :] + courant * ((weighted_x - before_x) + (weighted_y - before_y))
        elev[here, :] = e
        send(0, elev, r)
        right = [pltpu.roll(e[:, c * K : (c + 1) * K], K - 1, 1) for c in range(cols // K)] + [0.0]
        right = jnp.concatenate(
            [jnp.where(lane == K - 1, right[c + 1], right[c]) for c in range(cols // K)], axis=1
        )
        fy[here, :] = flux_y + courant * (right - e)
        send(2, fy, r)
        fx[here, :] = flux_x + courant * (jnp.where(row == K - 1, 0.0, pltpu.roll(e, K - 1, 0)) - e)
        if r > 0:
            end = slice(r * K - 8, r * K)
            fx[end, :] = fx[end, :] + jnp.where(row[:8] == 7, courant * e[0:1, :], 0.0)
            send(1, fx, r - 1)
        if r == 0:
            erow[...] = e[0:1, :]
        ecol[:, here] = e[:, :K].T[0:1, :]
        for a in range(per):
            for w in range(cols // tile_w):
                tile = e[a * tile_h : (a + 1) * tile_h, w * tile_w : (w + 1) * tile_w]
                for b in range(modes):
                    at = b * (rows // tile_h) + r * per + a
                    mom[at : at + 1, w * tile_w : (w + 1) * tile_w] = jnp.sum(
                        tile * basis[b], axis=0, keepdims=True
                    )
    send(1, fx, steps - 1)
    for copy in last[1:]:
        copy.wait()
    tiles_y, tiles_x = wet.shape
    ones = jnp.ones((8, tile_w), bf16)
    pieces = []
    for w in range(tiles_y):
        high, low = halves(mom[:, w * tile_w : (w + 1) * tile_w])
        line = (mm(ones, high, NT) + mm(ones, low, NT))[0:1, :]
        keep = wet[w : w + 1, :].astype(f32)
        for b in range(modes):
            pieces.append(line[:, b * tiles_x : (b + 1) * tiles_x] * keep)
    high, low = halves(jnp.concatenate(pieces, axis=0))
    table = jnp.concatenate([high, low], axis=0)
    own = owner[...]
    device_of = iota((devices, count), 0) == lax.shift_right_logical(own, slots.bit_length() - 1)
    device_of = device_of.astype(f32).astype(bf16)
    slot_of = iota((slots, count), 0) == (own & (slots - 1))
    lines = tiles_y * modes
    acc = jnp.zeros((lines, count), f32)
    for step in range(2):
        both = mm(table, at_row[step], NN)
        acc = acc + (both[:lines] + both[lines:]) * share[step]
    total = jnp.sum(acc, axis=0, keepdims=True)
    placed = jnp.concatenate(halves(jnp.where(slot_of, total, 0.0)), axis=0)
    both = mm(device_of, placed, NT)
    sums = both[:, :slots] + both[:, slots:]
    parts[...] = jnp.concatenate([sums, jnp.zeros((devices, K - slots), f32)], axis=1)
    outs.append(pltpu.make_async_copy(parts, parts_out, sems.at[10]))
    outs[-1].start()
    for copy in outs:
        copy.wait()


def elevation(tx, near, carried, adj, depth, basis, wet, owner):
    rows, cols = depth.shape
    modes, tile_h, tile_w = basis.shape
    devices = lax.axis_size("gx") * lax.axis_size("gy")
    steps = rows // K
    wet = wet.T
    owner = owner.reshape(1, -1)
    field = ((rows, cols), f32)
    far = (len(near), *near[0].shape)
    parts = ((devices, K), f32)
    halos = [((1, cols), f32), ((1, rows), f32)]
    like = lambda *arrays: [pltpu.VMEM(a.shape, a.dtype) for a in arrays]
    return pl.pallas_call(
        elev_kernel,
        out_shape=(
            pltpu.HBM((3, rows, cols), f32),
            pltpu.HBM(*parts),
            *(jax.ShapeDtypeStruct(*h) for h in halos),
        ),
        in_specs=[vmem_spec()] + [pl.BlockSpec(memory_space=pl.ANY)] * 4 + [hbm_spec()] * 10,
        out_specs=(hbm_spec(), hbm_spec(), vmem_spec(), vmem_spec()),
        scratch_shapes=[pltpu.VMEM(far, f32)]
        + like(*carried)
        + [pltpu.VMEM((3, rows, cols), f32), pltpu.VMEM(*field)]
        + like(basis, wet, owner)
        + [pltpu.VMEM(*field)] * 3
        + [
            pltpu.VMEM((far[0] * far[1] * 8, far[3]), f32),
            pltpu.VMEM((rows // tile_h * modes, cols), f32),
            pltpu.VMEM(*parts),
            pltpu.SemaphoreType.DMA((17,)),
            pltpu.SemaphoreType.DMA((steps // 2, 2)),
            pltpu.SemaphoreType.DMA((steps, 3)),
        ],
        compiler_params=pltpu.CompilerParams(vmem_limit_bytes=32 << 20),
        cost_estimate=cost(12 * rows * cols * K, 10 << 20),
        name="elevation",
    )(tx, *near, *in_hbm(*carried, adj, depth, basis, wet, owner))


def finish_kernel(
    fields_in, sums, hrow, hcol, bottom_in, edge_in, fields, grad_out, bottom, edge, grad, out_sems
):
    u = lax.axis_index("gx")
    v = lax.axis_index("gy")
    size_x = lax.axis_size("gx")
    size_y = lax.axis_size("gy")
    rows, cols = fields.shape[1:]

    right = hcol[...] * jnp.where(v + 1 < size_y, courant, 0.0)
    right = jnp.broadcast_to(right, (8, rows)).T[:, 0:1]
    edge[...] = edge_in[...] + jnp.where(iota((rows, K), 1) == K - 1, right, 0.0)
    below = hrow[...] * jnp.where(u + 1 < size_x, courant, 0.0)
    bottom[...] = bottom_in[...] + jnp.where(iota((8, cols), 0) == 7, below, 0.0)
    total = jnp.sum(sums[...], axis=0, keepdims=True)
    grad[...] = total[:, : grad.shape[1]]
    writes = [
        pltpu.make_async_copy(edge, fields.at[2, :, pl.ds(cols - K, K)], out_sems.at[0]),
        pltpu.make_async_copy(bottom, fields.at[1, pl.ds(rows - 8, 8), :], out_sems.at[1]),
        pltpu.make_async_copy(grad, grad_out, out_sems.at[2]),
    ]
    for copy in writes:
        copy.start()
    for copy in writes:
        copy.wait()


def finish(fields, sums, hrow, hcol, slots):
    _, rows, cols = fields.shape
    bottom = fields[1, rows - 8 :, :]
    edge = fields[2, :, cols - K :]
    return pl.pallas_call(
        finish_kernel,
        out_shape=(pltpu.HBM(fields.shape, f32), pltpu.HBM((1, slots), f32)),
        in_specs=[hbm_spec()] + [vmem_spec()] * 5,
        out_specs=(hbm_spec(), hbm_spec()),
        input_output_aliases={0: 0},
        scratch_shapes=[
            pltpu.VMEM((8, cols), f32),
            pltpu.VMEM((rows, K), f32),
            pltpu.VMEM((1, slots), f32),
            pltpu.SemaphoreType.DMA((3,)),
        ],
        compiler_params=pltpu.CompilerParams(vmem_limit_bytes=16 << 20),
        cost_estimate=cost(1 << 20, 1 << 20),
        name="finish",
    )(*in_hbm(fields), sums, hrow, hcol, bottom, edge)


def partner(axis, bit):
    return [(i, i ^ bit) for i in range(lax.axis_size(axis))]


def previous(axis):
    size = lax.axis_size(axis)
    return [(i, (i - 1) % size) for i in range(size)]


def body(
    adj_fields, depth, block_x, reduced_x, block_y, reduced_y, basis, coef, footprint, owner, wet
):
    size_x = lax.axis_size("gx")
    size_y = lax.axis_size("gy")
    px, py = ends(adj_fields, depth, block_x, block_y, size_x, size_y)
    tx = lax.all_to_all(px, "gx", split_axis=0, concat_axis=0, tiled=True)
    carried = carry(block_x, block_y, reduced_x, reduced_y, coef, footprint, wet)
    ty = py[None]
    ty = jnp.concatenate([ty, lax.ppermute(ty, "gy", partner("gy", size_y // 2))], axis=0)
    near = [ty] + [lax.ppermute(ty, "gy", partner("gy", bits)) for bits in range(1, size_y // 2)]
    fields, parts, erow, ecol = elevation(tx, near, carried, adj_fields, depth, basis, wet, owner)
    devices = size_x * size_y
    hrow = lax.ppermute(erow, "gx", previous("gx"))
    hcol = lax.ppermute(ecol, "gy", previous("gy"))
    sums = lax.all_to_all(
        parts[:, None, :], ("gx", "gy"), split_axis=0, concat_axis=0, tiled=True
    )
    slots = owner.shape[0] // devices
    adj_before, grad = finish(fields, sums[:, 0, :], hrow, hcol, slots)
    return adj_before, grad.reshape(slots)


def solution(mesh):
    in_specs = (
        P(None, "gx", "gy"),
        P("gx", "gy"),
        P(),
        P(),
        P(),
        P(),
        P(),
        P(),
        P(),
        P(),
        P("gx", "gy"),
    )
    out_specs = (P(None, "gx", "gy"), P(("gx", "gy")))
    return jax.shard_map(body, mesh=mesh, in_specs=in_specs, out_specs=out_specs, check_vma=False)
```
